512 devices in a mesh: row: 32 (over z_lo, y, core), col: 16 (over x, z_hi).
Axes of the slice: x: 4, y: 8, z: 8 (z_hi: 4, z_lo: 2; z = z_hi * 2 + z_lo), core: 2. Of those that a mesh axis runs over, the one named last changes fastest.
Arguments:
- positions: float32 [3, 32768], P(None, ('row', 'col')), may hold values from -1 to 1
- normals: float32 [3, 32768], P(None, ('row', 'col')), may hold values from -4 to 4
- areas: float32 [32768], P(('row', 'col')), may hold values from 0.00012207031 to 0.0012207031
- direct: bfloat16 [32768, 64], P(('row', 'col')), may hold values from -6 to 6
- adjoint: bfloat16 [32768, 64], P(('row', 'col')), may hold values from -6 to 6
- spline: bfloat16 [512, 256, 512], P(('row', 'col')), may hold values from -0.375 to 0.375
- block_lists: int32 [128, 4], replicated, may hold values from 0 to 511, all different within a row
- patch_counts: int32 [64], replicated, may hold values from 1 to 8, 128 in all
- patch_owner: int32 [64], replicated, may hold values from 0 to 63, each once
Outputs:
- densities: float32 [32768], P(('row', 'col'))
- patch_grad: float32 [64, 512], P('row')
The draws below stay inside these ranges and needn't reach their ends.
Inputs may be any that keep to these rules, and one draw needn't show every extreme that they name: `block_lists`: each row names 4 different spline blocks, and every spline block is named by some row. `patch_counts`: the counts sum to 128; the largest is exactly 8. `patch_owner`: A permutation of the patches.
All inputs are finite; a program needn't handle non-finite values.
Results may differ from the reference program's by a relative error of at most 0.0029.
Values may be sent and summed in bfloat16 or wider, within the bound.
No kernel may reach another device: no remote copies, remote signals or barrier semaphores. Data moves between devices by JAX's collectives and lax.ppermute only.
A program may use at most 64 MiB of HBM per device.

```python
import math
import jax
import jax.numpy as jnp
import numpy as np
from jax import lax

P_SIZE = 32768
H = 32
BPAN = 256
CTRL = 512
LISTS = 4
NPATCH = 64
MOSTB = 8
NBLK = 128
NSPL = 512
COLS = 64


def block_scale(rng, extent, cuts, least, high):
    gain = 1.0
    for dim, blocks in cuts:
        draws = jax.random.uniform(jax.random.fold_in(jax.random.fold_in(rng, 6), dim), (blocks,), jnp.float32, least / len(cuts), high / len(cuts))
        gain = gain * jnp.repeat(jnp.exp(draws), extent[dim] // blocks).reshape((-1,) + (1,) * (len(extent) - 1 - dim))
    return gain


def picks_of(stream_key, rows, count, top, lift):
    order = jax.random.permutation(jax.random.fold_in(stream_key, 1), count)
    favour = order
    for power in range(3):
        favour = favour * favour // count
    favour = favour * lift // count
    chance = jax.random.randint(jax.random.fold_in(stream_key, 2), (rows, count), 0, 4096) + favour
    sure = jax.random.permutation(jax.random.fold_in(stream_key, 3), rows)[jnp.arange(count) % rows]
    chance = jnp.where(jnp.arange(rows)[:, None] == sure[None, :], 1 << 14, chance)
    priority = chance * count + jnp.arange(count)
    return lax.top_k(priority.astype(jnp.int32), top)[1].astype(jnp.int32)


def split_up(amount, total, limit, lean):
    loads = [(1 << 20) // math.isqrt(rank ** lean) + 1 for rank in range(2, amount + 1)]
    rest, given = total - limit - (amount - 1), [1] * (amount - 1)
    while rest > 0:
        movable = [i for i in range(amount - 1) if given[i] < limit]
        mass, remaining = sum([loads[i] for i in movable]), rest
        for i in movable:
            addition = min(limit - given[i], max(1, remaining * loads[i] // mass), rest)
            given[i] = given[i] + addition
            rest = rest - addition
    return np.array([limit] + given)


def ragged(stream_key, number_of, total, most, skew):
    if number_of == 2:
        one = jax.random.randint(stream_key, (), max(1, total - most), min(most, total - 1) + 1)
        return jnp.stack([one, total - one])
    lengths = jnp.asarray(split_up(number_of, total, most, skew), jnp.int32)
    pairs = (number_of - 1) // 2
    donor, receiver = lengths[1:1 + 2 * pairs:2], lengths[2:2 + 2 * pairs:2]
    room = jnp.minimum(donor - 1, most - receiver)
    moved = jax.random.randint(jax.random.fold_in(stream_key, 1), (pairs,), 0, 1 << 20) % (room + 1)
    lengths = lengths.at[1:1 + 2 * pairs:2].set(donor - moved).at[2:2 + 2 * pairs:2].set(receiver + moved)
    return lengths[jax.random.permutation(jax.random.fold_in(stream_key, 2), number_of)]


def bell_draw(rng, shape, width, most, split=(), kind=jnp.bfloat16):
    loudness = block_scale(rng, shape, split, -0.22, 0.18) if split else 1.0
    drawn = jax.random.normal(rng, shape, jnp.float32) * width * loudness
    return jnp.minimum(jnp.maximum(drawn, -most), most).astype(kind)


def setup_inputs(seed: int = 0) -> dict:
    seeds = jax.random.split(jax.random.key(seed), 10)
    positions = jnp.clip(jax.random.uniform(seeds[0], (3, P_SIZE), jnp.float32, -1.0, 1.0) * block_scale(seeds[0], (3, P_SIZE), ((1, 512),), -0.4, 0.0), -1.0, 1.0)
    normals = bell_draw(seeds[1], (3, P_SIZE), 1.0, 4.0, ((1, 512),), jnp.float32)
    areas = jnp.clip(jnp.exp(math.log(0.0012207031) - 2.3025851 * jax.random.uniform(seeds[2], (P_SIZE,), jnp.float32) ** block_scale(seeds[2], (P_SIZE,), ((0, 512),), -0.2, 0.2)), 0.00012207031, 0.0012207031)
    direct = bell_draw(seeds[3], (P_SIZE, COLS), 1.0, 6.0, ((0, 512),))
    adjoint = bell_draw(seeds[4], (P_SIZE, COLS), 1.0, 6.0, ((0, 512),))
    spline = bell_draw(seeds[5], (NSPL, BPAN, CTRL), BPAN ** -0.5, 0.375, ((0, 512),))
    block_lists = picks_of(seeds[6], NBLK, NSPL, LISTS, 128)
    patch_counts = ragged(seeds[7], NPATCH, NBLK, MOSTB, 2).astype(jnp.int32)
    patch_owner = jax.random.permutation(seeds[8], NPATCH).astype(jnp.int32)
    return dict(positions=positions, normals=normals, areas=areas, direct=direct, adjoint=adjoint, spline=spline, block_lists=block_lists, patch_counts=patch_counts, patch_owner=patch_owner)


wave_number = 6.0
inv_four_pi = 0.07957747154594767

def kernel_block(tgt_pos, tgt_nrm, src_pos, src_area):
    depth_t = 0.5 * (tgt_pos[2] - 1.2)
    depth_s = 0.5 * (src_pos[2] - 1.2)
    delta_x = tgt_pos[0][:, None] - src_pos[0][None, :]
    delta_y = tgt_pos[1][:, None] - src_pos[1][None, :]
    delta_z = depth_t[:, None] - depth_s[None, :]
    image_z = depth_t[:, None] + depth_s[None, :]
    area_row = src_area[None, :]
    level = delta_x * delta_x + delta_y * delta_y
    near = level + delta_z * delta_z + area_row
    mirror = level + image_z * image_z + area_row
    slope = tgt_nrm[0][:, None] * delta_x + tgt_nrm[1][:, None] * delta_y
    vertical = tgt_nrm[2][:, None]
    rankine = (slope + vertical * delta_z) / (near * jnp.sqrt(near))
    reflect = (slope + vertical * image_z) / (mirror * jnp.sqrt(mirror))
    waves = 2.0 * wave_number * jnp.exp(wave_number * image_z) * vertical * jnp.cos(wave_number * jnp.sqrt(level + area_row))
    return area_row * (rankine + reflect - waves) * inv_four_pi

def reference(positions, normals, areas, direct, adjoint, spline, block_lists, patch_counts, patch_owner):
    step_rows = min(P_SIZE, 256)
    count = P_SIZE // step_rows

    def advance(carry, index):
        start = (index * step_rows).astype(jnp.int32)
        tgt_pos = lax.dynamic_slice_in_dim(positions, start, step_rows, 1)
        tgt_nrm = lax.dynamic_slice_in_dim(normals, start, step_rows, 1)
        adj_rows = lax.dynamic_slice_in_dim(adjoint, start, step_rows, 0)
        tile = kernel_block(tgt_pos, tgt_nrm, positions, areas).astype(jnp.bfloat16)
        image_rows = jnp.dot(tile, direct, preferred_element_type=jnp.float32)
        carry = carry + lax.dot_general(tile, adj_rows, (((0,), (0,)), ((), ())), preferred_element_type=jnp.float32)
        return (carry, image_rows)
    adjoint_image, pieces = lax.scan(advance, jnp.zeros((P_SIZE, 2 * H), jnp.float32), jnp.arange(count, dtype=jnp.int32))
    direct_image = pieces.reshape(P_SIZE, 2 * H)
    densities = lax.optimization_barrier(jnp.sum(adjoint.astype(jnp.float32) * direct_image + direct.astype(jnp.float32) * adjoint_image, axis=1))
    blocks = densities.reshape(NBLK, BPAN)

    def one_block(item):
        values, listed = item
        basis = lax.optimization_barrier(jnp.sum(spline[listed].astype(jnp.float32), axis=0))
        return jnp.dot(values, basis, precision=lax.Precision.HIGHEST)
    block_grad = lax.map(one_block, (blocks, block_lists))
    ends = jnp.cumsum(patch_counts).astype(jnp.int32)
    starts = ends - patch_counts
    block_ids = jnp.arange(NBLK, dtype=jnp.int32)
    inside = ((starts[:, None] <= block_ids[None, :]) & (block_ids[None, :] < ends[:, None])).astype(jnp.float32)
    owners = (patch_owner[None, :] == jnp.arange(NPATCH, dtype=jnp.int32)[:, None]).astype(jnp.float32)
    owned = jnp.dot(owners, inside, precision=lax.Precision.HIGHEST)
    patch_grad = jnp.dot(owned, block_grad, precision=lax.Precision.HIGHEST)
    return (densities, patch_grad)
```

```python
import jax
import jax.numpy as jnp
import numpy as np
from jax import lax
from jax.experimental import pallas as pl
from jax.experimental.pallas import tpu as pltpu
from jax.sharding import PartitionSpec as P

F32 = jnp.float32
BF16 = jnp.bfloat16
BPAN = 256
NPATCH = 64
NBLK = 128
LANES = 128
wave_number = 6.0
inv_four_pi = 0.07957747154594767

TURNS = wave_number / (2.0 * np.pi)
DEGREE = 6


def cosine_coefficients():
    k = np.arange(64)
    nodes = 0.125 + 0.125 * np.cos(np.pi * (2 * k + 1) / 128)
    fit = np.polynomial.chebyshev.Chebyshev.fit(
        nodes, np.cos(2 * np.pi * np.sqrt(nodes)), DEGREE, domain=[0.0, 0.25]
    )
    return fit.convert(kind=np.polynomial.Polynomial).coef


COEF = cosine_coefficients()
LEAD = float(COEF[-1])
MONIC = [float(c / COEF[-1]) for c in COEF[:-1]]
ROUNDER = float(3 << 22)
AREA_SCALE = float(TURNS**2 * inv_four_pi)
WAVE_SCALE = float(2.0 * wave_number * inv_four_pi * LEAD)

GEO = 64
T_NAMES = 6
S_NAMES = 4


def split3(v):
    hi = v.astype(BF16)
    rest = v - hi.astype(F32)
    mid = rest.astype(BF16)
    lo = (rest - mid.astype(F32)).astype(BF16)
    return hi, mid, lo


def pack_kernel(pos_ref, nrm_ref, area_ref, dir_ref, adj_ref, tgt_ref, src_ref):
    pos = pos_ref[...]
    row = lax.broadcasted_iota(jnp.int32, pos.shape, 0)
    pos = jnp.where(row == 2, 0.5 * (pos - 1.2), pos) * TURNS

    def rows(values):
        h, m, l = split3(values)
        return jnp.concatenate([h.astype(F32), m.astype(F32), l.astype(F32)], axis=0)

    def lay(parts, cols, ref):
        stacked = jnp.concatenate(parts, axis=0)
        depth = stacked.shape[0]
        place = lax.broadcasted_iota(jnp.int32, (depth, LANES), 1) == (
            lax.broadcasted_iota(jnp.int32, (depth, LANES), 0) + GEO
        )
        geo = lax.dot_general(
            stacked.astype(BF16),
            place.astype(F32).astype(BF16),
            (((0,), (0,)), ((), ())),
            preferred_element_type=F32,
        ).astype(BF16)
        wide = jnp.concatenate([cols, cols], axis=1)
        lane = lax.broadcasted_iota(jnp.int32, geo.shape, 1)
        ref[...] = jnp.where(lane < GEO, wide.astype(F32), geo.astype(F32)).astype(BF16)

    lay([rows(pos), rows(nrm_ref[...])], adj_ref[...], tgt_ref)
    lay([rows(pos), rows(area_ref[...] * TURNS**2)], dir_ref[...], src_ref)


def pack(positions, normals, areas, direct, adjoint):
    panels = positions.shape[1]
    out = jax.ShapeDtypeStruct((panels, LANES), BF16)
    return pl.pallas_call(pack_kernel, out_shape=(out, out), name="pack")(
        positions, normals, areas.reshape(1, panels), direct, adjoint
    )


def target_lane(k, part):
    return GEO + (0 if k < 3 else 9) + 3 * part + k % 3


def source_lane(k, part):
    return GEO + 3 * part + k if k < 3 else GEO + 9 + part


def picks(shape, axis, lanes):
    where = lax.broadcasted_iota(jnp.int32, shape, axis)
    hit = (where == lanes[0]) | (where == lanes[1]) | (where == lanes[2])
    return jnp.where(hit, 1.0, 0.0).astype(BF16)


ROWS = 16
CHUNK = 256


def tile_kernel(tgt_ref, src_ref, row_ref, col_ref, tgeo, sgeo, images, rowacc):
    targets, sources = tgt_ref.shape[0], src_ref.shape[0]
    contract_last = (((1,), (1,)), ((), ()))
    for k in range(T_NAMES):
        spread = picks((LANES, LANES), 0, [target_lane(k, p) for p in range(3)])
        tgeo[k] = jnp.dot(tgt_ref[...], spread, preferred_element_type=F32)
    tgeo[6] = (WAVE_SCALE * tgeo[5]) * jnp.exp((wave_number / TURNS) * tgeo[2])
    for k in range(S_NAMES):
        spread = picks((8, LANES), 1, [source_lane(k, p) for p in range(3)])
        sgeo[k] = lax.dot_general(spread, src_ref[...], contract_last, preferred_element_type=F32)
    sgeo[4] = (sgeo[3] * (1.0 / TURNS**2)) * jnp.exp((wave_number / TURNS) * sgeo[2])
    sgeo[5] = sgeo[3] * (AREA_SCALE / TURNS**2)
    rowacc[...] = jnp.zeros_like(rowacc)

    def chunk(j, _):
        s0 = pl.multiple_of(j * CHUNK, CHUNK)
        images[...] = lax.dot_general(
            tgt_ref[:, :GEO],
            src_ref[pl.ds(s0, CHUNK), :GEO],
            contract_last,
            preferred_element_type=F32,
        )
        halves = range(CHUNK // LANES)

        def wide(k, h):
            v = sgeo[k, :, pl.ds(pl.multiple_of(s0 + h * LANES, LANES), LANES)]
            return jnp.concatenate([v] * (ROWS // 8), axis=0)

        src = [[wide(k, h) for k in range(6)] for h in halves]

        def step(i, acc):
            t0 = pl.multiple_of(i * ROWS, ROWS)
            xt, yt, zt, nx, ny, nz, amp = (tgeo[k, pl.ds(t0, ROWS), :] for k in range(7))
            zt4, nz2 = 4.0 * zt, 2.0 * nz
            new, total = [], rowacc[pl.ds(t0, ROWS), :]
            for h in halves:
                xs, ys, zs, area, ebb, share = src[h]
                dx, dy, dz = xt - xs, yt - ys, zt - zs
                flat = dx * dx + dy * dy + area
                near = flat + dz * dz
                mirror = near + zt4 * zs
                top = nx * dx + ny * dy + nz * dz
                topi = top + nz2 * zs
                i1, i2, i3 = lax.rsqrt(near), lax.rsqrt(mirror), lax.rsqrt(flat)
                pair = top * (i1 * i1 * i1) + topi * (i2 * i2 * i2)
                phase = flat * i3
                f = phase - ((phase + ROUNDER) - ROUNDER)
                g = f * f
                p = g + MONIC[-1]
                for c in MONIC[-2::-1]:
                    p = p * g + c
                kern = share * pair - (amp * ebb) * p
                w = kern.astype(BF16).astype(F32) * images[pl.ds(t0, ROWS), h * LANES : (h + 1) * LANES]
                new.append(acc[h] + w)
                total = total + w
            rowacc[pl.ds(t0, ROWS), :] = total
            return tuple(new)

        zero = jnp.zeros((ROWS, LANES), F32)
        acc = lax.fori_loop(0, targets // ROWS, step, (zero,) * len(halves), unroll=2)
        for h in halves:
            col_ref[0:1, pl.ds(pl.multiple_of(s0 + h * LANES, LANES), LANES)] = jnp.sum(acc[h], axis=0, keepdims=True)
        return 0

    lax.fori_loop(0, sources // CHUNK, chunk, 0)
    for g in range(targets // LANES):
        line = jnp.sum(rowacc[g * LANES : (g + 1) * LANES, :].T, axis=0, keepdims=True)
        row_ref[g // 2 : g // 2 + 1, (g % 2) * LANES : (g % 2 + 1) * LANES] = line


def tile(tgt, src):
    targets, sources = tgt.shape[0], src.shape[0]
    return pl.pallas_call(
        tile_kernel,
        out_shape=(
            jax.ShapeDtypeStruct((targets // BPAN, BPAN), F32),
            jax.ShapeDtypeStruct((1, sources), F32),
        ),
        scratch_shapes=[
            pltpu.VMEM((7, targets, LANES), F32),
            pltpu.VMEM((6, 8, sources), F32),
            pltpu.VMEM((targets, CHUNK), F32),
            pltpu.VMEM((targets, LANES), F32),
        ],
        compiler_params=pltpu.CompilerParams(vmem_limit_bytes=24 << 20),
        name="tile",
    )(tgt, src)


def patch_kernel(mix_ref, dens_ref, spline_ref, out_ref):
    hi, mid, lo = split3(dens_ref[...])
    mix = mix_ref[...].astype(BF16)
    got = sum(jnp.dot(mix, part, preferred_element_type=F32) for part in (lo, mid, hi))
    hi, mid, lo = split3(got)
    spline = spline_ref[...]
    out_ref[...] = sum(jnp.dot(part, spline, preferred_element_type=F32) for part in (lo, mid, hi))


def patch(mix, blocks, spline):
    return pl.pallas_call(
        patch_kernel,
        out_shape=jax.ShapeDtypeStruct((NPATCH, spline.shape[1]), F32),
        compiler_params=pltpu.CompilerParams(vmem_limit_bytes=16 << 20),
        name="patch",
    )(mix, blocks, spline)


def exchange(pieces, axis):
    return lax.all_to_all(pieces, axis, 0, 0, tiled=True)


def spread(value, axis, count):
    return exchange(jnp.broadcast_to(value[None], (count,) + value.shape), axis)


def solution(mesh):
    nrow, ncol = mesh.shape["row"], mesh.shape["col"]

    def on_device(
        positions, normals, areas, direct, adjoint, spline, block_lists, patch_counts, patch_owner
    ):
        panels = positions.shape[1]
        col = lax.axis_index("col")
        holder = lax.axis_index("row") * ncol + col
        patches = jnp.arange(NPATCH, dtype=jnp.int32)
        before = patches[None, :] < patches[:, None]
        starts = jnp.sum(jnp.where(before, patch_counts[None, :], 0), axis=1)
        ends = starts + patch_counts
        ids = jnp.arange(NBLK, dtype=jnp.int32)
        inside = (starts[:, None] <= ids[None, :]) & (ids[None, :] < ends[:, None])
        row_of = jnp.sum(jnp.where(inside, patch_owner[:, None], 0), axis=0)
        listed = jnp.any(block_lists == holder, axis=1)
        mix = ((row_of[None, :] == patches[:, None]) & listed[None, :]).astype(F32)

        tgt, src = pack(positions, normals, areas, direct, adjoint)
        tgt_all = spread(tgt, "col", ncol).reshape(ncol * panels, LANES)
        src_all = spread(src, "row", nrow).reshape(nrow * panels, LANES)
        row_part, col_part = tile(tgt_all, src_all)

        mine = jnp.sum(exchange(col_part.reshape(nrow, 1, panels), "row"), axis=0)
        per = BPAN // panels
        at_row = lax.broadcasted_iota(jnp.int32, row_part.shape, 0) == col // per
        at_lane = lax.broadcasted_iota(jnp.int32, row_part.shape, 1) // panels == col % per
        row_part = row_part + jnp.where(at_row & at_lane, jnp.tile(mine, (1, per)), 0.0)
        row_dens = jnp.sum(spread(row_part, "col", ncol), axis=0)
        densities = lax.dynamic_slice(row_dens, (col // per, (col % per) * panels), (1, panels)).reshape(panels)
        blocks = spread(row_dens, "row", nrow).reshape(NBLK, BPAN)

        contrib = patch(mix, blocks, spline[0])
        rows = NPATCH // nrow
        partial = jnp.sum(exchange(contrib.reshape(nrow, rows, contrib.shape[1]), "row"), axis=0)
        patch_grad = jnp.sum(spread(partial, "col", ncol), axis=0)
        return densities, patch_grad

    placed = (
        P(None, ("row", "col")),
        P(None, ("row", "col")),
        P(("row", "col")),
        P(("row", "col"), None),
        P(("row", "col"), None),
        P(("row", "col"), None, None),
        P(),
        P(),
        P(),
    )
    return jax.shard_map(
        on_device,
        mesh=mesh,
        in_specs=placed,
        out_specs=(P(("row", "col")), P("row", None)),
        check_vma=False,
    )
```

```python
import jax
import jax.numpy as jnp
import numpy as np
from jax import lax
from jax.experimental import pallas as pl
from jax.experimental.pallas import tpu as pltpu
from jax.sharding import Mesh
from jax.sharding import PartitionSpec as P

F32 = jnp.float32
BF16 = jnp.bfloat16
BPAN = 256
NPATCH = 64
NBLK = 128
LANES = 128
wave_number = 6.0
inv_four_pi = 0.07957747154594767

TURNS = wave_number / (2.0 * np.pi)
DEGREE = 6


def cosine_coefficients():
    k = np.arange(64)
    nodes = 0.125 + 0.125 * np.cos(np.pi * (2 * k + 1) / 128)
    fit = np.polynomial.chebyshev.Chebyshev.fit(
        nodes, np.cos(2 * np.pi * np.sqrt(nodes)), DEGREE, domain=[0.0, 0.25]
    )
    return fit.convert(kind=np.polynomial.Polynomial).coef


COEF = cosine_coefficients()
LEAD = float(COEF[-1])
MONIC = [float(c / COEF[-1]) for c in COEF[:-1]]
ROUNDER = float(3 << 22)
AREA_SCALE = float(TURNS**2 * inv_four_pi)
WAVE_SCALE = float(2.0 * wave_number * inv_four_pi * LEAD)

PARTS = {"z_lo": 2, "y": 8, "core": 2, "x": 4, "z_hi": 4}
NAMES = tuple(PARTS)
TGT_AXES = ("y", "core")
SRC_AXES = ("z_lo", "x", "z_hi")
NTGT = PARTS["y"] * PARTS["core"]
NSRC = PARTS["z_lo"] * PARTS["x"] * PARTS["z_hi"]

GEO = 64
T_NAMES = 6
S_NAMES = 4


def split3(v):
    hi = v.astype(BF16)
    rest = v - hi.astype(F32)
    mid = rest.astype(BF16)
    lo = (rest - mid.astype(F32)).astype(BF16)
    return hi, mid, lo


def pack_kernel(pos_ref, nrm_ref, area_ref, dir_ref, adj_ref, tgt_ref, src_ref):
    pos = pos_ref[...]
    row = lax.broadcasted_iota(jnp.int32, pos.shape, 0)
    pos = jnp.where(row == 2, 0.5 * (pos - 1.2), pos) * TURNS

    def rows(values):
        h, m, l = split3(values)
        return jnp.concatenate([h.astype(F32), m.astype(F32), l.astype(F32)], axis=0)

    def lay(parts, cols, ref):
        stacked = jnp.concatenate(parts, axis=0)
        depth = stacked.shape[0]
        place = lax.broadcasted_iota(jnp.int32, (depth, LANES), 1) == (
            lax.broadcasted_iota(jnp.int32, (depth, LANES), 0) + GEO
        )
        geo = lax.dot_general(
            stacked.astype(BF16),
            place.astype(F32).astype(BF16),
            (((0,), (0,)), ((), ())),
            preferred_element_type=F32,
        ).astype(BF16)
        wide = jnp.concatenate([cols, cols], axis=1)
        lane = lax.broadcasted_iota(jnp.int32, geo.shape, 1)
        features = jnp.where(lane < GEO, wide.astype(F32), geo.astype(F32)).astype(BF16)
        for piece in range(ref.shape[0]):
            ref[piece] = features

    lay([rows(pos), rows(nrm_ref[...])], adj_ref[...], tgt_ref)
    lay([rows(pos), rows(area_ref[...] * TURNS**2)], dir_ref[...], src_ref)


def pack(positions, normals, areas, direct, adjoint):
    panels = positions.shape[1]
    out = [jax.ShapeDtypeStruct((n, panels, LANES), BF16) for n in (NTGT, NSRC)]
    return pl.pallas_call(pack_kernel, out_shape=out, name="pack")(
        positions, normals, areas.reshape(1, panels), direct, adjoint
    )


def target_lane(k, part):
    return GEO + (0 if k < 3 else 9) + 3 * part + k % 3


def source_lane(k, part):
    return GEO + 3 * part + k if k < 3 else GEO + 9 + part


def picks(shape, axis, lanes):
    where = lax.broadcasted_iota(jnp.int32, shape, axis)
    hit = (where == lanes[0]) | (where == lanes[1]) | (where == lanes[2])
    return jnp.where(hit, 1.0, 0.0).astype(BF16)


ROWS = 16
CHUNK = 256


def device_place():
    at = {name: lax.axis_index(name) for name in NAMES}
    rho = at["y"] * PARTS["core"] + at["core"]
    return rho, at["z_lo"] * PARTS["x"] + at["x"], at["z_hi"]


def mix_rows(counts_ref, owner_ref, lists_ref, mix_ref):
    rho, row, quarter = device_place()
    nx = PARTS["x"]
    holder = ((row // nx) * NTGT + rho) * (nx * PARTS["z_hi"]) + (row % nx) * PARTS["z_hi"] + quarter

    def iota(shape, dim):
        return lax.broadcasted_iota(jnp.int32, shape, dim)

    square = (NPATCH, NPATCH)
    counts = jnp.broadcast_to(counts_ref[...], square)
    eye = iota(square, 0) == iota(square, 1)
    starts = jnp.sum(jnp.where(iota(square, 1) < iota(square, 0), counts, 0).astype(F32), axis=1, keepdims=True)
    own_counts = jnp.sum(jnp.where(eye, counts, 0).astype(F32), axis=1, keepdims=True)
    lines = (NPATCH, NBLK)
    ids = iota(lines, 1).astype(F32)
    inside = (starts <= ids) & (ids < starts + own_counts)
    owner = jnp.broadcast_to(owner_ref[...], square)
    place = iota(square, 0)
    output = ((place % 4) // 2) * (2 * NTGT) + 2 * (place // 4) + place % 2
    owned = jnp.where(owner == output, 1.0, 0.0).astype(BF16)
    listed = jnp.max(jnp.where(lists_ref[...] == holder, 1.0, 0.0), axis=0, keepdims=True)
    member = jnp.where(inside, jnp.broadcast_to(listed, lines), 0.0).astype(BF16)
    by_block = jnp.dot(owned, member, preferred_element_type=F32).astype(BF16)
    cut = (NBLK, NBLK)
    k = iota(cut, 1)
    block = ((k % 8) // nx) * (NTGT * nx) + (k // 8) * nx + k % nx
    order = jnp.where(iota(cut, 0) == block, 1.0, 0.0).astype(BF16)
    mix_ref[...] = jnp.dot(by_block, order, preferred_element_type=F32).astype(BF16)


def tile_kernel(
    tgt_ref, src_ref, counts_ref, owner_ref, lists_ref, row_ref, col_ref, mix_ref, tgeo, sgeo, images, rowacc, colacc
):
    mix_rows(counts_ref, owner_ref, lists_ref, mix_ref)
    targets, sources = tgt_ref.shape[0], src_ref.shape[0]
    contract_last = (((1,), (1,)), ((), ()))
    for k in range(T_NAMES):
        spread = picks((LANES, LANES), 0, [target_lane(k, p) for p in range(3)])
        tgeo[k] = jnp.dot(tgt_ref[...], spread, preferred_element_type=F32)
    tgeo[6] = (WAVE_SCALE * tgeo[5]) * jnp.exp((wave_number / TURNS) * tgeo[2])
    for k in range(S_NAMES):
        spread = picks((8, LANES), 1, [source_lane(k, p) for p in range(3)])
        sgeo[k] = lax.dot_general(spread, src_ref[...], contract_last, preferred_element_type=F32)
    sgeo[4] = (sgeo[3] * (1.0 / TURNS**2)) * jnp.exp((wave_number / TURNS) * sgeo[2])
    sgeo[5] = sgeo[3] * (AREA_SCALE / TURNS**2)
    rowacc[...] = jnp.zeros_like(rowacc)

    def chunk(j, _):
        s0 = pl.multiple_of(j * CHUNK, CHUNK)
        images[...] = lax.dot_general(
            tgt_ref[:, :GEO],
            src_ref[pl.ds(s0, CHUNK), :GEO],
            contract_last,
            preferred_element_type=F32,
        )
        halves = range(CHUNK // LANES)

        def wide(k, h):
            v = sgeo[k, :, pl.ds(pl.multiple_of(s0 + h * LANES, LANES), LANES)]
            return jnp.concatenate([v] * (ROWS // 8), axis=0)

        src = [[wide(k, h) for k in range(6)] for h in halves]

        def step(i, acc):
            t0 = pl.multiple_of(i * ROWS, ROWS)
            xt, yt, zt, nx, ny, nz, amp = (tgeo[k, pl.ds(t0, ROWS), :] for k in range(7))
            zt4, nz2 = 4.0 * zt, 2.0 * nz
            new, total = [], rowacc[pl.ds(t0, ROWS), :]
            for h in halves:
                xs, ys, zs, area, ebb, share = src[h]
                dx, dy, dz = xt - xs, yt - ys, zt - zs
                flat = dx * dx + dy * dy + area
                near = flat + dz * dz
                mirror = near + zt4 * zs
                top = nx * dx + ny * dy + nz * dz
                topi = top + nz2 * zs
                i1, i2, i3 = lax.rsqrt(near), lax.rsqrt(mirror), lax.rsqrt(flat)
                pair = top * (i1 * i1 * i1) + topi * (i2 * i2 * i2)
                phase = flat * i3
                f = phase - ((phase + ROUNDER) - ROUNDER)
                g = f * f
                p = g + MONIC[-1]
                for c in MONIC[-2::-1]:
                    p = p * g + c
                kern = share * pair - (amp * ebb) * p
                w = kern.astype(BF16).astype(F32) * images[pl.ds(t0, ROWS), h * LANES : (h + 1) * LANES]
                new.append(acc[h] + w)
                total = total + w
            rowacc[pl.ds(t0, ROWS), :] = total
            return tuple(new)

        zero = jnp.zeros((ROWS, LANES), F32)
        acc = lax.fori_loop(0, targets // ROWS, step, (zero,) * len(halves), unroll=2)
        for h in halves:
            colacc[0:1, pl.ds(pl.multiple_of(s0 + h * LANES, LANES), LANES)] = jnp.sum(acc[h], axis=0, keepdims=True)
        return 0

    lax.fori_loop(0, sources // CHUNK, chunk, 0)
    for j in range(sources // BPAN):
        col_ref[j : j + 1, :] = colacc[0:1, j * BPAN : (j + 1) * BPAN]
    panels = row_ref.shape[2]
    for g in range(targets // LANES):
        line = jnp.sum(rowacc[g * LANES : (g + 1) * LANES, :].T, axis=0, keepdims=True)
        for half in range(LANES // panels):
            row_ref[g * (LANES // panels) + half] = line[:, half * panels : (half + 1) * panels]


def tile(tgt, src, patch_counts, patch_owner, block_lists):
    pieces, panels = tgt.shape[:2]
    targets, sources = pieces * panels, src.shape[0] * panels
    return pl.pallas_call(
        tile_kernel,
        out_shape=(
            jax.ShapeDtypeStruct((pieces, 1, panels), F32),
            jax.ShapeDtypeStruct((sources // BPAN, BPAN), F32),
            jax.ShapeDtypeStruct((NPATCH, NBLK), BF16),
        ),
        scratch_shapes=[
            pltpu.VMEM((7, targets, LANES), F32),
            pltpu.VMEM((6, 8, sources), F32),
            pltpu.VMEM((targets, CHUNK), F32),
            pltpu.VMEM((targets, LANES), F32),
            pltpu.VMEM((1, sources), F32),
        ],
        compiler_params=pltpu.CompilerParams(vmem_limit_bytes=24 << 20),
        name="tile",
    )(
        tgt.reshape(targets, LANES),
        src.reshape(sources, LANES),
        patch_counts.reshape(1, NPATCH),
        patch_owner.reshape(1, NPATCH),
        block_lists.T,
    )


def patch_kernel(mix_ref, dens_ref, spline_ref, out_ref, own_ref):
    hi, mid, lo = split3(dens_ref[...])
    mix = mix_ref[...]
    got = sum(jnp.dot(mix, part, preferred_element_type=F32) for part in (lo, mid, hi))
    hi, mid, lo = split3(got)
    spline = spline_ref[...]
    rows = sum(jnp.dot(part, spline, preferred_element_type=F32) for part in (lo, mid, hi))
    for piece in range(out_ref.shape[0]):
        depth = out_ref.shape[1]
        out_ref[piece] = rows[piece * depth : (piece + 1) * depth]
    rho, row, quarter = device_place()
    line = dens_ref[pl.ds(rho * 8 + row, 1), :]
    panels = own_ref.shape[1]
    mine = line[:, :panels]
    for q in range(1, BPAN // panels):
        mine = jnp.where(quarter == q, line[:, q * panels : (q + 1) * panels], mine)
    own_ref[...] = mine


def patch(mix, blocks, spline, panels):
    return pl.pallas_call(
        patch_kernel,
        out_shape=(
            jax.ShapeDtypeStruct((NTGT, NPATCH // NTGT, spline.shape[1]), F32),
            jax.ShapeDtypeStruct((1, panels), F32),
        ),
        compiler_params=pltpu.CompilerParams(vmem_limit_bytes=16 << 20),
        name="patch",
    )(mix, blocks, spline)


def exchange(pieces, axes):
    return lax.all_to_all(pieces, axes, 0, 0, tiled=True)


def copies(value, count):
    return jnp.broadcast_to(value[None], (count,) + value.shape)


def on_device(
    positions, normals, areas, direct, adjoint, spline, block_lists, patch_counts, patch_owner
):
    panels = positions.shape[1]
    tgt, src = pack(positions, normals, areas, direct, adjoint)
    src_all = exchange(src, SRC_AXES)
    tgt_all = exchange(tgt, TGT_AXES)
    row_part, col_part, mix = tile(tgt_all, src_all, patch_counts, patch_owner, block_lists)

    mine = jnp.sum(exchange(row_part, TGT_AXES), axis=0)
    _, row, quarter = device_place()
    at_row = lax.broadcasted_iota(jnp.int32, col_part.shape, 0) == row
    at_lane = lax.broadcasted_iota(jnp.int32, col_part.shape, 1) // panels == quarter
    col_part = col_part + jnp.where(at_row & at_lane, jnp.tile(mine, (1, BPAN // panels)), 0.0)
    dens = jnp.sum(exchange(copies(col_part, NSRC), SRC_AXES), axis=0)
    blocks = exchange(copies(dens, NTGT), TGT_AXES).reshape(NBLK, BPAN)

    contrib, own = patch(mix, blocks, spline[0], panels)
    rows = jnp.sum(exchange(contrib, TGT_AXES), axis=0)
    low = PARTS["z_lo"]
    rows = rows.reshape(low, 1, rows.shape[0] // low, rows.shape[1])
    rows = jnp.broadcast_to(rows, (low, NSRC // low) + rows.shape[2:]).reshape((NSRC,) + rows.shape[2:])
    patch_grad = jnp.sum(exchange(rows, SRC_AXES), axis=0)
    return own.reshape(panels), patch_grad


def solution(mesh):
    fine = Mesh(mesh.devices.reshape(tuple(PARTS.values())), NAMES)
    placed = (
        P(None, NAMES),
        P(None, NAMES),
        P(NAMES),
        P(NAMES, None),
        P(NAMES, None),
        P(NAMES, None, None),
        P(),
        P(),
        P(),
    )
    return jax.shard_map(
        on_device,
        mesh=fine,
        in_specs=placed,
        out_specs=(P(NAMES), P(("z_lo", "y", "core"), None)),
        check_vma=False,
    )
```

```python
import jax
import jax.numpy as jnp
import numpy as np
from jax import lax
from jax.experimental import pallas as pl
from jax.experimental.pallas import tpu as pltpu
from jax.sharding import Mesh
from jax.sharding import PartitionSpec as P

F32 = jnp.float32
BF16 = jnp.bfloat16
BPAN = 256
NPATCH = 64
NBLK = 128
LANES = 128
wave_number = 6.0
inv_four_pi = 0.07957747154594767

TURNS = wave_number / (2.0 * np.pi)
DEGREE = 5


def cosine_coefficients():
    k = np.arange(64)
    nodes = 0.125 + 0.125 * np.cos(np.pi * (2 * k + 1) / 128)
    fit = np.polynomial.chebyshev.Chebyshev.fit(
        nodes, np.cos(2 * np.pi * np.sqrt(nodes)), DEGREE, domain=[0.0, 0.25]
    )
    return fit.convert(kind=np.polynomial.Polynomial).coef


COEF = cosine_coefficients()
LEAD = float(COEF[-1])
MONIC = [float(c / COEF[-1]) for c in COEF[:-1]]
ROUNDER = float(3 << 22)
AREA_SCALE = float(TURNS**2 * inv_four_pi)
WAVE_SCALE = float(2.0 * wave_number * inv_four_pi * LEAD)

PARTS = {"z_lo": 2, "y": 8, "core": 2, "x": 4, "z_hi": 4}
NAMES = tuple(PARTS)
TGT_AXES = ("y", "core")
SRC_AXES = ("z_lo", "x", "z_hi")
NTGT = PARTS["y"] * PARTS["core"]
NSRC = PARTS["z_lo"] * PARTS["x"] * PARTS["z_hi"]

COLS = 64
HALF = 32
DEPTH = 40
X, Y, Z = (0, 2, 4), (1, 3, 5), (8, 9, 10)
NX, NY, NZ = (6, 7), (11, 12), (13, 14, 15)
AREA = (11, 12, 13)


def split3(v):
    hi = v.astype(BF16)
    rest = v - hi.astype(F32)
    mid = rest.astype(BF16)
    lo = (rest - mid.astype(F32)).astype(BF16)
    return hi, mid, lo


def pack_kernel(pos_ref, nrm_ref, area_ref, dir_ref, adj_ref, tgt_ref, src_ref):
    pos = pos_ref[...]
    row = lax.broadcasted_iota(jnp.int32, pos.shape, 0)
    pos = jnp.where(row == 2, 0.5 * (pos - 1.2), pos) * TURNS
    p = [v.astype(F32) for v in split3(pos)]
    n = [v.astype(F32) for v in split3(nrm_ref[...])]
    a = [v.astype(F32) for v in split3(area_ref[...] * TURNS**2)]
    flat = [v[0:2] for v in p]
    deep = [v[2:3] for v in p]
    none = jnp.zeros((2, pos.shape[1]), F32)

    def lay(cols, left, right, ref):
        geo = jnp.concatenate([jnp.concatenate(left, axis=0), jnp.concatenate(right, axis=0)], axis=1)
        top = jnp.concatenate([cols[:HALF].astype(F32), cols[HALF:].astype(F32)], axis=1)
        piece = jnp.concatenate([top, geo], axis=0).astype(BF16)
        for k in range(ref.shape[0]):
            ref[k] = piece

    lay(adj_ref[...], flat + [v[0:1] for v in n[:2]], deep + [v[1:2] for v in n[:2]] + [v[2:3] for v in n], tgt_ref)
    lay(dir_ref[...], flat + [none], deep + a + [none], src_ref)


def pack(positions, normals, areas, direct, adjoint):
    panels = positions.shape[1]
    out = [jax.ShapeDtypeStruct((count, DEPTH, LANES), BF16) for count in (NTGT, NSRC)]
    return pl.pallas_call(pack_kernel, out_shape=out, name="pack")(
        positions, normals, areas.reshape(1, panels), direct, adjoint
    )


def unpack(ref, k, cols):
    geo = []
    for m in (k, k + 1):
        piece = ref[m].astype(F32)
        cols[m * COLS : m * COLS + HALF, :] = piece[:HALF, :COLS].astype(BF16)
        cols[m * COLS + HALF : (m + 1) * COLS, :] = piece[:HALF, COLS:].astype(BF16)
        geo.append(piece[HALF:])
    return (
        jnp.concatenate([geo[0][:, :COLS], geo[1][:, :COLS]], axis=1),
        jnp.concatenate([geo[0][:, COLS:], geo[1][:, COLS:]], axis=1),
    )


ROWS = 16
CHUNK = 256


def device_place():
    at = {name: lax.axis_index(name) for name in NAMES}
    rho = at["y"] * PARTS["core"] + at["core"]
    return rho, (at["z_lo"] * PARTS["x"] + at["x"]) * PARTS["z_hi"] + at["z_hi"]


def mix_rows(counts_ref, owner_ref, lists_ref, mix_ref):
    rho, gamma = device_place()
    nx, ncol = PARTS["x"], PARTS["x"] * PARTS["z_hi"]
    holder = ((gamma // ncol) * NTGT + rho) * ncol + gamma % ncol

    def iota(shape, dim):
        return lax.broadcasted_iota(jnp.int32, shape, dim)

    square = (NPATCH, NPATCH)
    counts = jnp.broadcast_to(counts_ref[...], square)
    eye = iota(square, 0) == iota(square, 1)
    starts = jnp.sum(jnp.where(iota(square, 1) < iota(square, 0), counts, 0).astype(F32), axis=1, keepdims=True)
    own_counts = jnp.sum(jnp.where(eye, counts, 0).astype(F32), axis=1, keepdims=True)
    lines = (NPATCH, NBLK)
    ids = iota(lines, 1).astype(F32)
    inside = (starts <= ids) & (ids < starts + own_counts)
    owner = jnp.broadcast_to(owner_ref[...], square)
    place = iota(square, 0)
    output = ((place % 4) // 2) * (2 * NTGT) + 2 * (place // 4) + place % 2
    owned = jnp.where(owner == output, 1.0, 0.0).astype(BF16)
    listed = jnp.max(jnp.where(lists_ref[...] == holder, 1.0, 0.0), axis=0, keepdims=True)
    member = jnp.where(inside, jnp.broadcast_to(listed, lines), 0.0).astype(BF16)
    by_block = jnp.dot(owned, member, preferred_element_type=F32).astype(BF16)
    cut = (NBLK, NBLK // 2)
    k = iota(cut, 1)
    for high in range(2):
        rho_k = high * 8 + k % 8
        block = (k // (8 * nx)) * (NTGT * nx) + rho_k * nx + (k // 8) % nx
        order = jnp.where(iota(cut, 0) == block, 1.0, 0.0).astype(BF16)
        part = jnp.dot(by_block, order, preferred_element_type=F32).astype(BF16)
        mix_ref[high * NPATCH : (high + 1) * NPATCH, :] = part


def tile_kernel(
    tgt_ref, src_ref, counts_ref, owner_ref, lists_ref, row_ref, col_ref, mix_ref, own_ref,
    tcols, scols, tgeo, sgeo, images, rowacc, colacc,
):
    mix_rows(counts_ref, owner_ref, lists_ref, mix_ref)
    rho, _ = device_place()
    at_row = lax.broadcasted_iota(jnp.int32, own_ref.shape, 0) == rho % 8
    at_lane = lax.broadcasted_iota(jnp.int32, own_ref.shape, 1) // COLS == rho // 8
    own_ref[...] = jnp.where(at_row & at_lane, 1.0, 0.0)
    targets, sources = tcols.shape[0], scols.shape[0]
    contract_first, contract_last = (((0,), (0,)), ((), ())), (((1,), (1,)), ((), ()))
    part = lax.broadcasted_iota(jnp.int32, (16, LANES), 0)
    chosen = []
    for parts in (X, Y, Z, NX, NY, NZ):
        hit = part == parts[0]
        for m in parts[1:]:
            hit = hit | (part == m)
        chosen.append(jnp.where(hit, 1.0, 0.0))
    chosen = jnp.concatenate(chosen, axis=1).astype(BF16)
    for g in range(targets // LANES):
        here = slice(g * LANES, (g + 1) * LANES)
        geo = jnp.concatenate(unpack(tgt_ref, 2 * g, tcols), axis=0).astype(BF16)
        wide = lax.dot_general(geo, chosen, contract_first, preferred_element_type=F32)
        for k in range(6):
            tgeo[k, here, :] = wide[:, k * LANES : (k + 1) * LANES]
        z, nz = wide[:, 2 * LANES : 3 * LANES], wide[:, 5 * LANES :]
        tgeo[6, here, :] = (WAVE_SCALE * nz) * jnp.exp((wave_number / TURNS) * z)
    for g in range(sources // LANES):
        here = slice(g * LANES, (g + 1) * LANES)
        left, right = unpack(src_ref, 2 * g, scols)

        def line(value, parts):
            a, b, c = (value[m % 8 : m % 8 + 1, :] for m in parts)
            return jnp.broadcast_to(a + b + c, (8, LANES))

        z, area = line(right, Z), line(right, AREA)
        sgeo[0, :, here] = line(left, X)
        sgeo[1, :, here] = line(left, Y)
        sgeo[2, :, here] = z
        sgeo[3, :, here] = area
        sgeo[4, :, here] = (area * (1.0 / TURNS**2)) * jnp.exp((wave_number / TURNS) * z)
        sgeo[5, :, here] = area * (AREA_SCALE / TURNS**2)
    rowacc[...] = jnp.zeros_like(rowacc)

    def chunk(j, _):
        s0 = pl.multiple_of(j * CHUNK, CHUNK)
        images[...] = lax.dot_general(
            tcols[...],
            scols[pl.ds(s0, CHUNK), :],
            contract_last,
            preferred_element_type=F32,
        )
        halves = range(CHUNK // LANES)

        def wide(k, h):
            v = sgeo[k, :, pl.ds(pl.multiple_of(s0 + h * LANES, LANES), LANES)]
            return jnp.concatenate([v] * (ROWS // 8), axis=0)

        src = [[wide(k, h) for k in range(6)] for h in halves]

        def step(i, acc):
            t0 = pl.multiple_of(i * ROWS, ROWS)
            xt, yt, zt, nx, ny, nz, amp = (tgeo[k, pl.ds(t0, ROWS), :] for k in range(7))
            zt4, nz2 = 4.0 * zt, 2.0 * nz
            new, total = [], rowacc[pl.ds(t0, ROWS), :]
            for h in halves:
                xs, ys, zs, area, ebb, share = src[h]
                dx, dy, dz = xt - xs, yt - ys, zt - zs
                flat = dx * dx + dy * dy + area
                near = flat + dz * dz
                mirror = near + zt4 * zs
                top = nx * dx + ny * dy + nz * dz
                topi = top + nz2 * zs
                i1, i2, i3 = lax.rsqrt(near), lax.rsqrt(mirror), lax.rsqrt(flat)
                pair = top * (i1 * i1 * i1) + topi * (i2 * i2 * i2)
                phase = flat * i3
                f = phase - ((phase + ROUNDER) - ROUNDER)
                g = f * f
                p = g + MONIC[-1]
                for c in MONIC[-2::-1]:
                    p = p * g + c
                kern = share * pair - (amp * ebb) * p
                w = kern.astype(BF16).astype(F32) * images[pl.ds(t0, ROWS), h * LANES : (h + 1) * LANES]
                new.append(acc[h] + w)
                total = total + w
            rowacc[pl.ds(t0, ROWS), :] = total
            return tuple(new)

        zero = jnp.zeros((ROWS, LANES), F32)
        acc = lax.fori_loop(0, targets // ROWS, step, (zero,) * len(halves), unroll=4)
        for h in halves:
            colacc[0:1, pl.ds(pl.multiple_of(s0 + h * LANES, LANES), LANES)] = jnp.sum(acc[h], axis=0, keepdims=True)
        return 0

    lax.fori_loop(0, sources // CHUNK, chunk, 0)
    panels = col_ref.shape[2]
    for k in range(col_ref.shape[0]):
        col_ref[k] = colacc[0:1, k * panels : (k + 1) * panels]
    for g in range(targets // LANES):
        line = jnp.sum(rowacc[g * LANES : (g + 1) * LANES, :].T, axis=0, keepdims=True)
        for k in range(2):
            low, high = (2 * g + k) % 8, (2 * g + k) // 8
            row_ref[low : low + 1, high * panels : (high + 1) * panels] = line[:, k * panels : (k + 1) * panels]


def tile(tgt, src, patch_counts, patch_owner, block_lists, panels):
    targets, sources = tgt.shape[0] * panels, src.shape[0] * panels
    return pl.pallas_call(
        tile_kernel,
        out_shape=(
            jax.ShapeDtypeStruct((8, LANES), F32),
            jax.ShapeDtypeStruct((src.shape[0], 1, panels), F32),
            jax.ShapeDtypeStruct((2 * NPATCH, NBLK // 2), BF16),
            jax.ShapeDtypeStruct((8, LANES), F32),
        ),
        scratch_shapes=[
            pltpu.VMEM((targets, COLS), BF16),
            pltpu.VMEM((sources, COLS), BF16),
            pltpu.VMEM((7, targets, LANES), F32),
            pltpu.VMEM((6, 8, sources), F32),
            pltpu.VMEM((targets, CHUNK), F32),
            pltpu.VMEM((targets, LANES), F32),
            pltpu.VMEM((1, sources), F32),
        ],
        compiler_params=pltpu.CompilerParams(vmem_limit_bytes=24 << 20),
        name="tile",
    )(tgt, src, patch_counts.reshape(1, NPATCH), patch_owner.reshape(1, NPATCH), block_lists.T)


def patch_kernel(mix_ref, dens_ref, spline_ref, out_ref, own_ref):
    quarters = PARTS["z_hi"]
    panels = own_ref.shape[1]
    dens = jnp.concatenate(
        [
            jnp.concatenate([dens_ref[k] for k in range(q, dens_ref.shape[0], quarters)], axis=0)
            for q in range(quarters)
        ],
        axis=1,
    )
    mix = mix_ref[...]
    both = sum(jnp.dot(mix, part, preferred_element_type=F32) for part in split3(dens)[::-1])
    got = jnp.concatenate(
        [
            both[:NPATCH, q * LANES : q * LANES + panels] + both[NPATCH:, q * LANES + panels : (q + 1) * LANES]
            for q in range(quarters)
        ],
        axis=1,
    )
    spline = spline_ref[...]
    rows = sum(jnp.dot(part, spline, preferred_element_type=F32) for part in split3(got)[::-1])
    depth = out_ref.shape[1]
    for piece in range(out_ref.shape[0]):
        out_ref[piece] = rows[piece * depth : (piece + 1) * depth]
    rho, gamma = device_place()
    line = dens_ref[gamma, pl.ds(rho % 8, 1), :]
    own_ref[...] = jnp.where(rho // 8 == 0, line[:, :panels], line[:, panels:])


def patch(mix, blocks, spline, panels):
    return pl.pallas_call(
        patch_kernel,
        out_shape=(
            jax.ShapeDtypeStruct((NTGT, NPATCH // NTGT, spline.shape[1]), F32),
            jax.ShapeDtypeStruct((1, panels), F32),
        ),
        compiler_params=pltpu.CompilerParams(vmem_limit_bytes=16 << 20),
        name="patch",
    )(mix, blocks, spline)


def exchange(pieces, axes):
    return lax.all_to_all(pieces, axes, 0, 0, tiled=True)


def copies(value, count):
    return jnp.broadcast_to(value[None], (count,) + value.shape)


def on_device(
    positions, normals, areas, direct, adjoint, spline, block_lists, patch_counts, patch_owner
):
    panels = positions.shape[1]
    tgt, src = pack(positions, normals, areas, direct, adjoint)
    src_all = exchange(src, SRC_AXES)
    tgt_all = exchange(tgt, TGT_AXES)
    row_part, col_part, mix, own_place = tile(tgt_all, src_all, patch_counts, patch_owner, block_lists, panels)

    mine = jnp.sum(exchange(col_part, SRC_AXES), axis=0)
    row_part = row_part + own_place * jnp.tile(mine, (1, 2))
    dens = jnp.sum(exchange(copies(row_part, NTGT), TGT_AXES), axis=0)
    blocks = exchange(copies(dens, NSRC), SRC_AXES)

    contrib, own = patch(mix, blocks, spline[0], panels)
    rows = jnp.sum(exchange(contrib, TGT_AXES), axis=0)
    low = PARTS["z_lo"]
    rows = rows.reshape(low, 1, rows.shape[0] // low, rows.shape[1])
    rows = jnp.broadcast_to(rows, (low, NSRC // low) + rows.shape[2:]).reshape((NSRC,) + rows.shape[2:])
    patch_grad = jnp.sum(exchange(rows, SRC_AXES), axis=0)
    return own.reshape(panels), patch_grad


def solution(mesh):
    fine = Mesh(mesh.devices.reshape(tuple(PARTS.values())), NAMES)
    placed = (
        P(None, NAMES),
        P(None, NAMES),
        P(NAMES),
        P(NAMES, None),
        P(NAMES, None),
        P(NAMES, None, None),
        P(),
        P(),
        P(),
    )
    return jax.shard_map(
        on_device,
        mesh=fine,
        in_specs=placed,
        out_specs=(P(NAMES), P(("z_lo", "y", "core"), None)),
        check_vma=False,
    )
```

```python
import jax
import jax.numpy as jnp
import numpy as np
from jax import lax
from jax.experimental import pallas as pl
from jax.experimental.pallas import tpu as pltpu
from jax.sharding import Mesh
from jax.sharding import PartitionSpec as P

F32 = jnp.float32
BF16 = jnp.bfloat16
BPAN = 256
NPATCH = 64
NBLK = 128
LANES = 128
wave_number = 6.0
inv_four_pi = 0.07957747154594767

TURNS = wave_number / (2.0 * np.pi)
DEGREE = 5


def cosine_coefficients():
    k = np.arange(64)
    nodes = 0.125 + 0.125 * np.cos(np.pi * (2 * k + 1) / 128)
    fit = np.polynomial.chebyshev.Chebyshev.fit(
        nodes, np.cos(2 * np.pi * np.sqrt(nodes)), DEGREE, domain=[0.0, 0.25]
    )
    return fit.convert(kind=np.polynomial.Polynomial).coef


COEF = cosine_coefficients()
LEAD = float(COEF[-1])
MONIC = [float(c / COEF[-1]) for c in COEF[:-1]]
ROUNDER = float(3 << 22)
AREA_SCALE = float(TURNS**2 * inv_four_pi)
WAVE_SCALE = float(2.0 * wave_number * inv_four_pi * LEAD)

PARTS = {"z_lo": 2, "y": 8, "core": 2, "x": 4, "z_hi": 4}
NAMES = tuple(PARTS)
TGT_AXES = ("y", "core")
SRC_AXES = ("z_lo", "x", "z_hi")
NTGT = PARTS["y"] * PARTS["core"]
NSRC = PARTS["z_lo"] * PARTS["x"] * PARTS["z_hi"]

COLS = 64
HALF = 32
DEPTH = 40
X, Y, Z = (0, 2, 4), (1, 3, 5), (8, 9, 10)
NX, NY, NZ = (6, 7), (11, 12), (13, 14)
AREA = (11, 12, 13)

T_DOT, T_AMP, T_SQUARE, T_ONE, T_ROWS = 16, 19, 22, 25, 32
S_MOMENT, S_SHARE, S_SQUARE, S_ONE, S_ROWS = 16, 25, 28, 31, 32


def product_lanes():
    left, right = [], [{}, {}, {}]
    for d, n in enumerate((NX, NY, NZ)):
        for a in range(2):
            for b in range(3):
                lane = len(left)
                left.append(n[a])
                right[0][lane] = (S_MOMENT + 3 * d + b, -1.0)
                right[1][lane] = (S_MOMENT + 3 * d + b, 1.0 if d == 2 else -1.0)
    for a in range(3):
        for b in range(3):
            lane = len(left)
            left.append(T_DOT + a)
            right[0][lane] = right[1][lane] = (S_SHARE + b, 1.0)
    for d, p in enumerate((X, Y, Z)):
        for a in range(3):
            for b in range(3):
                right[2][len(left)] = (p[b], 2.0 if d == 2 else -2.0)
                left.append(p[a])
    for a in range(3):
        right[2][len(left)] = (S_ONE, 1.0)
        left.append(T_SQUARE + a)
    for b in range(3):
        right[2][len(left)] = (S_SQUARE + b, 1.0)
        left.append(T_ONE)
    return dict(enumerate(left)), right


LEFT, RIGHT = product_lanes()


def selector(rows, entries):
    lane = lax.broadcasted_iota(jnp.int32, (8, LANES), 1)
    where, value = jnp.full((8, LANES), -1, jnp.int32), jnp.zeros((8, LANES), F32)
    for key, (row, sign) in entries.items():
        where = jnp.where(lane == key, row, where)
        value = jnp.where(lane == key, sign, value)
    at = lax.broadcasted_iota(jnp.int32, (rows, LANES), 0)
    many = (rows // 8, 1)
    return jnp.where(at == jnp.tile(where, many), jnp.tile(value, many), 0.0)


def split3(v):
    hi = v.astype(BF16)
    rest = v - hi.astype(F32)
    mid = rest.astype(BF16)
    lo = (rest - mid.astype(F32)).astype(BF16)
    return hi, mid, lo


def pack_kernel(pos_ref, nrm_ref, area_ref, dir_ref, adj_ref, tgt_ref, src_ref):
    pos = pos_ref[...]
    row = lax.broadcasted_iota(jnp.int32, pos.shape, 0)
    pos = jnp.where(row == 2, 0.5 * (pos - 1.2), pos) * TURNS
    p = [v.astype(F32) for v in split3(pos)]
    n = [v.astype(F32) for v in split3(nrm_ref[...])]
    a = [v.astype(F32) for v in split3(area_ref[...] * TURNS**2)]
    flat = [v[0:2] for v in p]
    deep = [v[2:3] for v in p]
    none = jnp.zeros((2, pos.shape[1]), F32)

    def lay(top, left, right, ref):
        geo = jnp.concatenate([jnp.concatenate(left, axis=0), jnp.concatenate(right, axis=0)], axis=1)
        top = jnp.concatenate([top[:HALF], top[HALF:]], axis=1)
        piece = jnp.concatenate([top, geo], axis=0).astype(BF16)
        for k in range(ref.shape[0]):
            ref[k] = piece

    nx, ny, nz = ([v[k : k + 1] for v in n[:2]] for k in range(3))
    lay(adj_ref[...].astype(F32), flat + nx, deep + ny + nz + [none[:1]], tgt_ref)
    lay(dir_ref[...].astype(F32).T, flat + [none], deep + a + [none], src_ref)


def pack(positions, normals, areas, direct, adjoint):
    panels = positions.shape[1]
    out = [jax.ShapeDtypeStruct((count, DEPTH, LANES), BF16) for count in (NTGT, NSRC)]
    return pl.pallas_call(pack_kernel, out_shape=out, name="pack")(
        positions, normals, areas.reshape(1, panels), direct, adjoint
    )


def beside(a, b):
    return (
        jnp.concatenate([a[:, :COLS], b[:, :COLS]], axis=1),
        jnp.concatenate([a[:, COLS:], b[:, COLS:]], axis=1),
    )


def total(value, parts):
    return sum(value[m : m + 1, :] for m in parts)


def three(v):
    return [part.astype(F32) for part in split3(v)]


ROWS = 16, 19, 22, 25, 32
S_MOMENT, S_SHARE, S_SQUARE, S_ONE, S_ROWS = 16, 25, 28, 31, 32


def product_lanes():
    left, right = [], [{}, {}, {}]
    for d, n in enumerate((NX, NY, NZ)):
        for a in range(2):
            for b in range(3):
                lane = len(left)
                left.append(n[a])
                right[0][lane] = (S_MOMENT + 3 * d + b, -1.0)
                right[1][lane] = (S_MOMENT + 3 * d + b, 1.0 if d == 2 else -1.0)
    for a in range(3):
        for b in range(3):
            lane = len(left)
            left.append(T_DOT + a)
            right[0][lane] = right[1][lane] = (S_SHARE + b, 1.0)
    for d, p in enumerate((X, Y, Z)):
        for a in range(3):
            for b in range(3):
                right[2][len(left)] = (p[b], 2.0 if d == 2 else -2.0)
                left.append(p[a])
    for a in range(3):
        right[2][len(left)] = (S_ONE, 1.0)
        left.append(T_SQUARE + a)
    for b in range(3):
        right[2][len(left)] = (S_SQUARE + b, 1.0)
        left.append(T_ONE)
    return dict(enumerate(left)), right


LEFT, RIGHT = product_lanes()


def selector(rows, entries):
    lane = lax.broadcasted_iota(jnp.int32, (8, LANES), 1)
    where, value = jnp.full((8, LANES), -1, jnp.int32), jnp.zeros((8, LANES), F32)
    for key, (row, sign) in entries.items():
        where = jnp.where(lane == key, row, where)
        value = jnp.where(lane == key, sign, value)
    at = lax.broadcasted_iota(jnp.int32, (rows, LANES), 0)
    many = (rows // 8, 1)
    return jnp.where(at == jnp.tile(where, many), jnp.tile(value, many), 0.0)


def split3(v):
    hi = v.astype(BF16)
    rest = v - hi.astype(F32)
    mid = rest.astype(BF16)
    lo = (rest - mid.astype(F32)).astype(BF16)
    return hi, mid, lo


def pack_kernel(pos_ref, nrm_ref, area_ref, dir_ref, adj_ref, tgt_ref, src_ref):
    pos = pos_ref[...]
    row = lax.broadcasted_iota(jnp.int32, pos.shape, 0)
    pos = jnp.where(row == 2, 0.5 * (pos - 1.2), pos) * TURNS
    p = [v.astype(F32) for v in split3(pos)]
    n = [v.astype(F32) for v in split3(nrm_ref[...])]
    a = [v.astype(F32) for v in split3(area_ref[...] * TURNS**2)]
    flat = [v[0:2] for v in p]
    deep = [v[2:3] for v in p]
    none = jnp.zeros((2, pos.shape[1]), F32)

    def lay(top, left, right, ref):
        geo = jnp.concatenate([jnp.concatenate(left, axis=0), jnp.concatenate(right, axis=0)], axis=1)
        top = jnp.concatenate([top[:HALF], top[HALF:]], axis=1)
        piece = jnp.concatenate([top, geo], axis=0).astype(BF16)
        for k in range(ref.shape[0]):
            ref[k] = piece

    nx, ny, nz = ([v[k : k + 1] for v in n[:2]] for k in range(3))
    lay(adj_ref[...].astype(F32), flat + nx, deep + ny + nz + [none[:1]], tgt_ref)
    lay(dir_ref[...].astype(F32).T, flat + [none], deep + a + [none], src_ref)


def pack(positions, normals, areas, direct, adjoint):
    panels = positions.shape[1]
    out = [jax.ShapeDtypeStruct((count, DEPTH, LANES), BF16) for count in (NTGT, NSRC)]
    return pl.pallas_call(pack_kernel, out_shape=out, name="pack")(
        positions, normals, areas.reshape(1, panels), direct, adjoint
    )


def unpack(ref, k, cols):
    geo = []
    for m in (k, k + 1):
        piece = ref[m].astype(F32)
        cols[m * COLS : m * COLS + HALF, :] = piece[:HALF, :COLS].astype(BF16)
        cols[m * COLS + HALF : (m + 1) * COLS, :] = piece[:HALF, COLS:].astype(BF16)
        geo.append(piece[HALF:])
    return (
        jnp.concatenate([geo[0][:, :COLS], geo[1][:, :COLS]], axis=1),
        jnp.concatenate([geo[0][:, COLS:], geo[1][:, COLS:]], axis=1),
    )


ROWS = 16
CHUNK = 256
STEP = 256


def device_place():
    at = {name: lax.axis_index(name) for name in NAMES}
    rho = at["y"] * PARTS["core"] + at["core"]
    return rho, (at["z_lo"] * PARTS["x"] + at["x"]) * PARTS["z_hi"] + at["z_hi"]


def mix_rows(counts_ref, owner_ref, lists_ref, mix_ref):
    rho, gamma = device_place()
    nx, ncol = PARTS["x"], PARTS["x"] * PARTS["z_hi"]
    holder = ((gamma // ncol) * NTGT + rho) * ncol + gamma % ncol

    def iota(shape, dim):
        return lax.broadcasted_iota(jnp.int32, shape, dim)

    square = (NPATCH, NPATCH)
    counts = jnp.broadcast_to(counts_ref[...], square)
    eye = iota(square, 0) == iota(square, 1)
    starts = jnp.sum(jnp.where(iota(square, 1) < iota(square, 0), counts, 0).astype(F32), axis=1, keepdims=True)
    own_counts = jnp.sum(jnp.where(eye, counts, 0).astype(F32), axis=1, keepdims=True)
    lines = (NPATCH, NBLK)
    ids = iota(lines, 1).astype(F32)
    inside = (starts <= ids) & (ids < starts + own_counts)
    owner = jnp.broadcast_to(owner_ref[...], square)
    place = iota(square, 0)
    output = ((place % 4) // 2) * (2 * NTGT) + 2 * (place // 4) + place % 2
    owned = jnp.where(owner == output, 1.0, 0.0).astype(BF16)
    listed = jnp.max(jnp.where(lists_ref[...] == holder, 1.0, 0.0), axis=0, keepdims=True)
    member = jnp.where(inside, jnp.broadcast_to(listed, lines), 0.0).astype(BF16)
    by_block = jnp.dot(owned, member, preferred_element_type=F32).astype(BF16)
    cut = (NBLK, NBLK // 2)
    k = iota(cut, 1)
    for high in range(2):
        rho_k = high * 8 + k % 8
        block = (k // (8 * nx)) * (NTGT * nx) + rho_k * nx + (k // 8) % nx
        order = jnp.where(iota(cut, 0) == block, 1.0, 0.0).astype(BF16)
        part = jnp.dot(by_block, order, preferred_element_type=F32).astype(BF16)
        mix_ref[high * NPATCH : (high + 1) * NPATCH, :] = part


def tile_kernel(
    tgt_ref, src_ref, counts_ref, owner_ref, lists_ref, row_ref, col_ref, mix_ref, own_ref,
    tcols, scols, tfeat, sfeat, tgeo, sgeo, even, odd, rowacc, colacc,
):
    mix_rows(counts_ref, owner_ref, lists_ref, mix_ref)
    rho, _ = device_place()
    at_row = lax.broadcasted_iota(jnp.int32, own_ref.shape, 0) == rho % 8
    at_lane = lax.broadcasted_iota(jnp.int32, own_ref.shape, 1) // COLS == rho // 8
    own_ref[...] = jnp.where(at_row & at_lane, 1.0, 0.0)
    targets, sources = tcols.shape[0], scols.shape[1]
    scale = wave_number / TURNS

    part = lax.broadcasted_iota(jnp.int32, (T_ROWS, LANES), 0)
    chosen = [selector(T_ROWS, {lane: (row, 1.0) for lane, row in LEFT.items()})]
    for parts in (X, Y, Z, tuple(range(T_AMP, T_AMP + 3))):
        chosen.append(jnp.where((part == parts[0]) | (part == parts[1]) | (part == parts[2]), 1.0, 0.0))
    chosen = jnp.concatenate(chosen, axis=1).astype(BF16)
    for g in range(targets // LANES):
        here = slice(g * LANES, (g + 1) * LANES)
        pieces = [tgt_ref[m].astype(F32) for m in (2 * g, 2 * g + 1)]
        for m, piece in enumerate(pieces):
            row = g * LANES + m * COLS
            tcols[row : row + HALF, :] = piece[:HALF, :COLS].astype(BF16)
            tcols[row + HALF : row + COLS, :] = piece[:HALF, COLS:].astype(BF16)
        geo = jnp.concatenate(beside(*(p[HALF:] for p in pieces)), axis=0)
        x, y, z, nx, ny, nz = (total(geo, parts) for parts in (X, Y, Z, NX, NY, NZ))
        rows = three(nx * x + ny * y + nz * z) + three((WAVE_SCALE * nz) * jnp.exp(scale * z)) + three(x * x + y * y + z * z)
        rows = [geo] + rows + [jnp.ones_like(x), jnp.zeros((T_ROWS - T_ONE - 1, LANES), F32)]
        wide = lax.dot_general(
            jnp.concatenate(rows, axis=0).astype(BF16), chosen, (((0,), (0,)), ((), ())), preferred_element_type=F32
        )
        tfeat[here, :] = wide[:, :LANES].astype(BF16)
        for k in range(4):
            tgeo[k, here, :] = wide[:, (k + 1) * LANES : (k + 2) * LANES]
    rights = [selector(S_ROWS, entries).T.astype(BF16) for entries in RIGHT]
    for g in range(sources // LANES):
        here = slice(g * LANES, (g + 1) * LANES)
        left, right = beside(*(src_ref[m].astype(F32) for m in (2 * g, 2 * g + 1)))
        scols[:HALF, here] = left[:HALF].astype(BF16)
        scols[HALF:, here] = right[:HALF].astype(BF16)
        geo = jnp.concatenate([left[HALF:], right[HALF:]], axis=0)
        x, y, z, area = (total(geo, parts) for parts in (X, Y, Z, AREA))
        share = area * (AREA_SCALE / TURNS**2)
        rows = three(share * x) + three(share * y) + three(share * z) + three(share)
        rows += three(x * x + y * y + z * z + area)
        rows = jnp.concatenate([geo] + rows + [jnp.ones_like(x)], axis=0).astype(BF16)
        for k in range(3):
            sfeat[k, :, here] = jnp.dot(rights[k], rows, preferred_element_type=F32).astype(BF16)
        for k, v in enumerate((x, y, z, area, (area * (1.0 / TURNS**2)) * jnp.exp(scale * z))):
            sgeo[k, :, here] = jnp.broadcast_to(v, (8, LANES))
    rowacc[...] = jnp.zeros_like(rowacc)
    colacc[...] = jnp.zeros_like(colacc)
    blocks = targets // STEP
    steps = blocks * (sources // CHUNK)

    def corner(k):
        return pl.multiple_of(lax.rem(k, blocks) * STEP, STEP), pl.multiple_of(lax.div(k, blocks) * CHUNK, CHUNK)

    def products(k, into):
        t0, s0 = corner(k)
        features = tfeat[pl.ds(t0, STEP), :]
        for m in range(3):
            into[m] = jnp.dot(features, sfeat[m, :, pl.ds(s0, CHUNK)], preferred_element_type=F32)
        into[3] = jnp.dot(tcols[pl.ds(t0, STEP), :], scols[:, pl.ds(s0, CHUNK)], preferred_element_type=F32)

    halves = range(CHUNK // LANES)

    def elements(k, made):
        t0, s0 = corner(k)
        lanes = [pl.ds(pl.multiple_of(s0 + h * LANES, LANES), LANES) for h in halves]
        src = [[jnp.concatenate([sgeo[m, :, lanes[h]]] * (ROWS // 8), axis=0) for m in range(5)] for h in halves]
        acc = [None for _ in halves]
        for r in range(0, STEP, ROWS):
            rows = pl.ds(pl.multiple_of(t0 + r, ROWS), ROWS)
            xt, yt, zt, amp = (tgeo[m, rows, :] for m in range(4))
            along = rowacc[rows, :]
            for h in halves:
                top, topi, mirror, image = (made[m, r : r + ROWS, h * LANES : (h + 1) * LANES] for m in range(4))
                xs, ys, zs, area, ebb = src[h]
                dx, dy, dz = xt - xs, yt - ys, zt - zs
                flat = dx * dx + dy * dy + area
                near = flat + dz * dz
                i1, i2, i3 = lax.rsqrt(near), lax.rsqrt(mirror), lax.rsqrt(flat)
                pair = top * (i1 * i1 * i1) + topi * (i2 * i2 * i2)
                phase = flat * i3
                f = phase - ((phase + ROUNDER) - ROUNDER)
                g = f * f
                p = g + MONIC[-1]
                for c in MONIC[-2::-1]:
                    p = p * g + c
                kern = pair - (amp * ebb) * p
                w = kern.astype(BF16).astype(F32) * image
                acc[h] = w if acc[h] is None else acc[h] + w
                along = along + w
            rowacc[rows, :] = along
        for h in halves:
            colacc[:, lanes[h]] += sum(acc[h][m : m + 8] for m in range(0, ROWS, 8))

    products(0, even)

    def two(k, _):
        elements(2 * k, even)
        products(2 * k + 1, odd)
        elements(2 * k + 1, odd)
        products(jnp.minimum(2 * k + 2, steps - 1), even)
        return 0

    lax.fori_loop(0, steps // 2, two, 0)
    for g in range(sources // LANES):
        here = slice(g * LANES, (g + 1) * LANES)
        colacc[0:1, here] = jnp.sum(colacc[:, here], axis=0, keepdims=True)
    panels = col_ref.shape[2]
    for k in range(col_ref.shape[0]):
        col_ref[k] = colacc[0:1, k * panels : (k + 1) * panels]
    for g in range(targets // LANES):
        line = jnp.sum(rowacc[g * LANES : (g + 1) * LANES, :].T, axis=0, keepdims=True)
        for k in range(2):
            low, high = (2 * g + k) % 8, (2 * g + k) // 8
            row_ref[low : low + 1, high * panels : (high + 1) * panels] = line[:, k * panels : (k + 1) * panels]


def tile(tgt, src, patch_counts, patch_owner, block_lists, panels):
    targets, sources = tgt.shape[0] * panels, src.shape[0] * panels
    return pl.pallas_call(
        tile_kernel,
        out_shape=(
            jax.ShapeDtypeStruct((8, LANES), F32),
            jax.ShapeDtypeStruct((src.shape[0], 1, panels), F32),
            jax.ShapeDtypeStruct((2 * NPATCH, NBLK // 2), BF16),
            jax.ShapeDtypeStruct((8, LANES), F32),
        ),
        scratch_shapes=[
            pltpu.VMEM((targets, COLS), BF16),
            pltpu.VMEM((COLS, sources), BF16),
            pltpu.VMEM((targets, LANES), BF16),
            pltpu.VMEM((3, LANES, sources), BF16),
            pltpu.VMEM((4, targets, LANES), F32),
            pltpu.VMEM((5, 8, sources), F32),
            pltpu.VMEM((4, STEP, CHUNK), F32),
            pltpu.VMEM((4, STEP, CHUNK), F32),
            pltpu.VMEM((targets, LANES), F32),
            pltpu.VMEM((8, sources), F32),
        ],
        compiler_params=pltpu.CompilerParams(vmem_limit_bytes=24 << 20),
        name="tile",
    )(tgt, src, patch_counts.reshape(1, NPATCH), patch_owner.reshape(1, NPATCH), block_lists.T)


def patch_kernel(mix_ref, dens_ref, spline_ref, out_ref, own_ref):
    quarters = PARTS["z_hi"]
    panels = own_ref.shape[1]
    dens = jnp.concatenate(
        [
            jnp.concatenate([dens_ref[k] for k in range(q, dens_ref.shape[0], quarters)], axis=0)
            for q in range(quarters)
        ],
        axis=1,
    )
    mix = mix_ref[...]
    both = sum(jnp.dot(mix, part, preferred_element_type=F32) for part in split3(dens)[::-1])
    got = jnp.concatenate(
        [
            both[:NPATCH, q * LANES : q * LANES + panels] + both[NPATCH:, q * LANES + panels : (q + 1) * LANES]
            for q in range(quarters)
        ],
        axis=1,
    )
    spline = spline_ref[...]
    rows = sum(jnp.dot(part, spline, preferred_element_type=F32) for part in split3(got)[::-1])
    depth = out_ref.shape[1]
    for piece in range(out_ref.shape[0]):
        out_ref[piece] = rows[piece * depth : (piece + 1) * depth]
    rho, gamma = device_place()
    line = dens_ref[gamma, pl.ds(rho % 8, 1), :]
    own_ref[...] = jnp.where(rho // 8 == 0, line[:, :panels], line[:, panels:])


def patch(mix, blocks, spline, panels):
    return pl.pallas_call(
        patch_kernel,
        out_shape=(
            jax.ShapeDtypeStruct((NTGT, NPATCH // NTGT, spline.shape[1]), F32),
            jax.ShapeDtypeStruct((1, panels), F32),
        ),
        compiler_params=pltpu.CompilerParams(vmem_limit_bytes=16 << 20),
        name="patch",
    )(mix, blocks, spline)


def exchange(pieces, axes):
    return lax.all_to_all(pieces, axes, 0, 0, tiled=True)


def copies(value, count):
    return jnp.broadcast_to(value[None], (count,) + value.shape)


def on_device(
    positions, normals, areas, direct, adjoint, spline, block_lists, patch_counts, patch_owner
):
    panels = positions.shape[1]
    tgt, src = pack(positions, normals, areas, direct, adjoint)
    src_all = exchange(src, SRC_AXES)
    tgt_all = exchange(tgt, TGT_AXES)
    row_part, col_part, mix, own_place = tile(tgt_all, src_all, patch_counts, patch_owner, block_lists, panels)

    mine = jnp.sum(exchange(col_part, SRC_AXES), axis=0)
    row_part = row_part + own_place * jnp.tile(mine, (1, 2))
    dens = jnp.sum(exchange(copies(row_part, NTGT), TGT_AXES), axis=0)
    blocks = exchange(copies(dens, NSRC), SRC_AXES)

    contrib, own = patch(mix, blocks, spline[0], panels)
    rows = jnp.sum(exchange(contrib, TGT_AXES), axis=0)
    low = PARTS["z_lo"]
    rows = rows.reshape(low, 1, rows.shape[0] // low, rows.shape[1])
    rows = jnp.broadcast_to(rows, (low, NSRC // low) + rows.shape[2:]).reshape((NSRC,) + rows.shape[2:])
    patch_grad = jnp.sum(exchange(rows, SRC_AXES), axis=0)
    return own.reshape(panels), patch_grad


def solution(mesh):
    fine = Mesh(mesh.devices.reshape(tuple(PARTS.values())), NAMES)
    placed = (
        P(None, NAMES),
        P(None, NAMES),
        P(NAMES),
        P(NAMES, None),
        P(NAMES, None),
        P(NAMES, None, None),
        P(),
        P(),
        P(),
    )
    return jax.shard_map(
        on_device,
        mesh=fine,
        in_specs=placed,
        out_specs=(P(NAMES), P(("z_lo", "y", "core"), None)),
        check_vma=False,
    )
```

```python
import jax
import jax.numpy as jnp
import numpy as np
from jax import lax
from jax.experimental import pallas as pl
from jax.experimental.pallas import tpu as pltpu
from jax.sharding import Mesh
from jax.sharding import PartitionSpec as P

F32 = jnp.float32
BF16 = jnp.bfloat16
BPAN = 256
NPATCH = 64
NBLK = 128
LANES = 128
wave_number = 6.0
inv_four_pi = 0.07957747154594767

TURNS = wave_number / (2.0 * np.pi)
DEGREE = 3


def sine_coefficients():
    k = np.arange(64)
    nodes = 0.25 * np.cos(np.pi * (2 * k + 1) / 128)
    fit = np.polynomial.chebyshev.Chebyshev.fit(nodes, np.sin(2 * np.pi * nodes), 2 * DEGREE + 1, domain=[-0.25, 0.25])
    return fit.convert(kind=np.polynomial.Polynomial).coef[1::2]


COEF = sine_coefficients()
LEAD = float(COEF[-1])
MONIC = [float(c / COEF[-1]) for c in COEF[:-1]]
ROUNDER = float(3 << 22)
AREA_SCALE = float(TURNS**2 * inv_four_pi)
WAVE_SCALE = float(2.0 * wave_number * inv_four_pi * LEAD)

PARTS = {"z_lo": 2, "y": 8, "core": 2, "x": 4, "z_hi": 4}
NAMES = tuple(PARTS)
TGT_AXES = ("y", "core")
SRC_AXES = ("z_lo", "x", "z_hi")
NTGT = PARTS["y"] * PARTS["core"]
NSRC = PARTS["z_lo"] * PARTS["x"] * PARTS["z_hi"]

COLS = 64
HALF = 32
DEPTH = 40
X, Y, Z = (0, 2, 4), (1, 3, 5), (8, 9, 10)
NX, NY, NZ = (6, 7), (11, 12), (13, 14)
AREA = (11, 12, 13)

T_DOT, T_AMP, T_SQUARE, T_ONE, T_ROWS = 16, 19, 22, 25, 32
S_MOMENT, S_SHARE, S_SQUARE, S_ONE, S_ROWS = 16, 25, 28, 31, 32


def product_lanes():
    left, right = [], [{}, {}, {}]
    for d, n in enumerate((NX, NY, NZ)):
        for a in range(2):
            for b in range(3):
                lane = len(left)
                left.append(n[a])
                right[0][lane] = (S_MOMENT + 3 * d + b, -1.0)
                right[1][lane] = (S_MOMENT + 3 * d + b, 1.0 if d == 2 else -1.0)
    for a in range(3):
        for b in range(3):
            lane = len(left)
            left.append(T_DOT + a)
            right[0][lane] = right[1][lane] = (S_SHARE + b, 1.0)
    for d, p in enumerate((X, Y, Z)):
        for a in range(3):
            for b in range(3):
                right[2][len(left)] = (p[b], 2.0 if d == 2 else -2.0)
                left.append(p[a])
    for a in range(3):
        right[2][len(left)] = (S_ONE, 1.0)
        left.append(T_SQUARE + a)
    for b in range(3):
        right[2][len(left)] = (S_SQUARE + b, 1.0)
        left.append(T_ONE)
    return dict(enumerate(left)), right


LEFT, RIGHT = product_lanes()


def selector(rows, entries):
    lane = lax.broadcasted_iota(jnp.int32, (8, LANES), 1)
    where, value = jnp.full((8, LANES), -1, jnp.int32), jnp.zeros((8, LANES), F32)
    for key, (row, sign) in entries.items():
        where = jnp.where(lane == key, row, where)
        value = jnp.where(lane == key, sign, value)
    at = lax.broadcasted_iota(jnp.int32, (rows, LANES), 0)
    many = (rows // 8, 1)
    return jnp.where(at == jnp.tile(where, many), jnp.tile(value, many), 0.0)


def split3(v):
    hi = v.astype(BF16)
    rest = v - hi.astype(F32)
    mid = rest.astype(BF16)
    lo = (rest - mid.astype(F32)).astype(BF16)
    return hi, mid, lo


def three(v):
    return [part.astype(F32) for part in split3(v)]


def scaled(pos):
    row = lax.broadcasted_iota(jnp.int32, pos.shape, 0)
    parts = three(jnp.where(row == 2, 0.5 * (pos - 1.2), pos) * TURNS)
    return [v[0:2] for v in parts], [v[2:3] for v in parts]


def lay(top, left, right, ref):
    geo = jnp.concatenate([jnp.concatenate(left, axis=0), jnp.concatenate(right, axis=0)], axis=1)
    top = jnp.concatenate([top[:HALF], top[HALF:]], axis=1)
    piece = jnp.concatenate([top, geo], axis=0).astype(BF16)
    for k in range(ref.shape[0]):
        ref[k] = piece


def pack_targets_kernel(pos_ref, nrm_ref, adj_ref, ref):
    flat, deep = scaled(pos_ref[...])
    nx, ny, nz = ([v[k : k + 1] for v in three(nrm_ref[...])[:2]] for k in range(3))
    lay(adj_ref[...].astype(F32), flat + nx, deep + ny + nz + [jnp.zeros_like(deep[0])], ref)


def pack_sources_kernel(pos_ref, area_ref, dir_ref, ref):
    flat, deep = scaled(pos_ref[...])
    none = jnp.zeros((2, pos_ref.shape[1]), F32)
    lay(dir_ref[...].astype(F32).T, flat + [none], deep + three(area_ref[...] * TURNS**2) + [none], ref)


def pack(kernel, count, *arrays):
    out = jax.ShapeDtypeStruct((count, DEPTH, LANES), BF16)
    return pl.pallas_call(kernel, out_shape=out, name="pack")(*arrays)


def beside(a, b):
    return (
        jnp.concatenate([a[:, :COLS], b[:, :COLS]], axis=1),
        jnp.concatenate([a[:, COLS:], b[:, COLS:]], axis=1),
    )


def total(value, parts):
    return sum(value[m : m + 1, :] for m in parts)


ROWS = 16
CHUNK = 256
STEP = 512


def device_place():
    at = {name: lax.axis_index(name) for name in NAMES}
    rho = at["y"] * PARTS["core"] + at["core"]
    return rho, (at["z_lo"] * PARTS["x"] + at["x"]) * PARTS["z_hi"] + at["z_hi"]


def mixing_kernel(counts_ref, owner_ref, lists_ref, mix_ref):
    rho, gamma = device_place()
    nx, ncol = PARTS["x"], PARTS["x"] * PARTS["z_hi"]
    holder = ((gamma // ncol) * NTGT + rho) * ncol + gamma % ncol

    def iota(shape, dim):
        return lax.broadcasted_iota(jnp.int32, shape, dim)

    square = (NPATCH, NPATCH)
    counts = jnp.broadcast_to(counts_ref[...], square)
    eye = iota(square, 0) == iota(square, 1)
    starts = jnp.sum(jnp.where(iota(square, 1) < iota(square, 0), counts, 0).astype(F32), axis=1, keepdims=True)
    own_counts = jnp.sum(jnp.where(eye, counts, 0).astype(F32), axis=1, keepdims=True)
    lines = (NPATCH, NBLK)
    ids = iota(lines, 1).astype(F32)
    inside = (starts <= ids) & (ids < starts + own_counts)
    owner = jnp.broadcast_to(owner_ref[...], square)
    place = iota(square, 0)
    output = ((place % 4) // 2) * (2 * NTGT) + 2 * (place // 4) + place % 2
    owned = jnp.where(owner == output, 1.0, 0.0).astype(BF16)
    listed = jnp.max(jnp.where(lists_ref[...] == holder, 1.0, 0.0), axis=0, keepdims=True)
    member = jnp.where(inside, jnp.broadcast_to(listed, lines), 0.0).astype(BF16)
    by_block = jnp.dot(owned, member, preferred_element_type=F32).astype(BF16)
    cut = (NBLK, NBLK // 2)
    k = iota(cut, 1)
    for high in range(2):
        rho_k = high * 8 + k % 8
        block = (k // (8 * nx)) * (NTGT * nx) + rho_k * nx + (k // 8) % nx
        order = jnp.where(iota(cut, 0) == block, 1.0, 0.0).astype(BF16)
        part = jnp.dot(by_block, order, preferred_element_type=F32).astype(BF16)
        mix_ref[high * NPATCH : (high + 1) * NPATCH, :] = part


def mixing(patch_counts, patch_owner, block_lists):
    return pl.pallas_call(
        mixing_kernel,
        out_shape=jax.ShapeDtypeStruct((2 * NPATCH, NBLK // 2), BF16),
        name="mixing",
    )(patch_counts.reshape(1, NPATCH), patch_owner.reshape(1, NPATCH), block_lists.T)


def tile_kernel(
    tgt_ref, src_ref, row_ref, col_ref, own_ref, tcols, scols, tfeat, sfeat, tgeo, sgeo, even, odd, rowacc, colacc
):
    rho, _ = device_place()
    at_row = lax.broadcasted_iota(jnp.int32, own_ref.shape, 0) == rho % 8
    at_lane = lax.broadcasted_iota(jnp.int32, own_ref.shape, 1) // COLS == rho // 8
    own_ref[...] = jnp.where(at_row & at_lane, 1.0, 0.0)
    targets, sources = tcols.shape[0], scols.shape[1]
    scale = wave_number / TURNS

    part = lax.broadcasted_iota(jnp.int32, (T_ROWS, LANES), 0)
    chosen = [selector(T_ROWS, {lane: (row, 1.0) for lane, row in LEFT.items()})]
    for parts in (X, Y, Z, tuple(range(T_AMP, T_AMP + 3))):
        chosen.append(jnp.where((part == parts[0]) | (part == parts[1]) | (part == parts[2]), 1.0, 0.0))
    chosen = jnp.concatenate(chosen, axis=1).astype(BF16)
    for g in range(targets // LANES):
        here = slice(g * LANES, (g + 1) * LANES)
        pieces = [tgt_ref[m].astype(F32) for m in (2 * g, 2 * g + 1)]
        for m, piece in enumerate(pieces):
            row = g * LANES + m * COLS
            tcols[row : row + HALF, :] = piece[:HALF, :COLS].astype(BF16)
            tcols[row + HALF : row + COLS, :] = piece[:HALF, COLS:].astype(BF16)
        geo = jnp.concatenate(beside(*(p[HALF:] for p in pieces)), axis=0)
        x, y, z, nx, ny, nz = (total(geo, parts) for parts in (X, Y, Z, NX, NY, NZ))
        rows = three(nx * x + ny * y + nz * z) + three((WAVE_SCALE * nz) * jnp.exp(scale * z)) + three(x * x + y * y + z * z)
        rows = [geo] + rows + [jnp.ones_like(x), jnp.zeros((T_ROWS - T_ONE - 1, LANES), F32)]
        wide = lax.dot_general(
            jnp.concatenate(rows, axis=0).astype(BF16), chosen, (((0,), (0,)), ((), ())), preferred_element_type=F32
        )
        tfeat[here, :] = wide[:, :LANES].astype(BF16)
        for k in range(4):
            tgeo[k, here, :] = wide[:, (k + 1) * LANES : (k + 2) * LANES]
    rights = [selector(S_ROWS, entries).T.astype(BF16) for entries in RIGHT]
    for g in range(sources // LANES):
        here = slice(g * LANES, (g + 1) * LANES)
        left, right = beside(*(src_ref[m].astype(F32) for m in (2 * g, 2 * g + 1)))
        scols[:HALF, here] = left[:HALF].astype(BF16)
        scols[HALF:, here] = right[:HALF].astype(BF16)
        geo = jnp.concatenate([left[HALF:], right[HALF:]], axis=0)
        x, y, z, area = (total(geo, parts) for parts in (X, Y, Z, AREA))
        share = area * (AREA_SCALE / TURNS**2)
        rows = three(share * x) + three(share * y) + three(share * z) + three(share)
        rows += three(x * x + y * y + z * z + area)
        rows = jnp.concatenate([geo] + rows + [jnp.ones_like(x)], axis=0).astype(BF16)
        for k in range(3):
            sfeat[k, :, here] = jnp.dot(rights[k], rows, preferred_element_type=F32).astype(BF16)
        for k, v in enumerate((x, y, z, area, (area * (1.0 / TURNS**2)) * jnp.exp(scale * z))):
            sgeo[k, :, here] = jnp.broadcast_to(v, (8, LANES))
    rowacc[...] = jnp.zeros_like(rowacc)
    colacc[...] = jnp.zeros_like(colacc)
    blocks = targets // STEP
    steps = blocks * (sources // CHUNK)

    def corner(k):
        return pl.multiple_of(lax.rem(k, blocks) * STEP, STEP), pl.multiple_of(lax.div(k, blocks) * CHUNK, CHUNK)

    def products(k, into):
        t0, s0 = corner(k)
        features = tfeat[pl.ds(t0, STEP), :]
        for m in range(3):
            into[m] = jnp.dot(features, sfeat[m, :, pl.ds(s0, CHUNK)], preferred_element_type=F32)
        into[3] = jnp.dot(tcols[pl.ds(t0, STEP), :], scols[:, pl.ds(s0, CHUNK)], preferred_element_type=F32)

    halves = range(CHUNK // LANES)

    def elements(k, made):
        t0, s0 = corner(k)
        lanes = [pl.ds(pl.multiple_of(s0 + h * LANES, LANES), LANES) for h in halves]
        src = [[jnp.concatenate([sgeo[m, :, lanes[h]]] * (ROWS // 8), axis=0) for m in range(5)] for h in halves]
        acc = [None for _ in halves]
        for r in range(0, STEP, ROWS):
            rows = pl.ds(pl.multiple_of(t0 + r, ROWS), ROWS)
            xt, yt, zt, amp = (tgeo[m, rows, :] for m in range(4))
            along = rowacc[rows, :]
            for h in halves:
                top, topi, mirror, image = (made[m, r : r + ROWS, h * LANES : (h + 1) * LANES] for m in range(4))
                xs, ys, zs, area, ebb = src[h]
                dx, dy, dz = xt - xs, yt - ys, zt - zs
                flat = dx * dx + dy * dy + area
                near = flat + dz * dz
                i1, i2, i3 = lax.rsqrt(near), lax.rsqrt(mirror), lax.rsqrt(flat)
                pair = top * (i1 * i1 * i1) + topi * (i2 * i2 * i2)
                phase = flat * i3
                f = phase - ((phase + ROUNDER) - ROUNDER)
                turn = 0.25 - jnp.abs(f)
                g = turn * turn
                p = g + MONIC[-1]
                for c in MONIC[-2::-1]:
                    p = p * g + c
                kern = pair - (amp * ebb) * (turn * p)
                w = kern.astype(BF16).astype(F32) * image
                acc[h] = w if acc[h] is None else acc[h] + w
                along = along + w
            rowacc[rows, :] = along
        for h in halves:
            colacc[:, lanes[h]] += sum(acc[h][m : m + 8] for m in range(0, ROWS, 8))

    products(0, even)

    def two(k, _):
        elements(2 * k, even)
        products(2 * k + 1, odd)
        elements(2 * k + 1, odd)
        products(jnp.minimum(2 * k + 2, steps - 1), even)
        return 0

    lax.fori_loop(0, steps // 2, two, 0)
    for g in range(sources // LANES):
        here = slice(g * LANES, (g + 1) * LANES)
        colacc[0:1, here] = jnp.sum(colacc[:, here], axis=0, keepdims=True)
    panels = col_ref.shape[2]
    for k in range(col_ref.shape[0]):
        col_ref[k] = colacc[0:1, k * panels : (k + 1) * panels]
    for g in range(targets // LANES):
        line = jnp.sum(rowacc[g * LANES : (g + 1) * LANES, :].T, axis=0, keepdims=True)
        for k in range(2):
            low, high = (2 * g + k) % 8, (2 * g + k) // 8
            row_ref[low : low + 1, high * panels : (high + 1) * panels] = line[:, k * panels : (k + 1) * panels]


def tile(tgt, src, panels):
    targets, sources = tgt.shape[0] * panels, src.shape[0] * panels
    return pl.pallas_call(
        tile_kernel,
        out_shape=(
            jax.ShapeDtypeStruct((8, LANES), F32),
            jax.ShapeDtypeStruct((src.shape[0], 1, panels), F32),
            jax.ShapeDtypeStruct((8, LANES), F32),
        ),
        scratch_shapes=[
            pltpu.VMEM((targets, COLS), BF16),
            pltpu.VMEM((COLS, sources), BF16),
            pltpu.VMEM((targets, LANES), BF16),
            pltpu.VMEM((3, LANES, sources), BF16),
            pltpu.VMEM((4, targets, LANES), F32),
            pltpu.VMEM((5, 8, sources), F32),
            pltpu.VMEM((4, STEP, CHUNK), F32),
            pltpu.VMEM((4, STEP, CHUNK), F32),
            pltpu.VMEM((targets, LANES), F32),
            pltpu.VMEM((8, sources), F32),
        ],
        compiler_params=pltpu.CompilerParams(vmem_limit_bytes=24 << 20),
        name="tile",
    )(tgt, src)


def patch_kernel(mix_ref, dens_ref, spline_ref, out_ref, own_ref):
    quarters = PARTS["z_hi"]
    panels = own_ref.shape[1]
    dens = jnp.concatenate(
        [
            jnp.concatenate([dens_ref[k] for k in range(q, dens_ref.shape[0], quarters)], axis=0)
            for q in range(quarters)
        ],
        axis=1,
    )
    mix = mix_ref[...]
    both = sum(jnp.dot(mix, part, preferred_element_type=F32) for part in split3(dens)[::-1])
    got = jnp.concatenate(
        [
            both[:NPATCH, q * LANES : q * LANES + panels] + both[NPATCH:, q * LANES + panels : (q + 1) * LANES]
            for q in range(quarters)
        ],
        axis=1,
    )
    spline = spline_ref[...]
    rows = sum(jnp.dot(part, spline, preferred_element_type=F32) for part in split3(got)[::-1])
    depth = out_ref.shape[1]
    for piece in range(out_ref.shape[0]):
        out_ref[piece] = rows[piece * depth : (piece + 1) * depth]
    rho, gamma = device_place()
    line = dens_ref[gamma, pl.ds(rho % 8, 1), :]
    own_ref[...] = jnp.where(rho // 8 == 0, line[:, :panels], line[:, panels:])


def patch(mix, blocks, spline, panels):
    return pl.pallas_call(
        patch_kernel,
        out_shape=(
            jax.ShapeDtypeStruct((NTGT, NPATCH // NTGT, spline.shape[1]), F32),
            jax.ShapeDtypeStruct((1, panels), F32),
        ),
        compiler_params=pltpu.CompilerParams(vmem_limit_bytes=16 << 20),
        name="patch",
    )(mix, blocks, spline)


def exchange(pieces, axes):
    return lax.all_to_all(pieces, axes, 0, 0, tiled=True)


def copies(value, count):
    return jnp.broadcast_to(value[None], (count,) + value.shape)


def on_device(
    positions, normals, areas, direct, adjoint, spline, block_lists, patch_counts, patch_owner
):
    panels = positions.shape[1]
    tgt = pack(pack_targets_kernel, NTGT, positions, normals, adjoint)
    src = pack(pack_sources_kernel, NSRC, positions, areas.reshape(1, panels), direct)
    mix = mixing(patch_counts, patch_owner, block_lists)
    tgt_all = exchange(tgt, TGT_AXES)
    src_all = exchange(src, SRC_AXES)
    row_part, col_part, own_place = tile(tgt_all, src_all, panels)

    mine = jnp.sum(exchange(col_part, SRC_AXES), axis=0)
    row_part = row_part + own_place * jnp.tile(mine, (1, 2))
    dens = jnp.sum(exchange(copies(row_part, NTGT), TGT_AXES), axis=0)
    blocks = exchange(copies(dens, NSRC), SRC_AXES)

    contrib, own = patch(mix, blocks, spline[0], panels)
    rows = jnp.sum(exchange(contrib, TGT_AXES), axis=0)
    low = PARTS["z_lo"]
    rows = rows.reshape(low, 1, rows.shape[0] // low, rows.shape[1])
    rows = jnp.broadcast_to(rows, (low, NSRC // low) + rows.shape[2:]).reshape((NSRC,) + rows.shape[2:])
    patch_grad = jnp.sum(exchange(rows, SRC_AXES), axis=0)
    return own.reshape(panels), patch_grad


def solution(mesh):
    fine = Mesh(mesh.devices.reshape(tuple(PARTS.values())), NAMES)
    placed = (
        P(None, NAMES),
        P(None, NAMES),
        P(NAMES),
        P(NAMES, None),
        P(NAMES, None),
        P(NAMES, None, None),
        P(),
        P(),
        P(),
    )
    return jax.shard_map(
        on_device,
        mesh=fine,
        in_specs=placed,
        out_specs=(P(NAMES), P(("z_lo", "y", "core"), None)),
        check_vma=False,
    )
```

```python
import jax
import jax.numpy as jnp
import numpy as np
from jax import lax
from jax.experimental import pallas as pl
from jax.experimental.pallas import tpu as pltpu
from jax.sharding import Mesh
from jax.sharding import PartitionSpec as P

F32 = jnp.float32
BF16 = jnp.bfloat16
BPAN = 256
NPATCH = 64
NBLK = 128
LANES = 128
wave_number = 6.0
inv_four_pi = 0.07957747154594767

TURNS = wave_number / (2.0 * np.pi)
DEGREE = 3


def sine_coefficients():
    k = np.arange(64)
    nodes = 0.25 * np.cos(np.pi * (2 * k + 1) / 128)
    fit = np.polynomial.chebyshev.Chebyshev.fit(nodes, np.sin(2 * np.pi * nodes), 2 * DEGREE + 1, domain=[-0.25, 0.25])
    return fit.convert(kind=np.polynomial.Polynomial).coef[1::2]


COEF = sine_coefficients()
LEAD = float(COEF[-1])
MONIC = [float(c / COEF[-1]) for c in COEF[:-1]]
ROUNDER = float(3 << 22)
AREA_SCALE = float(TURNS**2 * inv_four_pi)
WAVE_SCALE = float(2.0 * wave_number * inv_four_pi * LEAD)

PARTS = {"z_lo": 2, "y": 8, "core": 2, "x": 4, "z_hi": 4}
NAMES = tuple(PARTS)
TGT_AXES = ("y", "core")
SRC_AXES = ("z_lo", "x", "z_hi")
NTGT = PARTS["y"] * PARTS["core"]
NSRC = PARTS["z_lo"] * PARTS["x"] * PARTS["z_hi"]

COLS = 64
HALF = 32
DEPTH = 40
X, Y, Z = (0, 2, 4), (1, 3, 5), (8, 9, 10)
NX, NY, NZ = (6, 7), (11, 12), (13, 14)
AREA = (11, 12, 13)

T_DOT, T_AMP, T_SQUARE, T_ONE, T_ROWS = 16, 19, 22, 25, 32
S_MOMENT, S_SHARE, S_SQUARE, S_ONE, S_ROWS = 16, 25, 28, 31, 32


def product_lanes():
    left, right = [], [{}, {}, {}]
    for d, n in enumerate((NX, NY, NZ)):
        for a in range(2):
            for b in range(3):
                lane = len(left)
                left.append(n[a])
                right[0][lane] = (S_MOMENT + 3 * d + b, -1.0)
                right[1][lane] = (S_MOMENT + 3 * d + b, 1.0 if d == 2 else -1.0)
    for a in range(3):
        for b in range(3):
            lane = len(left)
            left.append(T_DOT + a)
            right[0][lane] = right[1][lane] = (S_SHARE + b, 1.0)
    for d, p in enumerate((X, Y, Z)):
        for a in range(3):
            for b in range(3):
                right[2][len(left)] = (p[b], 2.0 if d == 2 else -2.0)
                left.append(p[a])
    for a in range(3):
        right[2][len(left)] = (S_ONE, 1.0)
        left.append(T_SQUARE + a)
    for b in range(3):
        right[2][len(left)] = (S_SQUARE + b, 1.0)
        left.append(T_ONE)
    return dict(enumerate(left)), right


LEFT, RIGHT = product_lanes()


def selector(rows, entries):
    lane = lax.broadcasted_iota(jnp.int32, (8, LANES), 1)
    where, value = jnp.full((8, LANES), -1, jnp.int32), jnp.zeros((8, LANES), F32)
    for key, (row, sign) in entries.items():
        where = jnp.where(lane == key, row, where)
        value = jnp.where(lane == key, sign, value)
    at = lax.broadcasted_iota(jnp.int32, (rows, LANES), 0)
    many = (rows // 8, 1)
    return jnp.where(at == jnp.tile(where, many), jnp.tile(value, many), 0.0)


def split3(v):
    hi = v.astype(BF16)
    rest = v - hi.astype(F32)
    mid = rest.astype(BF16)
    lo = (rest - mid.astype(F32)).astype(BF16)
    return hi, mid, lo


def three(v):
    return [part.astype(F32) for part in split3(v)]


def scaled(pos):
    row = lax.broadcasted_iota(jnp.int32, pos.shape, 0)
    parts = three(jnp.where(row == 2, 0.5 * (pos - 1.2), pos) * TURNS)
    return [v[0:2] for v in parts], [v[2:3] for v in parts]


def lay(top, left, right, ref):
    geo = jnp.concatenate([jnp.concatenate(left, axis=0), jnp.concatenate(right, axis=0)], axis=1)
    top = jnp.concatenate([top[:HALF], top[HALF:]], axis=1)
    piece = jnp.concatenate([top, geo], axis=0).astype(BF16)
    for k in range(ref.shape[0]):
        ref[k] = piece


def pack_targets_kernel(pos_ref, nrm_ref, adj_ref, ref):
    flat, deep = scaled(pos_ref[...])
    nx, ny, nz = ([v[k : k + 1] for v in three(nrm_ref[...])[:2]] for k in range(3))
    lay(adj_ref[...].astype(F32), flat + nx, deep + ny + nz + [jnp.zeros_like(deep[0])], ref)


def pack_sources_kernel(pos_ref, area_ref, dir_ref, ref):
    flat, deep = scaled(pos_ref[...])
    none = jnp.zeros((2, pos_ref.shape[1]), F32)
    lay(dir_ref[...].astype(F32).T, flat + [none], deep + three(area_ref[...] * TURNS**2) + [none], ref)


def pack(kernel, count, *arrays):
    out = jax.ShapeDtypeStruct((count, DEPTH, LANES), BF16)
    return pl.pallas_call(kernel, out_shape=out, name="pack")(*arrays)


def beside(a, b):
    return (
        jnp.concatenate([a[:, :COLS], b[:, :COLS]], axis=1),
        jnp.concatenate([a[:, COLS:], b[:, COLS:]], axis=1),
    )


def total(value, parts):
    return sum(value[m : m + 1, :] for m in parts)


ROWS = 16
CHUNK = 256
STEP = 512


def device_place():
    at = {name: lax.axis_index(name) for name in NAMES}
    rho = at["y"] * PARTS["core"] + at["core"]
    return rho, (at["z_lo"] * PARTS["x"] + at["x"]) * PARTS["z_hi"] + at["z_hi"]


def mixing_kernel(counts_ref, owner_ref, lists_ref, mix_ref):
    rho, gamma = device_place()
    nx, ncol = PARTS["x"], PARTS["x"] * PARTS["z_hi"]
    holder = ((gamma // ncol) * NTGT + rho) * ncol + gamma % ncol

    def iota(shape, dim):
        return lax.broadcasted_iota(jnp.int32, shape, dim)

    square = (NPATCH, NPATCH)
    counts = jnp.broadcast_to(counts_ref[...], square)
    eye = iota(square, 0) == iota(square, 1)
    starts = jnp.sum(jnp.where(iota(square, 1) < iota(square, 0), counts, 0).astype(F32), axis=1, keepdims=True)
    own_counts = jnp.sum(jnp.where(eye, counts, 0).astype(F32), axis=1, keepdims=True)
    lines = (NPATCH, NBLK)
    ids = iota(lines, 1).astype(F32)
    inside = (starts <= ids) & (ids < starts + own_counts)
    owner = jnp.broadcast_to(owner_ref[...], square)
    place = iota(square, 0)
    output = ((place % 4) // 2) * (2 * NTGT) + 2 * (place // 4) + place % 2
    owned = jnp.where(owner == output, 1.0, 0.0).astype(BF16)
    listed = jnp.max(jnp.where(lists_ref[...] == holder, 1.0, 0.0), axis=0, keepdims=True)
    member = jnp.where(inside, jnp.broadcast_to(listed, lines), 0.0).astype(BF16)
    by_block = jnp.dot(owned, member, preferred_element_type=F32).astype(BF16)
    cut = (NBLK, NBLK // 2)
    k = iota(cut, 1)
    for high in range(2):
        rho_k = high * 8 + k % 8
        block = (k // (8 * nx)) * (NTGT * nx) + rho_k * nx + (k // 8) % nx
        order = jnp.where(iota(cut, 0) == block, 1.0, 0.0).astype(BF16)
        part = jnp.dot(by_block, order, preferred_element_type=F32).astype(BF16)
        mix_ref[high * NPATCH : (high + 1) * NPATCH, :] = part


def mixing(patch_counts, patch_owner, block_lists):
    return pl.pallas_call(
        mixing_kernel,
        out_shape=jax.ShapeDtypeStruct((2 * NPATCH, NBLK // 2), BF16),
        name="mixing",
    )(patch_counts.reshape(1, NPATCH), patch_owner.reshape(1, NPATCH), block_lists.T)


def tile_kernel(
    tgt_ref, src_ref, row_ref, col_ref, own_ref, tcols, scols, tfeat, sfeat, tgeo, sgeo, even, odd, rowacc, colacc
):
    rho, _ = device_place()
    at_row = lax.broadcasted_iota(jnp.int32, own_ref.shape, 0) == rho % 8
    at_lane = lax.broadcasted_iota(jnp.int32, own_ref.shape, 1) // COLS == rho // 8
    own_ref[...] = jnp.where(at_row & at_lane, 1.0, 0.0)
    targets, sources = tcols.shape[0], scols.shape[1]
    scale = wave_number / TURNS

    part = lax.broadcasted_iota(jnp.int32, (T_ROWS, LANES), 0)
    chosen = [selector(T_ROWS, {lane: (row, 1.0) for lane, row in LEFT.items()})]
    for parts in (X, Y, Z, tuple(range(T_AMP, T_AMP + 3))):
        chosen.append(jnp.where((part == parts[0]) | (part == parts[1]) | (part == parts[2]), 1.0, 0.0))
    chosen = jnp.concatenate(chosen, axis=1).astype(BF16)
    for g in range(targets // LANES):
        here = slice(g * LANES, (g + 1) * LANES)
        pieces = [tgt_ref[m].astype(F32) for m in (2 * g, 2 * g + 1)]
        for m, piece in enumerate(pieces):
            row = g * LANES + m * COLS
            tcols[row : row + HALF, :] = piece[:HALF, :COLS].astype(BF16)
            tcols[row + HALF : row + COLS, :] = piece[:HALF, COLS:].astype(BF16)
        geo = jnp.concatenate(beside(*(p[HALF:] for p in pieces)), axis=0)
        x, y, z, nx, ny, nz = (total(geo, parts) for parts in (X, Y, Z, NX, NY, NZ))
        rows = three(nx * x + ny * y + nz * z) + three((WAVE_SCALE * nz) * jnp.exp(scale * z)) + three(x * x + y * y + z * z)
        rows = [geo] + rows + [jnp.ones_like(x), jnp.zeros((T_ROWS - T_ONE - 1, LANES), F32)]
        wide = lax.dot_general(
            jnp.concatenate(rows, axis=0).astype(BF16), chosen, (((0,), (0,)), ((), ())), preferred_element_type=F32
        )
        tfeat[here, :] = wide[:, :LANES].astype(BF16)
        for k in range(4):
            tgeo[k, here, :] = wide[:, (k + 1) * LANES : (k + 2) * LANES]
    rights = [selector(S_ROWS, entries).T.astype(BF16) for entries in RIGHT]
    for g in range(sources // LANES):
        here = slice(g * LANES, (g + 1) * LANES)
        left, right = beside(*(src_ref[m].astype(F32) for m in (2 * g, 2 * g + 1)))
        scols[:HALF, here] = left[:HALF].astype(BF16)
        scols[HALF:, here] = right[:HALF].astype(BF16)
        geo = jnp.concatenate([left[HALF:], right[HALF:]], axis=0)
        x, y, z, area = (total(geo, parts) for parts in (X, Y, Z, AREA))
        share = area * (AREA_SCALE / TURNS**2)
        rows = three(share * x) + three(share * y) + three(share * z) + three(share)
        rows += three(x * x + y * y + z * z + area)
        rows = jnp.concatenate([geo] + rows + [jnp.ones_like(x)], axis=0).astype(BF16)
        for k in range(3):
            sfeat[k, :, here] = jnp.dot(rights[k], rows, preferred_element_type=F32).astype(BF16)
        for k, v in enumerate((x, y, z, area, (area * (1.0 / TURNS**2)) * jnp.exp(scale * z))):
            sgeo[k, :, here] = jnp.broadcast_to(v, (8, LANES))
    rowacc[...] = jnp.zeros_like(rowacc)
    colacc[...] = jnp.zeros_like(colacc)
    blocks = targets // STEP
    steps = blocks * (sources // CHUNK)

    def corner(k):
        return pl.multiple_of(lax.rem(k, blocks) * STEP, STEP), pl.multiple_of(lax.div(k, blocks) * CHUNK, CHUNK)

    def products(k, into):
        t0, s0 = corner(k)
        features = tfeat[pl.ds(t0, STEP), :]
        for m in range(3):
            into[m] = jnp.dot(features, sfeat[m, :, pl.ds(s0, CHUNK)], preferred_element_type=F32)
        into[3] = jnp.dot(tcols[pl.ds(t0, STEP), :], scols[:, pl.ds(s0, CHUNK)], preferred_element_type=F32)

    halves = range(CHUNK // LANES)

    def elements(k, made):
        t0, s0 = corner(k)
        lanes = [pl.ds(pl.multiple_of(s0 + h * LANES, LANES), LANES) for h in halves]
        src = [[jnp.concatenate([sgeo[m, :, lanes[h]]] * (ROWS // 8), axis=0) for m in range(5)] for h in halves]
        acc = [None for _ in halves]
        for r in range(0, STEP, ROWS):
            rows = pl.ds(pl.multiple_of(t0 + r, ROWS), ROWS)
            xt, yt, zt, amp = (tgeo[m, rows, :] for m in range(4))
            along = rowacc[rows, :]
            for h in halves:
                top, topi, mirror, image = (made[m, r : r + ROWS, h * LANES : (h + 1) * LANES] for m in range(4))
                xs, ys, zs, area, ebb = src[h]
                dx, dy, dz = xt - xs, yt - ys, zt - zs
                flat = dx * dx + dy * dy + area
                near = flat + dz * dz
                i1, i2, i3 = lax.rsqrt(near), lax.rsqrt(mirror), lax.rsqrt(flat)
                pair = top * (i1 * i1 * i1) + topi * (i2 * i2 * i2)
                phase = flat * i3
                f = phase - ((phase + ROUNDER) - ROUNDER)
                turn = 0.25 - jnp.abs(f)
                g = turn * turn
                p = g + MONIC[-1]
                for c in MONIC[-2::-1]:
                    p = p * g + c
                kern = pair - (amp * ebb) * (turn * p)
                w = kern.astype(BF16).astype(F32) * image
                acc[h] = w if acc[h] is None else acc[h] + w
                along = along + w
            rowacc[rows, :] = along
        for h in halves:
            colacc[:, lanes[h]] += sum(acc[h][m : m + 8] for m in range(0, ROWS, 8))

    products(0, even)

    def two(k, _):
        elements(2 * k, even)
        products(2 * k + 1, odd)
        elements(2 * k + 1, odd)
        products(jnp.minimum(2 * k + 2, steps - 1), even)
        return 0

    lax.fori_loop(0, steps // 2, two, 0)
    for g in range(sources // LANES):
        here = slice(g * LANES, (g + 1) * LANES)
        colacc[0:1, here] = jnp.sum(colacc[:, here], axis=0, keepdims=True)
    panels = col_ref.shape[2]
    for k in range(col_ref.shape[0]):
        col_ref[k] = colacc[0:1, k * panels : (k + 1) * panels]
    for g in range(targets // LANES):
        line = jnp.sum(rowacc[g * LANES : (g + 1) * LANES, :].T, axis=0, keepdims=True)
        for k in range(2):
            low, high = (2 * g + k) % 8, (2 * g + k) // 8
            row_ref[low : low + 1, high * panels : (high + 1) * panels] = line[:, k * panels : (k + 1) * panels]


def tile(tgt, src, panels):
    targets, sources = tgt.shape[0] * panels, src.shape[0] * panels
    return pl.pallas_call(
        tile_kernel,
        out_shape=(
            jax.ShapeDtypeStruct((8, LANES), F32),
            jax.ShapeDtypeStruct((src.shape[0], 1, panels), F32),
            jax.ShapeDtypeStruct((8, LANES), F32),
        ),
        scratch_shapes=[
            pltpu.VMEM((targets, COLS), BF16),
            pltpu.VMEM((COLS, sources), BF16),
            pltpu.VMEM((targets, LANES), BF16),
            pltpu.VMEM((3, LANES, sources), BF16),
            pltpu.VMEM((4, targets, LANES), F32),
            pltpu.VMEM((5, 8, sources), F32),
            pltpu.VMEM((4, STEP, CHUNK), F32),
            pltpu.VMEM((4, STEP, CHUNK), F32),
            pltpu.VMEM((targets, LANES), F32),
            pltpu.VMEM((8, sources), F32),
        ],
        compiler_params=pltpu.CompilerParams(vmem_limit_bytes=24 << 20),
        name="tile",
    )(tgt, src)


def patch_kernel(mix_ref, dens_ref, spline_ref, out_ref, own_ref):
    quarters = PARTS["z_hi"]
    panels = own_ref.shape[1]
    dens = jnp.concatenate(
        [
            jnp.concatenate([dens_ref[k] for k in range(q, dens_ref.shape[0], quarters)], axis=0)
            for q in range(quarters)
        ],
        axis=1,
    )
    mix = mix_ref[...]
    both = sum(jnp.dot(mix, part, preferred_element_type=F32) for part in split3(dens)[::-1])
    got = jnp.concatenate(
        [
            both[:NPATCH, q * LANES : q * LANES + panels] + both[NPATCH:, q * LANES + panels : (q + 1) * LANES]
            for q in range(quarters)
        ],
        axis=1,
    )
    spline = spline_ref[...]
    rows = sum(jnp.dot(part, spline, preferred_element_type=F32) for part in split3(got)[::-1])
    for piece in range(out_ref.shape[0]):
        for k in range(out_ref.shape[1] // 2):
            low, lanes = divmod(k, spline.shape[1] // LANES)
            row = 4 * piece + 2 * low
            out_ref[piece, 2 * k : 2 * k + 2, :] = rows[row : row + 2, lanes * LANES : (lanes + 1) * LANES]
    rho, gamma = device_place()
    line = dens_ref[gamma, pl.ds(rho % 8, 1), :]
    own_ref[...] = jnp.where(rho // 8 == 0, line[:, :panels], line[:, panels:])


def patch(mix, blocks, spline, panels):
    return pl.pallas_call(
        patch_kernel,
        out_shape=(
            jax.ShapeDtypeStruct((NTGT, NPATCH // NTGT * spline.shape[1] // LANES, LANES), F32),
            jax.ShapeDtypeStruct((1, panels), F32),
        ),
        compiler_params=pltpu.CompilerParams(vmem_limit_bytes=16 << 20),
        name="patch",
    )(mix, blocks, spline)


def exchange(pieces, axes):
    return lax.all_to_all(pieces, axes, 0, 0, tiled=True)


def copies(value, count):
    return jnp.broadcast_to(value[None], (count,) + value.shape)


def on_device(
    positions, normals, areas, direct, adjoint, spline, block_lists, patch_counts, patch_owner
):
    panels = positions.shape[1]
    tgt = pack(pack_targets_kernel, NTGT, positions, normals, adjoint)
    src = pack(pack_sources_kernel, NSRC, positions, areas.reshape(1, panels), direct)
    mix = mixing(patch_counts, patch_owner, block_lists)
    tgt_all = exchange(tgt, TGT_AXES)
    src, mix = lax.optimization_barrier((src, mix))
    src_all = exchange(src, SRC_AXES)
    row_part, col_part, own_place = tile(tgt_all, src_all, panels)

    mine = jnp.sum(exchange(col_part, SRC_AXES), axis=0)
    row_part = row_part + own_place * jnp.tile(mine, (1, 2))
    dens = jnp.sum(exchange(copies(row_part, NTGT), TGT_AXES), axis=0)
    blocks = exchange(copies(dens, NSRC), SRC_AXES)

    contrib, own = patch(mix, blocks, spline[0], panels)
    rows = jnp.sum(exchange(contrib, TGT_AXES), axis=0)
    low = PARTS["z_lo"]
    rows = rows.reshape(low, 1, 8, LANES)
    rows = jnp.broadcast_to(rows, (low, NSRC // low, 8, LANES)).reshape(NSRC, 8, LANES)
    rows = jnp.sum(exchange(rows, SRC_AXES), axis=0)
    patch_grad = rows.reshape(4, 2, LANES).transpose(1, 0, 2).reshape(2, 4 * LANES)
    return own.reshape(panels), patch_grad


def solution(mesh):
    fine = Mesh(mesh.devices.reshape(tuple(PARTS.values())), NAMES)
    placed = (
        P(None, NAMES),
        P(None, NAMES),
        P(NAMES),
        P(NAMES, None),
        P(NAMES, None),
        P(NAMES, None, None),
        P(),
        P(),
        P(),
    )
    return jax.shard_map(
        on_device,
        mesh=fine,
        in_specs=placed,
        out_specs=(P(NAMES), P(("z_lo", "y", "core"), None)),
        check_vma=False,
    )
```

```python
import jax
import jax.numpy as jnp
import numpy as np
from jax import lax
from jax.experimental import pallas as pl
from jax.experimental.pallas import tpu as pltpu
from jax.sharding import Mesh
from jax.sharding import PartitionSpec as P

F32 = jnp.float32
BF16 = jnp.bfloat16
BPAN = 256
NPATCH = 64
NBLK = 128
LANES = 128
wave_number = 6.0
inv_four_pi = 0.07957747154594767

TURNS = wave_number / (2.0 * np.pi)
DEGREE = 3


def sine_coefficients():
    k = np.arange(64)
    nodes = 0.25 * np.cos(np.pi * (2 * k + 1) / 128)
    fit = np.polynomial.chebyshev.Chebyshev.fit(nodes, np.sin(2 * np.pi * nodes), 2 * DEGREE + 1, domain=[-0.25, 0.25])
    return fit.convert(kind=np.polynomial.Polynomial).coef[1::2]


COEF = sine_coefficients()
LEAD = float(COEF[-1])
MONIC = [float(c / COEF[-1]) for c in COEF[:-1]]
ROUNDER = float(3 << 22)
AREA_SCALE = float(TURNS**2 * inv_four_pi)
WAVE_SCALE = float(2.0 * wave_number * inv_four_pi * LEAD)

PARTS = {"z_lo": 2, "y": 8, "core": 2, "x": 4, "z_hi": 4}
NAMES = tuple(PARTS)
TGT_AXES = ("core", "y")
SRC_AXES = ("x", "z_lo", "z_hi")
NTGT = PARTS["y"] * PARTS["core"]
NSRC = PARTS["z_lo"] * PARTS["x"] * PARTS["z_hi"]

COLS = 64
HALF = 32
DEPTH = 40
X, Y, Z = (0, 2, 4), (1, 3, 5), (8, 9, 10)
NX, NY, NZ = (6, 7), (11, 12), (13, 14)
AREA = (11, 12, 13)

T_DOT, T_AMP, T_SQUARE, T_ONE, T_ROWS = 16, 19, 22, 25, 32
S_MOMENT, S_SHARE, S_SQUARE, S_ONE, S_ROWS = 16, 25, 28, 31, 32


def product_lanes():
    left, right = [], [{}, {}, {}]
    for d, n in enumerate((NX, NY, NZ)):
        for a in range(2):
            for b in range(3):
                lane = len(left)
                left.append(n[a])
                right[0][lane] = (S_MOMENT + 3 * d + b, -1.0)
                right[1][lane] = (S_MOMENT + 3 * d + b, 1.0 if d == 2 else -1.0)
    for a in range(3):
        for b in range(3):
            lane = len(left)
            left.append(T_DOT + a)
            right[0][lane] = right[1][lane] = (S_SHARE + b, 1.0)
    for d, p in enumerate((X, Y, Z)):
        for a in range(3):
            for b in range(3):
                right[2][len(left)] = (p[b], 2.0 if d == 2 else -2.0)
                left.append(p[a])
    for a in range(3):
        right[2][len(left)] = (S_ONE, 1.0)
        left.append(T_SQUARE + a)
    for b in range(3):
        right[2][len(left)] = (S_SQUARE + b, 1.0)
        left.append(T_ONE)
    return dict(enumerate(left)), right


LEFT, RIGHT = product_lanes()


def selector(rows, entries):
    lane = lax.broadcasted_iota(jnp.int32, (8, LANES), 1)
    where, value = jnp.full((8, LANES), -1, jnp.int32), jnp.zeros((8, LANES), F32)
    for key, (row, sign) in entries.items():
        where = jnp.where(lane == key, row, where)
        value = jnp.where(lane == key, sign, value)
    at = lax.broadcasted_iota(jnp.int32, (rows, LANES), 0)
    many = (rows // 8, 1)
    return jnp.where(at == jnp.tile(where, many), jnp.tile(value, many), 0.0)


def split3(v):
    hi = v.astype(BF16)
    rest = v - hi.astype(F32)
    mid = rest.astype(BF16)
    lo = (rest - mid.astype(F32)).astype(BF16)
    return hi, mid, lo


def three(v):
    return [part.astype(F32) for part in split3(v)]


def scaled(pos):
    row = lax.broadcasted_iota(jnp.int32, pos.shape, 0)
    parts = three(jnp.where(row == 2, 0.5 * (pos - 1.2), pos) * TURNS)
    return [v[0:2] for v in parts], [v[2:3] for v in parts]


def lay(top, left, right, ref):
    geo = jnp.concatenate([jnp.concatenate(left, axis=0), jnp.concatenate(right, axis=0)], axis=1)
    top = jnp.concatenate([top[:HALF], top[HALF:]], axis=1)
    piece = jnp.concatenate([top, geo], axis=0).astype(BF16)
    for k in range(ref.shape[0]):
        ref[k] = piece


def pack_targets_kernel(pos_ref, nrm_ref, adj_ref, ref):
    flat, deep = scaled(pos_ref[...])
    nx, ny, nz = ([v[k : k + 1] for v in three(nrm_ref[...])[:2]] for k in range(3))
    lay(adj_ref[...].astype(F32), flat + nx, deep + ny + nz + [jnp.zeros_like(deep[0])], ref)


def pack_sources_kernel(pos_ref, area_ref, dir_ref, ref):
    flat, deep = scaled(pos_ref[...])
    none = jnp.zeros((2, pos_ref.shape[1]), F32)
    lay(dir_ref[...].astype(F32).T, flat + [none], deep + three(area_ref[...] * TURNS**2) + [none], ref)


def pack(kernel, count, *arrays):
    out = jax.ShapeDtypeStruct((count, DEPTH, LANES), BF16)
    return pl.pallas_call(kernel, out_shape=out, name="pack")(*arrays)


def beside(a, b):
    return (
        jnp.concatenate([a[:, :COLS], b[:, :COLS]], axis=1),
        jnp.concatenate([a[:, COLS:], b[:, COLS:]], axis=1),
    )


def total(value, parts):
    return sum(value[m : m + 1, :] for m in parts)


ROWS = 16
CHUNK = 256
STEP = 512


def device_place():
    at = {name: lax.axis_index(name) for name in NAMES}
    rho = at["core"] * PARTS["y"] + at["y"]
    return rho, (at["x"] * PARTS["z_lo"] + at["z_lo"]) * PARTS["z_hi"] + at["z_hi"]


def mixing_kernel(counts_ref, owner_ref, lists_ref, mix_ref):
    holder = lax.axis_index(NAMES)
    nx, ncore, ny, nlow = (PARTS[name] for name in ("x", "core", "y", "z_lo"))

    def iota(shape, dim):
        return lax.broadcasted_iota(jnp.int32, shape, dim)

    square = (NPATCH, NPATCH)
    counts = jnp.broadcast_to(counts_ref[...], square)
    eye = iota(square, 0) == iota(square, 1)
    starts = jnp.sum(jnp.where(iota(square, 1) < iota(square, 0), counts, 0).astype(F32), axis=1, keepdims=True)
    own_counts = jnp.sum(jnp.where(eye, counts, 0).astype(F32), axis=1, keepdims=True)
    lines = (NPATCH, NBLK)
    ids = iota(lines, 1).astype(F32)
    inside = (starts <= ids) & (ids < starts + own_counts)
    owner = jnp.broadcast_to(owner_ref[...], square)
    place = iota(square, 0)
    rho = place // 4
    output = ((place % 4) // 2) * (2 * NTGT) + 2 * ((rho % ny) * ncore + rho // ny) + place % 2
    owned = jnp.where(owner == output, 1.0, 0.0).astype(BF16)
    listed = jnp.max(jnp.where(lists_ref[...] == holder, 1.0, 0.0), axis=0, keepdims=True)
    member = jnp.where(inside, jnp.broadcast_to(listed, lines), 0.0).astype(BF16)
    by_block = jnp.dot(owned, member, preferred_element_type=F32).astype(BF16)
    cut = (NBLK, NBLK // 2)
    k = iota(cut, 1)
    for high in range(ncore):
        block = ((k // ny) % nlow) * (NTGT * nx) + ((k % ny) * ncore + high) * nx + k // (ny * nlow)
        order = jnp.where(iota(cut, 0) == block, 1.0, 0.0).astype(BF16)
        part = jnp.dot(by_block, order, preferred_element_type=F32).astype(BF16)
        mix_ref[high * NPATCH : (high + 1) * NPATCH, :] = part


def mixing(patch_counts, patch_owner, block_lists):
    return pl.pallas_call(
        mixing_kernel,
        out_shape=jax.ShapeDtypeStruct((2 * NPATCH, NBLK // 2), BF16),
        name="mixing",
    )(patch_counts.reshape(1, NPATCH), patch_owner.reshape(1, NPATCH), block_lists.T)


def tile_kernel(
    tgt_ref, src_ref, row_ref, col_ref, own_ref, tcols, scols, tfeat, sfeat, tgeo, sgeo, even, odd, rowacc, colacc
):
    rho, _ = device_place()
    at_row = lax.broadcasted_iota(jnp.int32, own_ref.shape, 0) == rho % 8
    at_lane = lax.broadcasted_iota(jnp.int32, own_ref.shape, 1) // COLS == rho // 8
    own_ref[...] = jnp.where(at_row & at_lane, 1.0, 0.0)
    targets, sources = tcols.shape[0], scols.shape[1]
    scale = wave_number / TURNS

    part = lax.broadcasted_iota(jnp.int32, (T_ROWS, LANES), 0)
    chosen = [selector(T_ROWS, {lane: (row, 1.0) for lane, row in LEFT.items()})]
    for parts in (X, Y, Z, tuple(range(T_AMP, T_AMP + 3))):
        chosen.append(jnp.where((part == parts[0]) | (part == parts[1]) | (part == parts[2]), 1.0, 0.0))
    chosen = jnp.concatenate(chosen, axis=1).astype(BF16)
    for g in range(targets // LANES):
        here = slice(g * LANES, (g + 1) * LANES)
        pieces = [tgt_ref[m].astype(F32) for m in (2 * g, 2 * g + 1)]
        for m, piece in enumerate(pieces):
            row = g * LANES + m * COLS
            tcols[row : row + HALF, :] = piece[:HALF, :COLS].astype(BF16)
            tcols[row + HALF : row + COLS, :] = piece[:HALF, COLS:].astype(BF16)
        geo = jnp.concatenate(beside(*(p[HALF:] for p in pieces)), axis=0)
        x, y, z, nx, ny, nz = (total(geo, parts) for parts in (X, Y, Z, NX, NY, NZ))
        rows = three(nx * x + ny * y + nz * z) + three((WAVE_SCALE * nz) * jnp.exp(scale * z)) + three(x * x + y * y + z * z)
        rows = [geo] + rows + [jnp.ones_like(x), jnp.zeros((T_ROWS - T_ONE - 1, LANES), F32)]
        wide = lax.dot_general(
            jnp.concatenate(rows, axis=0).astype(BF16), chosen, (((0,), (0,)), ((), ())), preferred_element_type=F32
        )
        tfeat[here, :] = wide[:, :LANES].astype(BF16)
        for k in range(4):
            tgeo[k, here, :] = wide[:, (k + 1) * LANES : (k + 2) * LANES]
    rights = [selector(S_ROWS, entries).T.astype(BF16) for entries in RIGHT]
    for g in range(sources // LANES):
        here = slice(g * LANES, (g + 1) * LANES)
        left, right = beside(*(src_ref[m].astype(F32) for m in (2 * g, 2 * g + 1)))
        scols[:HALF, here] = left[:HALF].astype(BF16)
        scols[HALF:, here] = right[:HALF].astype(BF16)
        geo = jnp.concatenate([left[HALF:], right[HALF:]], axis=0)
        x, y, z, area = (total(geo, parts) for parts in (X, Y, Z, AREA))
        share = area * (AREA_SCALE / TURNS**2)
        rows = three(share * x) + three(share * y) + three(share * z) + three(share)
        rows += three(x * x + y * y + z * z + area)
        rows = jnp.concatenate([geo] + rows + [jnp.ones_like(x)], axis=0).astype(BF16)
        for k in range(3):
            sfeat[k, :, here] = jnp.dot(rights[k], rows, preferred_element_type=F32).astype(BF16)
        for k, v in enumerate((x, y, z, area, (area * (1.0 / TURNS**2)) * jnp.exp(scale * z))):
            sgeo[k, :, here] = jnp.broadcast_to(v, (8, LANES))
    rowacc[...] = jnp.zeros_like(rowacc)
    colacc[...] = jnp.zeros_like(colacc)
    blocks = targets // STEP
    steps = blocks * (sources // CHUNK)

    def corner(k):
        return pl.multiple_of(lax.rem(k, blocks) * STEP, STEP), pl.multiple_of(lax.div(k, blocks) * CHUNK, CHUNK)

    def products(k, into):
        t0, s0 = corner(k)
        features = tfeat[pl.ds(t0, STEP), :]
        for m in range(3):
            into[m] = jnp.dot(features, sfeat[m, :, pl.ds(s0, CHUNK)], preferred_element_type=F32)
        into[3] = jnp.dot(tcols[pl.ds(t0, STEP), :], scols[:, pl.ds(s0, CHUNK)], preferred_element_type=F32)

    halves = range(CHUNK // LANES)

    def elements(k, made):
        t0, s0 = corner(k)
        lanes = [pl.ds(pl.multiple_of(s0 + h * LANES, LANES), LANES) for h in halves]
        src = [[jnp.concatenate([sgeo[m, :, lanes[h]]] * (ROWS // 8), axis=0) for m in range(5)] for h in halves]
        acc = [None for _ in halves]
        for r in range(0, STEP, ROWS):
            rows = pl.ds(pl.multiple_of(t0 + r, ROWS), ROWS)
            xt, yt, zt, amp = (tgeo[m, rows, :] for m in range(4))
            along = rowacc[rows, :]
            for h in halves:
                top, topi, mirror, image = (made[m, r : r + ROWS, h * LANES : (h + 1) * LANES] for m in range(4))
                xs, ys, zs, area, ebb = src[h]
                dx, dy, dz = xt - xs, yt - ys, zt - zs
                flat = dx * dx + dy * dy + area
                near = flat + dz * dz
                i1, i2, i3 = lax.rsqrt(near), lax.rsqrt(mirror), lax.rsqrt(flat)
                pair = top * (i1 * i1 * i1) + topi * (i2 * i2 * i2)
                phase = flat * i3
                f = phase - ((phase + ROUNDER) - ROUNDER)
                turn = 0.25 - jnp.abs(f)
                g = turn * turn
                p = g + MONIC[-1]
                for c in MONIC[-2::-1]:
                    p = p * g + c
                kern = pair - (amp * ebb) * (turn * p)
                w = kern.astype(BF16).astype(F32) * image
                acc[h] = w if acc[h] is None else acc[h] + w
                along = along + w
            rowacc[rows, :] = along
        for h in halves:
            colacc[:, lanes[h]] += sum(acc[h][m : m + 8] for m in range(0, ROWS, 8))

    products(0, even)

    def two(k, _):
        elements(2 * k, even)
        products(2 * k + 1, odd)
        elements(2 * k + 1, odd)
        products(jnp.minimum(2 * k + 2, steps - 1), even)
        return 0

    lax.fori_loop(0, steps // 2, two, 0)
    for g in range(sources // LANES):
        here = slice(g * LANES, (g + 1) * LANES)
        colacc[0:1, here] = jnp.sum(colacc[:, here], axis=0, keepdims=True)
    panels = col_ref.shape[2]
    for k in range(col_ref.shape[0]):
        col_ref[k] = colacc[0:1, k * panels : (k + 1) * panels]
    for g in range(targets // LANES):
        line = jnp.sum(rowacc[g * LANES : (g + 1) * LANES, :].T, axis=0, keepdims=True)
        for k in range(2):
            low, high = (2 * g + k) % 8, (2 * g + k) // 8
            row_ref[low : low + 1, high * panels : (high + 1) * panels] = line[:, k * panels : (k + 1) * panels]


def tile(tgt, src, panels):
    targets, sources = tgt.shape[0] * panels, src.shape[0] * panels
    return pl.pallas_call(
        tile_kernel,
        out_shape=(
            jax.ShapeDtypeStruct((8, LANES), F32),
            jax.ShapeDtypeStruct((src.shape[0], 1, panels), F32),
            jax.ShapeDtypeStruct((8, LANES), F32),
        ),
        scratch_shapes=[
            pltpu.VMEM((targets, COLS), BF16),
            pltpu.VMEM((COLS, sources), BF16),
            pltpu.VMEM((targets, LANES), BF16),
            pltpu.VMEM((3, LANES, sources), BF16),
            pltpu.VMEM((4, targets, LANES), F32),
            pltpu.VMEM((5, 8, sources), F32),
            pltpu.VMEM((4, STEP, CHUNK), F32),
            pltpu.VMEM((4, STEP, CHUNK), F32),
            pltpu.VMEM((targets, LANES), F32),
            pltpu.VMEM((8, sources), F32),
        ],
        compiler_params=pltpu.CompilerParams(vmem_limit_bytes=24 << 20),
        name="tile",
    )(tgt, src)


def patch_kernel(mix_ref, dens_ref, spline_ref, out_ref, own_ref):
    quarters = PARTS["z_hi"]
    panels = own_ref.shape[1]
    dens = jnp.concatenate(
        [
            jnp.concatenate([dens_ref[k] for k in range(q, dens_ref.shape[0], quarters)], axis=0)
            for q in range(quarters)
        ],
        axis=1,
    )
    mix = mix_ref[...]
    both = sum(jnp.dot(mix, part, preferred_element_type=F32) for part in split3(dens)[::-1])
    got = jnp.concatenate(
        [
            both[:NPATCH, q * LANES : q * LANES + panels] + both[NPATCH:, q * LANES + panels : (q + 1) * LANES]
            for q in range(quarters)
        ],
        axis=1,
    )
    spline = spline_ref[...]
    rows = sum(jnp.dot(part, spline, preferred_element_type=F32) for part in split3(got)[::-1])
    for piece in range(out_ref.shape[0]):
        for k in range(out_ref.shape[1] // 2):
            low, lanes = divmod(k, spline.shape[1] // LANES)
            row = 4 * piece + 2 * low
            out_ref[piece, 2 * k : 2 * k + 2, :] = rows[row : row + 2, lanes * LANES : (lanes + 1) * LANES]
    rho, gamma = device_place()
    line = dens_ref[gamma, pl.ds(rho % 8, 1), :]
    own_ref[...] = jnp.where(rho // 8 == 0, line[:, :panels], line[:, panels:])


def patch(mix, blocks, spline, panels):
    return pl.pallas_call(
        patch_kernel,
        out_shape=(
            jax.ShapeDtypeStruct((NTGT, NPATCH // NTGT * spline.shape[1] // LANES, LANES), F32),
            jax.ShapeDtypeStruct((1, panels), F32),
        ),
        compiler_params=pltpu.CompilerParams(vmem_limit_bytes=16 << 20),
        name="patch",
    )(mix, blocks, spline)


def exchange(pieces, axes):
    return lax.all_to_all(pieces, axes, 0, 0, tiled=True)


def copies(value, count):
    return jnp.broadcast_to(value[None], (count,) + value.shape)


def on_device(
    positions, normals, areas, direct, adjoint, spline, block_lists, patch_counts, patch_owner
):
    panels = positions.shape[1]
    tgt = pack(pack_targets_kernel, NTGT, positions, normals, adjoint)
    src = pack(pack_sources_kernel, NSRC, positions, areas.reshape(1, panels), direct)
    mix = mixing(patch_counts, patch_owner, block_lists)
    tgt_all = exchange(tgt, TGT_AXES)
    src, mix = lax.optimization_barrier((src, mix))
    src_all = exchange(src, SRC_AXES)
    row_part, col_part, own_place = tile(tgt_all, src_all, panels)

    mine = jnp.sum(exchange(col_part, SRC_AXES), axis=0)
    row_part = row_part + own_place * jnp.tile(mine, (1, 2))
    dens = jnp.sum(exchange(copies(row_part, NTGT), TGT_AXES), axis=0)
    blocks = exchange(copies(dens, NSRC), SRC_AXES)

    contrib, own = patch(mix, blocks, spline[0], panels)
    rows = jnp.sum(exchange(contrib, TGT_AXES), axis=0)
    low = PARTS["z_lo"]
    rows = rows.reshape(1, low, 1, 8, LANES)
    rows = jnp.broadcast_to(rows, (PARTS["x"], low, PARTS["z_hi"], 8, LANES)).reshape(NSRC, 8, LANES)
    rows = jnp.sum(exchange(rows, SRC_AXES), axis=0)
    patch_grad = rows.reshape(4, 2, LANES).transpose(1, 0, 2).reshape(2, 4 * LANES)
    return own.reshape(panels), patch_grad


def solution(mesh):
    fine = Mesh(mesh.devices.reshape(tuple(PARTS.values())), NAMES)
    placed = (
        P(None, NAMES),
        P(None, NAMES),
        P(NAMES),
        P(NAMES, None),
        P(NAMES, None),
        P(NAMES, None, None),
        P(),
        P(),
        P(),
    )
    return jax.shard_map(
        on_device,
        mesh=fine,
        in_specs=placed,
        out_specs=(P(NAMES), P(("z_lo", "y", "core"), None)),
        check_vma=False,
    )
```

```python
import jax
import jax.numpy as jnp
import numpy as np
from jax import lax
from jax.experimental import pallas as pl
from jax.experimental.pallas import tpu as pltpu
from jax.sharding import Mesh
from jax.sharding import PartitionSpec as P

F32 = jnp.float32
BF16 = jnp.bfloat16
BPAN = 256
NPATCH = 64
NBLK = 128
LANES = 128
wave_number = 6.0
inv_four_pi = 0.07957747154594767

TURNS = wave_number / (2.0 * np.pi)
DEGREE = 3


def sine_coefficients():
    k = np.arange(64)
    nodes = 0.25 * np.cos(np.pi * (2 * k + 1) / 128)
    fit = np.polynomial.chebyshev.Chebyshev.fit(nodes, np.sin(2 * np.pi * nodes), 2 * DEGREE + 1, domain=[-0.25, 0.25])
    return fit.convert(kind=np.polynomial.Polynomial).coef[1::2]


COEF = sine_coefficients()
LEAD = float(COEF[-1])
MONIC = [float(c / COEF[-1]) for c in COEF[:-1]]
ROUNDER = float(3 << 22)
AREA_SCALE = float(TURNS**2 * inv_four_pi)
WAVE_SCALE = float(2.0 * wave_number * inv_four_pi * LEAD)

PARTS = {"z_lo": 2, "y": 8, "core": 2, "x": 4, "z_hi": 4}
NAMES = tuple(PARTS)
TGT_AXES = ("core", "y")
SRC_AXES = ("x", "z_lo", "z_hi")
NTGT = PARTS["y"] * PARTS["core"]
NSRC = PARTS["z_lo"] * PARTS["x"] * PARTS["z_hi"]

COLS = 64
HALF = 32
DEPTH = 40
X, Y, Z = (0, 2, 4), (1, 3, 5), (8, 9, 10)
NX, NY, NZ = (6, 7), (11, 12), (13, 14)
AREA = (11, 12, 13)

T_DOT, T_AMP, T_SQUARE, T_ONE, T_ROWS = 16, 19, 22, 25, 32
S_MOMENT, S_SHARE, S_SQUARE, S_ONE, S_ROWS = 16, 25, 28, 31, 32


def product_lanes():
    left, right = [], [{}, {}, {}]
    for d, n in enumerate((NX, NY, NZ)):
        for a in range(2):
            for b in range(3):
                lane = len(left)
                left.append(n[a])
                right[0][lane] = (S_MOMENT + 3 * d + b, -1.0)
                right[1][lane] = (S_MOMENT + 3 * d + b, 1.0 if d == 2 else -1.0)
    for a in range(3):
        for b in range(3):
            lane = len(left)
            left.append(T_DOT + a)
            right[0][lane] = right[1][lane] = (S_SHARE + b, 1.0)
    for d, p in enumerate((X, Y, Z)):
        for a in range(3):
            for b in range(3):
                right[2][len(left)] = (p[b], 2.0 if d == 2 else -2.0)
                left.append(p[a])
    for a in range(3):
        right[2][len(left)] = (S_ONE, 1.0)
        left.append(T_SQUARE + a)
    for b in range(3):
        right[2][len(left)] = (S_SQUARE + b, 1.0)
        left.append(T_ONE)
    return dict(enumerate(left)), right


LEFT, RIGHT = product_lanes()


def selector(rows, entries):
    lane = lax.broadcasted_iota(jnp.int32, (8, LANES), 1)
    where, value = jnp.full((8, LANES), -1, jnp.int32), jnp.zeros((8, LANES), F32)
    for key, (row, sign) in entries.items():
        where = jnp.where(lane == key, row, where)
        value = jnp.where(lane == key, sign, value)
    at = lax.broadcasted_iota(jnp.int32, (rows, LANES), 0)
    many = (rows // 8, 1)
    return jnp.where(at == jnp.tile(where, many), jnp.tile(value, many), 0.0)


def split3(v):
    hi = v.astype(BF16)
    rest = v - hi.astype(F32)
    mid = rest.astype(BF16)
    lo = (rest - mid.astype(F32)).astype(BF16)
    return hi, mid, lo


def three(v):
    return [part.astype(F32) for part in split3(v)]


def scaled(pos):
    row = lax.broadcasted_iota(jnp.int32, pos.shape, 0)
    parts = three(jnp.where(row == 2, 0.5 * (pos - 1.2), pos) * TURNS)
    return [v[0:2] for v in parts], [v[2:3] for v in parts]


def lay(top, left, right, ref):
    geo = jnp.concatenate([jnp.concatenate(left, axis=0), jnp.concatenate(right, axis=0)], axis=1)
    top = jnp.concatenate([top[:HALF], top[HALF:]], axis=1)
    piece = jnp.concatenate([top, geo], axis=0).astype(BF16)
    for k in range(ref.shape[0]):
        ref[k] = piece


def pack_targets_kernel(pos_ref, nrm_ref, adj_ref, ref):
    flat, deep = scaled(pos_ref[...])
    nx, ny, nz = ([v[k : k + 1] for v in three(nrm_ref[...])[:2]] for k in range(3))
    lay(adj_ref[...].astype(F32), flat + nx, deep + ny + nz + [jnp.zeros_like(deep[0])], ref)


def pack_sources_kernel(pos_ref, area_ref, dir_ref, ref):
    flat, deep = scaled(pos_ref[...])
    none = jnp.zeros((2, pos_ref.shape[1]), F32)
    lay(dir_ref[...].astype(F32).T, flat + [none], deep + three(area_ref[...] * TURNS**2) + [none], ref)


def pack(kernel, count, *arrays):
    out = jax.ShapeDtypeStruct((count, DEPTH, LANES), BF16)
    return pl.pallas_call(kernel, out_shape=out, name="pack")(*arrays)


def beside(a, b):
    return (
        jnp.concatenate([a[:, :COLS], b[:, :COLS]], axis=1),
        jnp.concatenate([a[:, COLS:], b[:, COLS:]], axis=1),
    )


def total(value, parts):
    return sum(value[m : m + 1, :] for m in parts)


ROWS = 16
CHUNK = 256
STEP = 512


def device_place():
    at = {name: lax.axis_index(name) for name in NAMES}
    rho = at["core"] * PARTS["y"] + at["y"]
    return rho, (at["x"] * PARTS["z_lo"] + at["z_lo"]) * PARTS["z_hi"] + at["z_hi"]


def mixing_kernel(counts_ref, owner_ref, lists_ref, mix_ref):
    holder = lax.axis_index(NAMES)
    nx, ncore, ny, nlow = (PARTS[name] for name in ("x", "core", "y", "z_lo"))

    def iota(shape, dim):
        return lax.broadcasted_iota(jnp.int32, shape, dim)

    square = (NPATCH, NPATCH)
    counts = jnp.broadcast_to(counts_ref[...], square)
    eye = iota(square, 0) == iota(square, 1)
    starts = jnp.sum(jnp.where(iota(square, 1) < iota(square, 0), counts, 0).astype(F32), axis=1, keepdims=True)
    own_counts = jnp.sum(jnp.where(eye, counts, 0).astype(F32), axis=1, keepdims=True)
    lines = (NPATCH, NBLK)
    ids = iota(lines, 1).astype(F32)
    inside = (starts <= ids) & (ids < starts + own_counts)
    owner = jnp.broadcast_to(owner_ref[...], square)
    place = iota(square, 0)
    rho = place // 4
    output = ((place % 4) // 2) * (2 * NTGT) + 2 * ((rho % ny) * ncore + rho // ny) + place % 2
    owned = jnp.where(owner == output, 1.0, 0.0).astype(BF16)
    listed = jnp.max(jnp.where(lists_ref[...] == holder, 1.0, 0.0), axis=0, keepdims=True)
    member = jnp.where(inside, jnp.broadcast_to(listed, lines), 0.0).astype(BF16)
    by_block = jnp.dot(owned, member, preferred_element_type=F32).astype(BF16)
    cut = (NBLK, NBLK // 2)
    k = iota(cut, 1)
    for high in range(ncore):
        block = ((k // ny) % nlow) * (NTGT * nx) + ((k % ny) * ncore + high) * nx + k // (ny * nlow)
        order = jnp.where(iota(cut, 0) == block, 1.0, 0.0).astype(BF16)
        part = jnp.dot(by_block, order, preferred_element_type=F32).astype(BF16)
        mix_ref[high * NPATCH : (high + 1) * NPATCH, :] = part


def mixing(patch_counts, patch_owner, block_lists):
    return pl.pallas_call(
        mixing_kernel,
        out_shape=jax.ShapeDtypeStruct((2 * NPATCH, NBLK // 2), BF16),
        name="mixing",
    )(patch_counts.reshape(1, NPATCH), patch_owner.reshape(1, NPATCH), block_lists.T)


def tile_kernel(
    tgt_ref, src_ref, row_ref, col_ref, own_ref, tcols, scols, tfeat, sfeat, tgeo, sgeo, even, odd, rowacc, colacc
):
    rho, _ = device_place()
    at_row = lax.broadcasted_iota(jnp.int32, own_ref.shape, 0) == rho % 8
    at_lane = lax.broadcasted_iota(jnp.int32, own_ref.shape, 1) // COLS == rho // 8
    own_ref[...] = jnp.where(at_row & at_lane, 1.0, 0.0)
    targets, sources = tcols.shape[0], scols.shape[1]
    scale = wave_number / TURNS

    part = lax.broadcasted_iota(jnp.int32, (T_ROWS, LANES), 0)
    chosen = [selector(T_ROWS, {lane: (row, 1.0) for lane, row in LEFT.items()})]
    for parts in (X, Y, Z, tuple(range(T_AMP, T_AMP + 3))):
        chosen.append(jnp.where((part == parts[0]) | (part == parts[1]) | (part == parts[2]), 1.0, 0.0))
    chosen = jnp.concatenate(chosen, axis=1).astype(BF16)
    for g in range(targets // LANES):
        here = slice(g * LANES, (g + 1) * LANES)
        pieces = [tgt_ref[m].astype(F32) for m in (2 * g, 2 * g + 1)]
        for m, piece in enumerate(pieces):
            row = g * LANES + m * COLS
            tcols[row : row + HALF, :] = piece[:HALF, :COLS].astype(BF16)
            tcols[row + HALF : row + COLS, :] = piece[:HALF, COLS:].astype(BF16)
        geo = jnp.concatenate(beside(*(p[HALF:] for p in pieces)), axis=0)
        x, y, z, nx, ny, nz = (total(geo, parts) for parts in (X, Y, Z, NX, NY, NZ))
        rows = three(nx * x + ny * y + nz * z) + three((WAVE_SCALE * nz) * jnp.exp(scale * z)) + three(x * x + y * y + z * z)
        rows = [geo] + rows + [jnp.ones_like(x), jnp.zeros((T_ROWS - T_ONE - 1, LANES), F32)]
        wide = lax.dot_general(
            jnp.concatenate(rows, axis=0).astype(BF16), chosen, (((0,), (0,)), ((), ())), preferred_element_type=F32
        )
        tfeat[here, :] = wide[:, :LANES].astype(BF16)
        for k in range(4):
            tgeo[k, here, :] = wide[:, (k + 1) * LANES : (k + 2) * LANES]
    rights = [selector(S_ROWS, entries).T.astype(BF16) for entries in RIGHT]
    for g in range(sources // LANES):
        here = slice(g * LANES, (g + 1) * LANES)
        left, right = beside(*(src_ref[m].astype(F32) for m in (2 * g, 2 * g + 1)))
        scols[:HALF, here] = left[:HALF].astype(BF16)
        scols[HALF:, here] = right[:HALF].astype(BF16)
        geo = jnp.concatenate([left[HALF:], right[HALF:]], axis=0)
        x, y, z, area = (total(geo, parts) for parts in (X, Y, Z, AREA))
        share = area * (AREA_SCALE / TURNS**2)
        rows = three(share * x) + three(share * y) + three(share * z) + three(share)
        rows += three(x * x + y * y + z * z + area)
        rows = jnp.concatenate([geo] + rows + [jnp.ones_like(x)], axis=0).astype(BF16)
        for k in range(3):
            sfeat[k, :, here] = jnp.dot(rights[k], rows, preferred_element_type=F32).astype(BF16)
        for k, v in enumerate((x, y, z, area, (area * (1.0 / TURNS**2)) * jnp.exp(scale * z))):
            sgeo[k, :, here] = jnp.broadcast_to(v, (8, LANES))
    rowacc[...] = jnp.zeros_like(rowacc)
    colacc[...] = jnp.zeros_like(colacc)
    blocks = targets // STEP
    steps = blocks * (sources // CHUNK)

    def corner(k):
        return pl.multiple_of(lax.rem(k, blocks) * STEP, STEP), pl.multiple_of(lax.div(k, blocks) * CHUNK, CHUNK)

    def products(k, into):
        t0, s0 = corner(k)
        features = tfeat[pl.ds(t0, STEP), :]
        for m in range(3):
            into[m] = jnp.dot(features, sfeat[m, :, pl.ds(s0, CHUNK)], preferred_element_type=F32)
        into[3] = jnp.dot(tcols[pl.ds(t0, STEP), :], scols[:, pl.ds(s0, CHUNK)], preferred_element_type=F32)

    halves = range(CHUNK // LANES)

    def elements(k, made):
        t0, s0 = corner(k)
        lanes = [pl.ds(pl.multiple_of(s0 + h * LANES, LANES), LANES) for h in halves]
        src = [[jnp.concatenate([sgeo[m, :, lanes[h]]] * (ROWS // 8), axis=0) for m in range(5)] for h in halves]
        acc = [None for _ in halves]
        for r in range(0, STEP, ROWS):
            rows = pl.ds(pl.multiple_of(t0 + r, ROWS), ROWS)
            xt, yt, zt, amp = (tgeo[m, rows, :] for m in range(4))
            along = rowacc[rows, :]
            for h in halves:
                top, topi, mirror, image = (made[m, r : r + ROWS, h * LANES : (h + 1) * LANES] for m in range(4))
                xs, ys, zs, area, ebb = src[h]
                dx, dy, dz = xt - xs, yt - ys, zt - zs
                flat = dx * dx + dy * dy + area
                near = flat + dz * dz
                i1, i2, i3 = lax.rsqrt(near), lax.rsqrt(mirror), lax.rsqrt(flat)
                pair = top * (i1 * i1 * i1) + topi * (i2 * i2 * i2)
                phase = flat * i3
                f = phase - ((phase + ROUNDER) - ROUNDER)
                turn = 0.25 - jnp.abs(f)
                g = turn * turn
                p = g + MONIC[-1]
                for c in MONIC[-2::-1]:
                    p = p * g + c
                kern = pair - (amp * ebb) * (turn * p)
                w = kern.astype(BF16).astype(F32) * image
                acc[h] = w if acc[h] is None else acc[h] + w
                along = along + w
            rowacc[rows, :] = along
        for h in halves:
            colacc[:, lanes[h]] += sum(acc[h][m : m + 8] for m in range(0, ROWS, 8))

    products(0, even)

    def two(k, _):
        elements(2 * k, even)
        products(2 * k + 1, odd)
        elements(2 * k + 1, odd)
        products(jnp.minimum(2 * k + 2, steps - 1), even)
        return 0

    lax.fori_loop(0, steps // 2, two, 0)
    for g in range(sources // LANES):
        here = slice(g * LANES, (g + 1) * LANES)
        colacc[0:1, here] = jnp.sum(colacc[:, here], axis=0, keepdims=True)
    panels = col_ref.shape[2]
    for k in range(col_ref.shape[0]):
        col_ref[k] = colacc[0:1, k * panels : (k + 1) * panels]
    for g in range(targets // LANES):
        line = jnp.sum(rowacc[g * LANES : (g + 1) * LANES, :].T, axis=0, keepdims=True)
        for k in range(2):
            low, high = (2 * g + k) % 8, (2 * g + k) // 8
            row_ref[low : low + 1, high * panels : (high + 1) * panels] = line[:, k * panels : (k + 1) * panels]


def tile(tgt, src, panels):
    targets, sources = tgt.shape[0] * panels, src.shape[0] * panels
    return pl.pallas_call(
        tile_kernel,
        out_shape=(
            jax.ShapeDtypeStruct((8, LANES), F32),
            jax.ShapeDtypeStruct((src.shape[0], 1, panels), F32),
            jax.ShapeDtypeStruct((8, LANES), F32),
        ),
        scratch_shapes=[
            pltpu.VMEM((targets, COLS), BF16),
            pltpu.VMEM((COLS, sources), BF16),
            pltpu.VMEM((targets, LANES), BF16),
            pltpu.VMEM((3, LANES, sources), BF16),
            pltpu.VMEM((4, targets, LANES), F32),
            pltpu.VMEM((5, 8, sources), F32),
            pltpu.VMEM((4, STEP, CHUNK), F32),
            pltpu.VMEM((4, STEP, CHUNK), F32),
            pltpu.VMEM((targets, LANES), F32),
            pltpu.VMEM((8, sources), F32),
        ],
        compiler_params=pltpu.CompilerParams(vmem_limit_bytes=24 << 20),
        name="tile",
    )(tgt, src)


def patch_kernel(mix_ref, dens_ref, spline_ref, out_ref, own_ref):
    quarters = PARTS["z_hi"]
    panels = own_ref.shape[1]
    dens = jnp.concatenate(
        [
            jnp.concatenate([dens_ref[k] for k in range(q, dens_ref.shape[0], quarters)], axis=0)
            for q in range(quarters)
        ],
        axis=1,
    )
    mix = mix_ref[...]
    both = sum(jnp.dot(mix, part, preferred_element_type=F32) for part in split3(dens)[::-1])
    got = jnp.concatenate(
        [
            both[:NPATCH, q * LANES : q * LANES + panels] + both[NPATCH:, q * LANES + panels : (q + 1) * LANES]
            for q in range(quarters)
        ],
        axis=1,
    )
    spline = spline_ref[...]
    rows = sum(jnp.dot(part, spline, preferred_element_type=F32) for part in split3(got)[::-1])
    for piece in range(out_ref.shape[0]):
        lines = []
        for k in range(out_ref.shape[1] // 2):
            low, lanes = divmod(k, spline.shape[1] // LANES)
            row = 4 * piece + 2 * low
            lines.append(rows[row : row + 2, lanes * LANES : (lanes + 1) * LANES])
        out_ref[piece] = jnp.concatenate(lines, axis=0).astype(BF16)
    rho, gamma = device_place()
    line = dens_ref[gamma, pl.ds(rho % 8, 1), :]
    own_ref[...] = jnp.where(rho // 8 == 0, line[:, :panels], line[:, panels:])


def patch(mix, blocks, spline, panels):
    return pl.pallas_call(
        patch_kernel,
        out_shape=(
            jax.ShapeDtypeStruct((NTGT, NPATCH // NTGT * spline.shape[1] // LANES, LANES), BF16),
            jax.ShapeDtypeStruct((1, panels), F32),
        ),
        compiler_params=pltpu.CompilerParams(vmem_limit_bytes=16 << 20),
        name="patch",
    )(mix, blocks, spline)


def exchange(pieces, axes):
    return lax.all_to_all(pieces, axes, 0, 0, tiled=True)


def copies(value, count):
    return jnp.broadcast_to(value[None], (count,) + value.shape)


def on_device(
    positions, normals, areas, direct, adjoint, spline, block_lists, patch_counts, patch_owner
):
    panels = positions.shape[1]
    tgt = pack(pack_targets_kernel, NTGT, positions, normals, adjoint)
    src = pack(pack_sources_kernel, NSRC, positions, areas.reshape(1, panels), direct)
    mix = mixing(patch_counts, patch_owner, block_lists)
    tgt_all = exchange(tgt, TGT_AXES)
    src, mix = lax.optimization_barrier((src, mix))
    src_all = exchange(src, SRC_AXES)
    row_part, col_part, own_place = tile(tgt_all, src_all, panels)

    mine = jnp.sum(exchange(col_part, SRC_AXES), axis=0)
    row_part = row_part + own_place * jnp.tile(mine, (1, 2))
    dens = jnp.sum(exchange(copies(row_part, NTGT), TGT_AXES), axis=0)
    blocks = exchange(copies(dens, NSRC), SRC_AXES)

    contrib, own = patch(mix, blocks, spline[0], panels)
    rows = jnp.sum(exchange(contrib, TGT_AXES).astype(F32), axis=0).astype(BF16)
    low = PARTS["z_lo"]
    rows = rows.reshape(1, low, 1, 8, LANES)
    rows = jnp.broadcast_to(rows, (PARTS["x"], low, PARTS["z_hi"], 8, LANES)).reshape(NSRC, 8, LANES)
    rows = jnp.sum(exchange(rows, SRC_AXES).astype(F32), axis=0)
    patch_grad = rows.reshape(4, 2, LANES).transpose(1, 0, 2).reshape(2, 4 * LANES)
    return own.reshape(panels), patch_grad


def solution(mesh):
    fine = Mesh(mesh.devices.reshape(tuple(PARTS.values())), NAMES)
    placed = (
        P(None, NAMES),
        P(None, NAMES),
        P(NAMES),
        P(NAMES, None),
        P(NAMES, None),
        P(NAMES, None, None),
        P(),
        P(),
        P(),
    )
    return jax.shard_map(
        on_device,
        mesh=fine,
        in_specs=placed,
        out_specs=(P(NAMES), P(("z_lo", "y", "core"), None)),
        check_vma=False,
    )
```

```python
import jax
import jax.numpy as jnp
import numpy as np
from jax import lax
from jax.experimental import pallas as pl
from jax.experimental.pallas import tpu as pltpu
from jax.sharding import Mesh
from jax.sharding import PartitionSpec as P

F32 = jnp.float32
BF16 = jnp.bfloat16
BPAN = 256
NPATCH = 64
NBLK = 128
LANES = 128
wave_number = 6.0
inv_four_pi = 0.07957747154594767

TURNS = wave_number / (2.0 * np.pi)
DEGREE = 3


def sine_coefficients():
    k = np.arange(64)
    nodes = 0.25 * np.cos(np.pi * (2 * k + 1) / 128)
    fit = np.polynomial.chebyshev.Chebyshev.fit(nodes, np.sin(2 * np.pi * nodes), 2 * DEGREE + 1, domain=[-0.25, 0.25])
    return fit.convert(kind=np.polynomial.Polynomial).coef[1::2]


COEF = sine_coefficients()
LEAD = float(COEF[-1])
MONIC = [float(c / COEF[-1]) for c in COEF[:-1]]
ROUNDER = float(3 << 22)
AREA_SCALE = float(TURNS**2 * inv_four_pi)
WAVE_SCALE = float(2.0 * wave_number * inv_four_pi * LEAD)

PARTS = {"z_lo": 2, "y": 8, "core": 2, "x": 4, "z_hi": 4}
NAMES = tuple(PARTS)
TGT_AXES = ("core", "y")
SRC_AXES = ("x", "z_lo", "z_hi")
NTGT = PARTS["y"] * PARTS["core"]
NSRC = PARTS["z_lo"] * PARTS["x"] * PARTS["z_hi"]

COLS = 64
HALF = 32
DEPTH = 40
X, Y, Z = (0, 2, 4), (1, 3, 5), (8, 9, 10)
NX, NY, NZ = (6, 7), (11, 12), (13, 14)
AREA = (11, 12, 13)

T_DOT, T_AMP, T_SQUARE, T_ONE, T_ROWS = 16, 19, 22, 25, 32
S_MOMENT, S_SHARE, S_SQUARE, S_ONE, S_ROWS = 16, 25, 28, 31, 32


def product_lanes():
    left, right = [], [{}, {}, {}]
    for d, n in enumerate((NX, NY, NZ)):
        for a in range(2):
            for b in range(3):
                lane = len(left)
                left.append(n[a])
                right[0][lane] = (S_MOMENT + 3 * d + b, -1.0)
                right[1][lane] = (S_MOMENT + 3 * d + b, 1.0 if d == 2 else -1.0)
    for a in range(3):
        for b in range(3):
            lane = len(left)
            left.append(T_DOT + a)
            right[0][lane] = right[1][lane] = (S_SHARE + b, 1.0)
    for d, p in enumerate((X, Y, Z)):
        for a in range(3):
            for b in range(3):
                right[2][len(left)] = (p[b], 2.0 if d == 2 else -2.0)
                left.append(p[a])
    for a in range(3):
        right[2][len(left)] = (S_ONE, 1.0)
        left.append(T_SQUARE + a)
    for b in range(3):
        right[2][len(left)] = (S_SQUARE + b, 1.0)
        left.append(T_ONE)
    return dict(enumerate(left)), right


LEFT, RIGHT = product_lanes()


def selector(rows, entries):
    lane = lax.broadcasted_iota(jnp.int32, (8, LANES), 1)
    where, value = jnp.full((8, LANES), -1, jnp.int32), jnp.zeros((8, LANES), F32)
    for key, (row, sign) in entries.items():
        where = jnp.where(lane == key, row, where)
        value = jnp.where(lane == key, sign, value)
    at = lax.broadcasted_iota(jnp.int32, (rows, LANES), 0)
    many = (rows // 8, 1)
    return jnp.where(at == jnp.tile(where, many), jnp.tile(value, many), 0.0)


def split3(v):
    hi = v.astype(BF16)
    rest = v - hi.astype(F32)
    mid = rest.astype(BF16)
    lo = (rest - mid.astype(F32)).astype(BF16)
    return hi, mid, lo


def three(v):
    return [part.astype(F32) for part in split3(v)]


def scaled(pos):
    row = lax.broadcasted_iota(jnp.int32, pos.shape, 0)
    parts = three(jnp.where(row == 2, 0.5 * (pos - 1.2), pos) * TURNS)
    return [v[0:2] for v in parts], [v[2:3] for v in parts]


def lay(top, left, right, ref):
    geo = jnp.concatenate([jnp.concatenate(left, axis=0), jnp.concatenate(right, axis=0)], axis=1)
    top = jnp.concatenate([top[:HALF], top[HALF:]], axis=1)
    piece = jnp.concatenate([top, geo], axis=0).astype(BF16)
    for k in range(ref.shape[0]):
        ref[k] = piece


def pack_targets_kernel(pos_ref, nrm_ref, adj_ref, ref):
    flat, deep = scaled(pos_ref[...])
    nx, ny, nz = ([v[k : k + 1] for v in three(nrm_ref[...])[:2]] for k in range(3))
    lay(adj_ref[...].astype(F32), flat + nx, deep + ny + nz + [jnp.zeros_like(deep[0])], ref)


def pack_sources_kernel(pos_ref, area_ref, dir_ref, ref):
    flat, deep = scaled(pos_ref[...])
    none = jnp.zeros((2, pos_ref.shape[1]), F32)
    lay(dir_ref[...].astype(F32).T, flat + [none], deep + three(area_ref[...] * TURNS**2) + [none], ref)


def pack(kernel, count, *arrays):
    out = jax.ShapeDtypeStruct((count, DEPTH, LANES), BF16)
    return pl.pallas_call(kernel, out_shape=out, name="pack")(*arrays)


def beside(a, b):
    return (
        jnp.concatenate([a[:, :COLS], b[:, :COLS]], axis=1),
        jnp.concatenate([a[:, COLS:], b[:, COLS:]], axis=1),
    )


def total(value, parts):
    return sum(value[m : m + 1, :] for m in parts)


ROWS = 16
CHUNK = 256
STEP = 1024


def device_place():
    at = {name: lax.axis_index(name) for name in NAMES}
    rho = at["core"] * PARTS["y"] + at["y"]
    return rho, (at["x"] * PARTS["z_lo"] + at["z_lo"]) * PARTS["z_hi"] + at["z_hi"]


def mixing_kernel(counts_ref, owner_ref, lists_ref, mix_ref):
    holder = lax.axis_index(NAMES)
    nx, ncore, ny, nlow = (PARTS[name] for name in ("x", "core", "y", "z_lo"))

    def iota(shape, dim):
        return lax.broadcasted_iota(jnp.int32, shape, dim)

    square = (NPATCH, NPATCH)
    counts = jnp.broadcast_to(counts_ref[...], square)
    eye = iota(square, 0) == iota(square, 1)
    starts = jnp.sum(jnp.where(iota(square, 1) < iota(square, 0), counts, 0).astype(F32), axis=1, keepdims=True)
    own_counts = jnp.sum(jnp.where(eye, counts, 0).astype(F32), axis=1, keepdims=True)
    lines = (NPATCH, NBLK)
    ids = iota(lines, 1).astype(F32)
    inside = (starts <= ids) & (ids < starts + own_counts)
    owner = jnp.broadcast_to(owner_ref[...], square)
    place = iota(square, 0)
    rho = place // 4
    output = ((place % 4) // 2) * (2 * NTGT) + 2 * ((rho % ny) * ncore + rho // ny) + place % 2
    owned = jnp.where(owner == output, 1.0, 0.0).astype(BF16)
    listed = jnp.max(jnp.where(lists_ref[...] == holder, 1.0, 0.0), axis=0, keepdims=True)
    member = jnp.where(inside, jnp.broadcast_to(listed, lines), 0.0).astype(BF16)
    by_block = jnp.dot(owned, member, preferred_element_type=F32).astype(BF16)
    cut = (NBLK, NBLK // 2)
    k = iota(cut, 1)
    for high in range(ncore):
        block = ((k // ny) % nlow) * (NTGT * nx) + ((k % ny) * ncore + high) * nx + k // (ny * nlow)
        order = jnp.where(iota(cut, 0) == block, 1.0, 0.0).astype(BF16)
        part = jnp.dot(by_block, order, preferred_element_type=F32).astype(BF16)
        mix_ref[high * NPATCH : (high + 1) * NPATCH, :] = part


def mixing(patch_counts, patch_owner, block_lists):
    return pl.pallas_call(
        mixing_kernel,
        out_shape=jax.ShapeDtypeStruct((2 * NPATCH, NBLK // 2), BF16),
        name="mixing",
    )(patch_counts.reshape(1, NPATCH), patch_owner.reshape(1, NPATCH), block_lists.T)


def tile_kernel(
    tgt_ref, src_ref, row_ref, col_ref, own_ref, tcols, scols, tfeat, sfeat, tgeo, sgeo, even, odd, rowacc, colacc
):
    rho, _ = device_place()
    at_row = lax.broadcasted_iota(jnp.int32, own_ref.shape, 0) == rho % 8
    at_lane = lax.broadcasted_iota(jnp.int32, own_ref.shape, 1) // COLS == rho // 8
    own_ref[...] = jnp.where(at_row & at_lane, 1.0, 0.0)
    targets, sources = tcols.shape[0], scols.shape[1]
    scale = wave_number / TURNS

    part = lax.broadcasted_iota(jnp.int32, (T_ROWS, LANES), 0)
    chosen = [selector(T_ROWS, {lane: (row, 1.0) for lane, row in LEFT.items()})]
    for parts in (X, Y, Z, tuple(range(T_AMP, T_AMP + 3))):
        chosen.append(jnp.where((part == parts[0]) | (part == parts[1]) | (part == parts[2]), 1.0, 0.0))
    chosen = jnp.concatenate(chosen, axis=1).astype(BF16)
    for g in range(targets // LANES):
        here = slice(g * LANES, (g + 1) * LANES)
        pieces = [tgt_ref[m].astype(F32) for m in (2 * g, 2 * g + 1)]
        for m, piece in enumerate(pieces):
            row = g * LANES + m * COLS
            tcols[row : row + HALF, :] = piece[:HALF, :COLS].astype(BF16)
            tcols[row + HALF : row + COLS, :] = piece[:HALF, COLS:].astype(BF16)
        geo = jnp.concatenate(beside(*(p[HALF:] for p in pieces)), axis=0)
        x, y, z, nx, ny, nz = (total(geo, parts) for parts in (X, Y, Z, NX, NY, NZ))
        rows = three(nx * x + ny * y + nz * z) + three((WAVE_SCALE * nz) * jnp.exp(scale * z)) + three(x * x + y * y + z * z)
        rows = [geo] + rows + [jnp.ones_like(x), jnp.zeros((T_ROWS - T_ONE - 1, LANES), F32)]
        wide = lax.dot_general(
            jnp.concatenate(rows, axis=0).astype(BF16), chosen, (((0,), (0,)), ((), ())), preferred_element_type=F32
        )
        tfeat[here, :] = wide[:, :LANES].astype(BF16)
        for k in range(4):
            tgeo[k, here, :] = wide[:, (k + 1) * LANES : (k + 2) * LANES]
    rights = [selector(S_ROWS, entries).T.astype(BF16) for entries in RIGHT]
    for g in range(sources // LANES):
        here = slice(g * LANES, (g + 1) * LANES)
        left, right = beside(*(src_ref[m].astype(F32) for m in (2 * g, 2 * g + 1)))
        scols[:HALF, here] = left[:HALF].astype(BF16)
        scols[HALF:, here] = right[:HALF].astype(BF16)
        geo = jnp.concatenate([left[HALF:], right[HALF:]], axis=0)
        x, y, z, area = (total(geo, parts) for parts in (X, Y, Z, AREA))
        share = area * (AREA_SCALE / TURNS**2)
        rows = three(share * x) + three(share * y) + three(share * z) + three(share)
        rows += three(x * x + y * y + z * z + area)
        rows = jnp.concatenate([geo] + rows + [jnp.ones_like(x)], axis=0).astype(BF16)
        for k in range(3):
            sfeat[k, :, here] = jnp.dot(rights[k], rows, preferred_element_type=F32).astype(BF16)
        for k, v in enumerate((x, y, z, area, (area * (1.0 / TURNS**2)) * jnp.exp(scale * z))):
            sgeo[k, :, here] = jnp.broadcast_to(v, (8, LANES))
    rowacc[...] = jnp.zeros_like(rowacc)
    colacc[...] = jnp.zeros_like(colacc)
    blocks = targets // STEP
    steps = blocks * (sources // CHUNK)

    def corner(k):
        return pl.multiple_of(lax.rem(k, blocks) * STEP, STEP), pl.multiple_of(lax.div(k, blocks) * CHUNK, CHUNK)

    def products(k, into):
        t0, s0 = corner(k)
        features = tfeat[pl.ds(t0, STEP), :]
        for m in range(3):
            into[m] = jnp.dot(features, sfeat[m, :, pl.ds(s0, CHUNK)], preferred_element_type=F32)
        into[3] = jnp.dot(tcols[pl.ds(t0, STEP), :], scols[:, pl.ds(s0, CHUNK)], preferred_element_type=F32)

    halves = range(CHUNK // LANES)

    def elements(k, made):
        t0, s0 = corner(k)
        lanes = [pl.ds(pl.multiple_of(s0 + h * LANES, LANES), LANES) for h in halves]
        src = [[jnp.concatenate([sgeo[m, :, lanes[h]]] * (ROWS // 8), axis=0) for m in range(5)] for h in halves]
        acc = [None for _ in halves]
        for r in range(0, STEP, ROWS):
            rows = pl.ds(pl.multiple_of(t0 + r, ROWS), ROWS)
            xt, yt, zt, amp = (tgeo[m, rows, :] for m in range(4))
            along = rowacc[rows, :]
            for h in halves:
                top, topi, mirror, image = (made[m, r : r + ROWS, h * LANES : (h + 1) * LANES] for m in range(4))
                xs, ys, zs, area, ebb = src[h]
                dx, dy, dz = xt - xs, yt - ys, zt - zs
                flat = dx * dx + dy * dy + area
                near = flat + dz * dz
                i1, i2, i3 = lax.rsqrt(near), lax.rsqrt(mirror), lax.rsqrt(flat)
                pair = top * (i1 * i1 * i1) + topi * (i2 * i2 * i2)
                phase = flat * i3
                f = phase - ((phase + ROUNDER) - ROUNDER)
                turn = 0.25 - jnp.abs(f)
                g = turn * turn
                p = g + MONIC[-1]
                for c in MONIC[-2::-1]:
                    p = p * g + c
                kern = pair - (amp * ebb) * (turn * p)
                w = kern.astype(BF16).astype(F32) * image
                acc[h] = w if acc[h] is None else acc[h] + w
                along = along + w
            rowacc[rows, :] = along
        for h in halves:
            colacc[:, lanes[h]] += sum(acc[h][m : m + 8] for m in range(0, ROWS, 8))

    products(0, even)

    def two(k, _):
        elements(2 * k, even)
        products(2 * k + 1, odd)
        elements(2 * k + 1, odd)
        products(jnp.minimum(2 * k + 2, steps - 1), even)
        return 0

    lax.fori_loop(0, steps // 2, two, 0)
    for g in range(sources // LANES):
        here = slice(g * LANES, (g + 1) * LANES)
        colacc[0:1, here] = jnp.sum(colacc[:, here], axis=0, keepdims=True)
    panels = col_ref.shape[2]
    for k in range(col_ref.shape[0]):
        col_ref[k] = colacc[0:1, k * panels : (k + 1) * panels]
    for g in range(targets // LANES):
        line = jnp.sum(rowacc[g * LANES : (g + 1) * LANES, :].T, axis=0, keepdims=True)
        for k in range(2):
            low, high = (2 * g + k) % 8, (2 * g + k) // 8
            row_ref[low : low + 1, high * panels : (high + 1) * panels] = line[:, k * panels : (k + 1) * panels]


def tile(tgt, src, panels):
    targets, sources = tgt.shape[0] * panels, src.shape[0] * panels
    return pl.pallas_call(
        tile_kernel,
        out_shape=(
            jax.ShapeDtypeStruct((8, LANES), F32),
            jax.ShapeDtypeStruct((src.shape[0], 1, panels), F32),
            jax.ShapeDtypeStruct((8, LANES), F32),
        ),
        scratch_shapes=[
            pltpu.VMEM((targets, COLS), BF16),
            pltpu.VMEM((COLS, sources), BF16),
            pltpu.VMEM((targets, LANES), BF16),
            pltpu.VMEM((3, LANES, sources), BF16),
            pltpu.VMEM((4, targets, LANES), F32),
            pltpu.VMEM((5, 8, sources), F32),
            pltpu.VMEM((4, STEP, CHUNK), F32),
            pltpu.VMEM((4, STEP, CHUNK), F32),
            pltpu.VMEM((targets, LANES), F32),
            pltpu.VMEM((8, sources), F32),
        ],
        compiler_params=pltpu.CompilerParams(vmem_limit_bytes=24 << 20),
        name="tile",
    )(tgt, src)


def patch_kernel(mix_ref, dens_ref, spline_ref, out_ref, own_ref):
    quarters = PARTS["z_hi"]
    panels = own_ref.shape[1]
    dens = jnp.concatenate(
        [
            jnp.concatenate([dens_ref[k] for k in range(q, dens_ref.shape[0], quarters)], axis=0)
            for q in range(quarters)
        ],
        axis=1,
    )
    mix = mix_ref[...]
    both = sum(jnp.dot(mix, part, preferred_element_type=F32) for part in split3(dens)[1::-1])
    got = jnp.concatenate(
        [
            both[:NPATCH, q * LANES : q * LANES + panels] + both[NPATCH:, q * LANES + panels : (q + 1) * LANES]
            for q in range(quarters)
        ],
        axis=1,
    )
    spline = spline_ref[...]
    rows = sum(jnp.dot(part, spline, preferred_element_type=F32) for part in split3(got)[1::-1])
    for piece in range(out_ref.shape[0]):
        for k in range(out_ref.shape[1] // 2):
            low, lanes = divmod(k, spline.shape[1] // LANES)
            row = 4 * piece + 2 * low
            out_ref[piece, 2 * k : 2 * k + 2, :] = rows[row : row + 2, lanes * LANES : (lanes + 1) * LANES]
    rho, gamma = device_place()
    line = dens_ref[gamma, pl.ds(rho % 8, 1), :]
    own_ref[...] = jnp.where(rho // 8 == 0, line[:, :panels], line[:, panels:])


def patch(mix, blocks, spline, panels):
    return pl.pallas_call(
        patch_kernel,
        out_shape=(
            jax.ShapeDtypeStruct((NTGT, NPATCH // NTGT * spline.shape[1] // LANES, LANES), F32),
            jax.ShapeDtypeStruct((1, panels), F32),
        ),
        compiler_params=pltpu.CompilerParams(vmem_limit_bytes=16 << 20),
        name="patch",
    )(mix, blocks, spline)


def exchange(pieces, axes):
    return lax.all_to_all(pieces, axes, 0, 0, tiled=True)


def copies(value, count):
    return jnp.broadcast_to(value[None], (count,) + value.shape)


def on_device(
    positions, normals, areas, direct, adjoint, spline, block_lists, patch_counts, patch_owner
):
    panels = positions.shape[1]
    tgt = pack(pack_targets_kernel, NTGT, positions, normals, adjoint)
    src = pack(pack_sources_kernel, NSRC, positions, areas.reshape(1, panels), direct)
    mix = mixing(patch_counts, patch_owner, block_lists)
    tgt_all = exchange(tgt, TGT_AXES)
    src, mix = lax.optimization_barrier((src, mix))
    src_all = exchange(src, SRC_AXES)
    row_part, col_part, own_place = tile(tgt_all, src_all, panels)

    mine = jnp.sum(exchange(col_part, SRC_AXES), axis=0)
    row_part = row_part + own_place * jnp.tile(mine, (1, 2))
    dens = jnp.sum(exchange(copies(row_part, NTGT), TGT_AXES), axis=0)
    blocks = exchange(copies(dens, NSRC), SRC_AXES)

    contrib, own = patch(mix, blocks, spline[0], panels)
    rows = jnp.sum(exchange(contrib, TGT_AXES), axis=0)
    low = PARTS["z_lo"]
    rows = rows.reshape(1, low, 1, 8, LANES)
    rows = jnp.broadcast_to(rows, (PARTS["x"], low, PARTS["z_hi"], 8, LANES)).reshape(NSRC, 8, LANES)
    rows = jnp.sum(exchange(rows, SRC_AXES), axis=0)
    patch_grad = rows.reshape(4, 2, LANES).transpose(1, 0, 2).reshape(2, 4 * LANES)
    return own.reshape(panels), patch_grad


def solution(mesh):
    fine = Mesh(mesh.devices.reshape(tuple(PARTS.values())), NAMES)
    placed = (
        P(None, NAMES),
        P(None, NAMES),
        P(NAMES),
        P(NAMES, None),
        P(NAMES, None),
        P(NAMES, None, None),
        P(),
        P(),
        P(),
    )
    return jax.shard_map(
        on_device,
        mesh=fine,
        in_specs=placed,
        out_specs=(P(NAMES), P(("z_lo", "y", "core"), None)),
        check_vma=False,
    )
```

```python
import jax
import jax.numpy as jnp
import numpy as np
from jax import lax
from jax.experimental import pallas as pl
from jax.experimental.pallas import tpu as pltpu
from jax.sharding import Mesh
from jax.sharding import PartitionSpec as P

F32 = jnp.float32
BF16 = jnp.bfloat16
BPAN = 256
NPATCH = 64
NBLK = 128
LANES = 128
wave_number = 6.0
inv_four_pi = 0.07957747154594767

TURNS = wave_number / (2.0 * np.pi)
DEGREE = 3


def sine_coefficients():
    k = np.arange(64)
    nodes = 0.25 * np.cos(np.pi * (2 * k + 1) / 128)
    fit = np.polynomial.chebyshev.Chebyshev.fit(nodes, np.sin(2 * np.pi * nodes), 2 * DEGREE + 1, domain=[-0.25, 0.25])
    return fit.convert(kind=np.polynomial.Polynomial).coef[1::2]


COEF = sine_coefficients()
LEAD = float(COEF[-1])
MONIC = [float(c / COEF[-1]) for c in COEF[:-1]]
ROUNDER = float(3 << 22)
AREA_SCALE = float(TURNS**2 * inv_four_pi)
WAVE_SCALE = float(2.0 * wave_number * inv_four_pi * LEAD)

PARTS = {"z_lo": 2, "y": 8, "core": 2, "x": 4, "z_hi": 4}
NAMES = tuple(PARTS)
TGT_AXES = ("core", "y")
SRC_AXES = ("x", "z_lo", "z_hi")
NTGT = PARTS["y"] * PARTS["core"]
NSRC = PARTS["z_lo"] * PARTS["x"] * PARTS["z_hi"]

COLS = 64
HALF = 32
DEPTH = 40
X, Y, Z = (0, 2, 4), (1, 3, 5), (8, 9, 10)
NX, NY, NZ = (6, 7), (11, 12), (13, 14)
AREA = (11, 12, 13)

T_DOT, T_AMP, T_SQUARE, T_ONE, T_ROWS = 16, 19, 22, 25, 32
S_MOMENT, S_SHARE, S_SQUARE, S_ONE, S_ROWS = 16, 25, 28, 31, 32


def product_lanes():
    left, right = [], [{}, {}, {}]
    for d, n in enumerate((NX, NY, NZ)):
        for a in range(2):
            for b in range(3):
                lane = len(left)
                left.append(n[a])
                right[0][lane] = (S_MOMENT + 3 * d + b, -1.0)
                right[1][lane] = (S_MOMENT + 3 * d + b, 1.0 if d == 2 else -1.0)
    for a in range(3):
        for b in range(3):
            lane = len(left)
            left.append(T_DOT + a)
            right[0][lane] = right[1][lane] = (S_SHARE + b, 1.0)
    for d, p in enumerate((X, Y, Z)):
        for a in range(3):
            for b in range(3):
                right[2][len(left)] = (p[b], 2.0 if d == 2 else -2.0)
                left.append(p[a])
    for a in range(3):
        right[2][len(left)] = (S_ONE, 1.0)
        left.append(T_SQUARE + a)
    for b in range(3):
        right[2][len(left)] = (S_SQUARE + b, 1.0)
        left.append(T_ONE)
    return dict(enumerate(left)), right


LEFT, RIGHT = product_lanes()


def selector(rows, entries):
    lane = lax.broadcasted_iota(jnp.int32, (8, LANES), 1)
    where, value = jnp.full((8, LANES), -1, jnp.int32), jnp.zeros((8, LANES), F32)
    for key, (row, sign) in entries.items():
        where = jnp.where(lane == key, row, where)
        value = jnp.where(lane == key, sign, value)
    at = lax.broadcasted_iota(jnp.int32, (rows, LANES), 0)
    many = (rows // 8, 1)
    return jnp.where(at == jnp.tile(where, many), jnp.tile(value, many), 0.0)


def split3(v):
    hi = v.astype(BF16)
    rest = v - hi.astype(F32)
    mid = rest.astype(BF16)
    lo = (rest - mid.astype(F32)).astype(BF16)
    return hi, mid, lo


def three(v):
    return [part.astype(F32) for part in split3(v)]


def scaled(pos):
    row = lax.broadcasted_iota(jnp.int32, pos.shape, 0)
    parts = three(jnp.where(row == 2, 0.5 * (pos - 1.2), pos) * TURNS)
    return [v[0:2] for v in parts], [v[2:3] for v in parts]


def lay(top, left, right, ref):
    geo = jnp.concatenate([jnp.concatenate(left, axis=0), jnp.concatenate(right, axis=0)], axis=1)
    top = jnp.concatenate([top[:HALF], top[HALF:]], axis=1)
    piece = jnp.concatenate([top, geo], axis=0).astype(BF16)
    for k in range(ref.shape[0]):
        ref[k] = piece


def pack_targets_kernel(pos_ref, nrm_ref, adj_ref, ref):
    flat, deep = scaled(pos_ref[...])
    nx, ny, nz = ([v[k : k + 1] for v in three(nrm_ref[...])[:2]] for k in range(3))
    lay(adj_ref[...].astype(F32), flat + nx, deep + ny + nz + [jnp.zeros_like(deep[0])], ref)


def pack_sources_kernel(pos_ref, area_ref, dir_ref, ref):
    flat, deep = scaled(pos_ref[...])
    none = jnp.zeros((2, pos_ref.shape[1]), F32)
    lay(dir_ref[...].astype(F32).T, flat + [none], deep + three(area_ref[...] * TURNS**2) + [none], ref)


def pack(kernel, count, *arrays):
    out = jax.ShapeDtypeStruct((count, DEPTH, LANES), BF16)
    return pl.pallas_call(kernel, out_shape=out, name="pack")(*arrays)


def beside(a, b):
    return (
        jnp.concatenate([a[:, :COLS], b[:, :COLS]], axis=1),
        jnp.concatenate([a[:, COLS:], b[:, COLS:]], axis=1),
    )


def total(value, parts):
    return sum(value[m : m + 1, :] for m in parts)


ROWS = 16
CHUNK = 256
STEP = 1024


def device_place():
    at = {name: lax.axis_index(name) for name in NAMES}
    rho = at["core"] * PARTS["y"] + at["y"]
    return rho, (at["x"] * PARTS["z_lo"] + at["z_lo"]) * PARTS["z_hi"] + at["z_hi"]


def mixing_kernel(counts_ref, owner_ref, lists_ref, mix_ref):
    holder = lax.axis_index(NAMES)
    nx, ncore, ny, nlow = (PARTS[name] for name in ("x", "core", "y", "z_lo"))

    def iota(shape, dim):
        return lax.broadcasted_iota(jnp.int32, shape, dim)

    square = (NPATCH, NPATCH)
    counts = jnp.broadcast_to(counts_ref[...], square)
    eye = iota(square, 0) == iota(square, 1)
    starts = jnp.sum(jnp.where(iota(square, 1) < iota(square, 0), counts, 0).astype(F32), axis=1, keepdims=True)
    own_counts = jnp.sum(jnp.where(eye, counts, 0).astype(F32), axis=1, keepdims=True)
    lines = (NPATCH, NBLK)
    ids = iota(lines, 1).astype(F32)
    inside = (starts <= ids) & (ids < starts + own_counts)
    owner = jnp.broadcast_to(owner_ref[...], square)
    place = iota(square, 0)
    rho = place // 4
    output = ((place % 4) // 2) * (2 * NTGT) + 2 * ((rho % ny) * ncore + rho // ny) + place % 2
    owned = jnp.where(owner == output, 1.0, 0.0).astype(BF16)
    listed = jnp.max(jnp.where(lists_ref[...] == holder, 1.0, 0.0), axis=0, keepdims=True)
    member = jnp.where(inside, jnp.broadcast_to(listed, lines), 0.0).astype(BF16)
    by_block = jnp.dot(owned, member, preferred_element_type=F32).astype(BF16)
    cut = (NBLK, NBLK // 2)
    k = iota(cut, 1)
    for high in range(ncore):
        block = ((k // ny) % nlow) * (NTGT * nx) + ((k % ny) * ncore + high) * nx + k // (ny * nlow)
        order = jnp.where(iota(cut, 0) == block, 1.0, 0.0).astype(BF16)
        part = jnp.dot(by_block, order, preferred_element_type=F32).astype(BF16)
        mix_ref[high * NPATCH : (high + 1) * NPATCH, :] = part


def mixing(patch_counts, patch_owner, block_lists):
    return pl.pallas_call(
        mixing_kernel,
        out_shape=jax.ShapeDtypeStruct((2 * NPATCH, NBLK // 2), BF16),
        name="mixing",
    )(patch_counts.reshape(1, NPATCH), patch_owner.reshape(1, NPATCH), block_lists.T)


def tile_kernel(
    tgt_ref, src_ref, row_ref, col_ref, own_ref, tcols, scols, tfeat, sfeat, tgeo, sgeo, even, odd, rowacc, colacc
):
    rho, _ = device_place()
    at_row = lax.broadcasted_iota(jnp.int32, own_ref.shape, 0) == rho % 8
    at_lane = lax.broadcasted_iota(jnp.int32, own_ref.shape, 1) // COLS == rho // 8
    own_ref[...] = jnp.where(at_row & at_lane, 1.0, 0.0)
    targets, sources = tcols.shape[0], scols.shape[1]
    scale = wave_number / TURNS

    part = lax.broadcasted_iota(jnp.int32, (T_ROWS, LANES), 0)
    chosen = [selector(T_ROWS, {lane: (row, 1.0) for lane, row in LEFT.items()})]
    for parts in (X, Y, Z, tuple(range(T_AMP, T_AMP + 3))):
        chosen.append(jnp.where((part == parts[0]) | (part == parts[1]) | (part == parts[2]), 1.0, 0.0))
    chosen = jnp.concatenate(chosen, axis=1).astype(BF16)
    for g in range(targets // LANES):
        here = slice(g * LANES, (g + 1) * LANES)
        pieces = [tgt_ref[m].astype(F32) for m in (2 * g, 2 * g + 1)]
        for m, piece in enumerate(pieces):
            row = g * LANES + m * COLS
            tcols[row : row + HALF, :] = piece[:HALF, :COLS].astype(BF16)
            tcols[row + HALF : row + COLS, :] = piece[:HALF, COLS:].astype(BF16)
        geo = jnp.concatenate(beside(*(p[HALF:] for p in pieces)), axis=0)
        x, y, z, nx, ny, nz = (total(geo, parts) for parts in (X, Y, Z, NX, NY, NZ))
        rows = three(nx * x + ny * y + nz * z) + three((WAVE_SCALE * nz) * jnp.exp(scale * z)) + three(x * x + y * y + z * z)
        rows = [geo] + rows + [jnp.ones_like(x), jnp.zeros((T_ROWS - T_ONE - 1, LANES), F32)]
        wide = lax.dot_general(
            jnp.concatenate(rows, axis=0).astype(BF16), chosen, (((0,), (0,)), ((), ())), preferred_element_type=F32
        )
        tfeat[here, :] = wide[:, :LANES].astype(BF16)
        for k in range(4):
            tgeo[k, here, :] = wide[:, (k + 1) * LANES : (k + 2) * LANES]
    rights = [selector(S_ROWS, entries).T.astype(BF16) for entries in RIGHT]
    for g in range(sources // LANES):
        here = slice(g * LANES, (g + 1) * LANES)
        left, right = beside(*(src_ref[m].astype(F32) for m in (2 * g, 2 * g + 1)))
        scols[:HALF, here] = left[:HALF].astype(BF16)
        scols[HALF:, here] = right[:HALF].astype(BF16)
        geo = jnp.concatenate([left[HALF:], right[HALF:]], axis=0)
        x, y, z, area = (total(geo, parts) for parts in (X, Y, Z, AREA))
        share = area * (AREA_SCALE / TURNS**2)
        rows = three(share * x) + three(share * y) + three(share * z) + three(share)
        rows += three(x * x + y * y + z * z + area)
        rows = jnp.concatenate([geo] + rows + [jnp.ones_like(x)], axis=0).astype(BF16)
        for k in range(3):
            sfeat[k, :, here] = jnp.dot(rights[k], rows, preferred_element_type=F32).astype(BF16)
        for k, v in enumerate((x, y, z, area, (area * (1.0 / TURNS**2)) * jnp.exp(scale * z))):
            sgeo[k, :, here] = jnp.broadcast_to(v, (8, LANES))
    rowacc[...] = jnp.zeros_like(rowacc)
    colacc[...] = jnp.zeros_like(colacc)
    blocks = targets // STEP
    steps = blocks * (sources // CHUNK)

    def corner(k):
        return pl.multiple_of(lax.rem(k, blocks) * STEP, STEP), pl.multiple_of(lax.div(k, blocks) * CHUNK, CHUNK)

    def products(k, into):
        t0, s0 = corner(k)
        features = tfeat[pl.ds(t0, STEP), :]
        for m in range(3):
            into[m] = jnp.dot(features, sfeat[m, :, pl.ds(s0, CHUNK)], preferred_element_type=F32)
        into[3] = jnp.dot(tcols[pl.ds(t0, STEP), :], scols[:, pl.ds(s0, CHUNK)], preferred_element_type=F32)

    halves = range(CHUNK // LANES)

    def elements(k, made):
        t0, s0 = corner(k)
        lanes = [pl.ds(pl.multiple_of(s0 + h * LANES, LANES), LANES) for h in halves]
        src = [[jnp.concatenate([sgeo[m, :, lanes[h]]] * (ROWS // 8), axis=0) for m in range(5)] for h in halves]
        acc = [None for _ in halves]
        for r in range(0, STEP, ROWS):
            rows = pl.ds(pl.multiple_of(t0 + r, ROWS), ROWS)
            xt, yt, zt, amp = (tgeo[m, rows, :] for m in range(4))
            along = rowacc[rows, :]
            for h in halves:
                top, topi, mirror, image = (made[m, r : r + ROWS, h * LANES : (h + 1) * LANES] for m in range(4))
                xs, ys, zs, area, ebb = src[h]
                dx, dy, dz = xt - xs, yt - ys, zt - zs
                flat = dx * dx + dy * dy + area
                near = flat + dz * dz
                i1, i2, i3 = lax.rsqrt(near), lax.rsqrt(mirror), lax.rsqrt(flat)
                pair = top * (i1 * i1 * i1) + topi * (i2 * i2 * i2)
                phase = flat * i3
                f = phase - ((phase + ROUNDER) - ROUNDER)
                turn = 0.25 - jnp.abs(f)
                g = turn * turn
                p = g + MONIC[-1]
                for c in MONIC[-2::-1]:
                    p = p * g + c
                kern = pair - (amp * ebb) * (turn * p)
                w = kern.astype(BF16).astype(F32) * image
                acc[h] = w if acc[h] is None else acc[h] + w
                along = along + w
            rowacc[rows, :] = along
        for h in halves:
            colacc[:, lanes[h]] += sum(acc[h][m : m + 8] for m in range(0, ROWS, 8))

    products(0, even)

    def two(k, _):
        elements(2 * k, even)
        products(2 * k + 1, odd)
        elements(2 * k + 1, odd)
        products(jnp.minimum(2 * k + 2, steps - 1), even)
        return 0

    lax.fori_loop(0, steps // 2, two, 0)
    for g in range(sources // LANES):
        here = slice(g * LANES, (g + 1) * LANES)
        colacc[0:1, here] = jnp.sum(colacc[:, here], axis=0, keepdims=True)
    panels = col_ref.shape[2]
    for k in range(col_ref.shape[0]):
        col_ref[k] = colacc[0:1, k * panels : (k + 1) * panels]
    for g in range(targets // LANES):
        line = jnp.sum(rowacc[g * LANES : (g + 1) * LANES, :].T, axis=0, keepdims=True)
        for k in range(2):
            low, high = (2 * g + k) % 8, (2 * g + k) // 8
            row_ref[low : low + 1, high * panels : (high + 1) * panels] = line[:, k * panels : (k + 1) * panels]


def tile(tgt, src, panels):
    targets, sources = tgt.shape[0] * panels, src.shape[0] * panels
    return pl.pallas_call(
        tile_kernel,
        out_shape=(
            jax.ShapeDtypeStruct((8, LANES), F32),
            jax.ShapeDtypeStruct((src.shape[0], 1, panels), F32),
            jax.ShapeDtypeStruct((8, LANES), F32),
        ),
        scratch_shapes=[
            pltpu.VMEM((targets, COLS), BF16),
            pltpu.VMEM((COLS, sources), BF16),
            pltpu.VMEM((targets, LANES), BF16),
            pltpu.VMEM((3, LANES, sources), BF16),
            pltpu.VMEM((4, targets, LANES), F32),
            pltpu.VMEM((5, 8, sources), F32),
            pltpu.VMEM((4, STEP, CHUNK), F32),
            pltpu.VMEM((4, STEP, CHUNK), F32),
            pltpu.VMEM((targets, LANES), F32),
            pltpu.VMEM((8, sources), F32),
        ],
        compiler_params=pltpu.CompilerParams(vmem_limit_bytes=24 << 20),
        name="tile",
    )(tgt, src)


def patch_kernel(mix_ref, dens_ref, spline_ref, out_ref, own_ref):
    quarters = PARTS["z_hi"]
    panels = own_ref.shape[1]
    dens = jnp.concatenate(
        [
            jnp.concatenate([dens_ref[k] for k in range(q, dens_ref.shape[0], quarters)], axis=0)
            for q in range(quarters)
        ],
        axis=1,
    )
    mix = mix_ref[...]
    both = sum(jnp.dot(mix, part, preferred_element_type=F32) for part in split3(dens)[1::-1])
    got = jnp.concatenate(
        [
            both[:NPATCH, q * LANES : q * LANES + panels] + both[NPATCH:, q * LANES + panels : (q + 1) * LANES]
            for q in range(quarters)
        ],
        axis=1,
    )
    spline = spline_ref[...]
    rows = sum(jnp.dot(part, spline, preferred_element_type=F32) for part in split3(got)[1::-1])
    for piece in range(out_ref.shape[0]):
        for k in range(out_ref.shape[1] // 2):
            low, lanes = divmod(k, spline.shape[1] // LANES)
            row = 4 * piece + 2 * low
            out_ref[piece, 2 * k : 2 * k + 2, :] = rows[row : row + 2, lanes * LANES : (lanes + 1) * LANES]
    rho, gamma = device_place()
    line = dens_ref[gamma, pl.ds(rho % 8, 1), :]
    own_ref[...] = jnp.where(rho // 8 == 0, line[:, :panels], line[:, panels:])


def patch(mix, blocks, spline, panels):
    return pl.pallas_call(
        patch_kernel,
        out_shape=(
            jax.ShapeDtypeStruct((NTGT, NPATCH // NTGT * spline.shape[1] // LANES, LANES), F32),
            jax.ShapeDtypeStruct((1, panels), F32),
        ),
        compiler_params=pltpu.CompilerParams(vmem_limit_bytes=16 << 20),
        name="patch",
    )(mix, blocks, spline)


def exchange(pieces, axes):
    return lax.all_to_all(pieces, axes, 0, 0, tiled=True)


def copies(value, count):
    return jnp.broadcast_to(value[None], (count,) + value.shape)


def on_device(
    positions, normals, areas, direct, adjoint, spline, block_lists, patch_counts, patch_owner
):
    panels = positions.shape[1]
    tgt = pack(pack_targets_kernel, NTGT, positions, normals, adjoint)
    src = pack(pack_sources_kernel, NSRC, positions, areas.reshape(1, panels), direct)
    mix = mixing(patch_counts, patch_owner, block_lists)
    src_all = exchange(src, SRC_AXES)
    tgt, mix, src_all = lax.optimization_barrier((tgt, mix, src_all))
    tgt_all = exchange(tgt, TGT_AXES)
    row_part, col_part, own_place = tile(tgt_all, src_all, panels)

    mine = jnp.sum(exchange(col_part, SRC_AXES), axis=0)
    row_part = row_part + own_place * jnp.tile(mine, (1, 2))
    dens = jnp.sum(exchange(copies(row_part, NTGT), TGT_AXES), axis=0)
    blocks = exchange(copies(dens, NSRC), SRC_AXES)

    contrib, own = patch(mix, blocks, spline[0], panels)
    rows = jnp.sum(exchange(contrib, TGT_AXES), axis=0)
    low = PARTS["z_lo"]
    rows = rows.reshape(1, low, 1, 8, LANES)
    rows = jnp.broadcast_to(rows, (PARTS["x"], low, PARTS["z_hi"], 8, LANES)).reshape(NSRC, 8, LANES)
    rows = jnp.sum(exchange(rows, SRC_AXES), axis=0)
    patch_grad = rows.reshape(4, 2, LANES).transpose(1, 0, 2).reshape(2, 4 * LANES)
    return own.reshape(panels), patch_grad


def solution(mesh):
    fine = Mesh(mesh.devices.reshape(tuple(PARTS.values())), NAMES)
    placed = (
        P(None, NAMES),
        P(None, NAMES),
        P(NAMES),
        P(NAMES, None),
        P(NAMES, None),
        P(NAMES, None, None),
        P(),
        P(),
        P(),
    )
    return jax.shard_map(
        on_device,
        mesh=fine,
        in_specs=placed,
        out_specs=(P(NAMES), P(("z_lo", "y", "core"), None)),
        check_vma=False,
    )
```

```python
import jax
import jax.numpy as jnp
import numpy as np
from jax import lax
from jax.experimental import pallas as pl
from jax.experimental.pallas import tpu as pltpu
from jax.sharding import Mesh
from jax.sharding import PartitionSpec as P

F32 = jnp.float32
BF16 = jnp.bfloat16
BPAN = 256
NPATCH = 64
NBLK = 128
LANES = 128
wave_number = 6.0
inv_four_pi = 0.07957747154594767

TURNS = wave_number / (2.0 * np.pi)
DEGREE = 3


def sine_coefficients():
    k = np.arange(64)
    nodes = 0.25 * np.cos(np.pi * (2 * k + 1) / 128)
    fit = np.polynomial.chebyshev.Chebyshev.fit(nodes, np.sin(2 * np.pi * nodes), 2 * DEGREE + 1, domain=[-0.25, 0.25])
    return fit.convert(kind=np.polynomial.Polynomial).coef[1::2]


COEF = sine_coefficients()
LEAD = float(COEF[-1])
MONIC = [float(c / COEF[-1]) for c in COEF[:-1]]
ROUNDER = float(3 << 22)
AREA_SCALE = float(TURNS**2 * inv_four_pi)
WAVE_SCALE = float(2.0 * wave_number * inv_four_pi * LEAD)

PARTS = {"z_lo": 2, "y": 8, "core": 2, "x": 4, "z_hi": 4}
NAMES = tuple(PARTS)
TGT_AXES = ("core", "y")
SRC_AXES = ("x", "z_lo", "z_hi")
NTGT = PARTS["y"] * PARTS["core"]
NSRC = PARTS["z_lo"] * PARTS["x"] * PARTS["z_hi"]

COLS = 64
HALF = 32
DEPTH = 40
X, Y, Z = (0, 2, 4), (1, 3, 5), (8, 9, 10)
NX, NY, NZ = (6, 7), (11, 12), (13, 14)
AREA = (11, 12, 13)

T_DOT, T_AMP, T_SQUARE, T_ONE, T_ROWS = 16, 19, 22, 25, 32
S_MOMENT, S_SHARE, S_SQUARE, S_ONE, S_ROWS = 16, 25, 28, 31, 32


def product_lanes():
    left, right = [], [{}, {}, {}]
    for d, n in enumerate((NX, NY, NZ)):
        for a in range(2):
            for b in range(3):
                lane = len(left)
                left.append(n[a])
                right[0][lane] = (S_MOMENT + 3 * d + b, -1.0)
                right[1][lane] = (S_MOMENT + 3 * d + b, 1.0 if d == 2 else -1.0)
    for a in range(3):
        for b in range(3):
            lane = len(left)
            left.append(T_DOT + a)
            right[0][lane] = right[1][lane] = (S_SHARE + b, 1.0)
    for d, p in enumerate((X, Y, Z)):
        for a in range(3):
            for b in range(3):
                right[2][len(left)] = (p[b], 2.0 if d == 2 else -2.0)
                left.append(p[a])
    for a in range(3):
        right[2][len(left)] = (S_ONE, 1.0)
        left.append(T_SQUARE + a)
    for b in range(3):
        right[2][len(left)] = (S_SQUARE + b, 1.0)
        left.append(T_ONE)
    return dict(enumerate(left)), right


LEFT, RIGHT = product_lanes()


def selector(rows, entries):
    lane = lax.broadcasted_iota(jnp.int32, (8, LANES), 1)
    where, value = jnp.full((8, LANES), -1, jnp.int32), jnp.zeros((8, LANES), F32)
    for key, (row, sign) in entries.items():
        where = jnp.where(lane == key, row, where)
        value = jnp.where(lane == key, sign, value)
    at = lax.broadcasted_iota(jnp.int32, (rows, LANES), 0)
    many = (rows // 8, 1)
    return jnp.where(at == jnp.tile(where, many), jnp.tile(value, many), 0.0)


def split3(v):
    hi = v.astype(BF16)
    rest = v - hi.astype(F32)
    mid = rest.astype(BF16)
    lo = (rest - mid.astype(F32)).astype(BF16)
    return hi, mid, lo


def three(v):
    return [part.astype(F32) for part in split3(v)]


def scaled(pos):
    row = lax.broadcasted_iota(jnp.int32, pos.shape, 0)
    parts = three(jnp.where(row == 2, 0.5 * (pos - 1.2), pos) * TURNS)
    return [v[0:2] for v in parts], [v[2:3] for v in parts]


def lay(top, left, right, ref):
    geo = jnp.concatenate([jnp.concatenate(left, axis=0), jnp.concatenate(right, axis=0)], axis=1)
    top = jnp.concatenate([top[:HALF], top[HALF:]], axis=1)
    piece = jnp.concatenate([top, geo], axis=0).astype(BF16)
    for k in range(ref.shape[0]):
        ref[k] = piece


def pack_targets_kernel(pos_ref, nrm_ref, adj_ref, ref):
    flat, deep = scaled(pos_ref[...])
    nx, ny, nz = ([v[k : k + 1] for v in three(nrm_ref[...])[:2]] for k in range(3))
    lay(adj_ref[...].astype(F32), flat + nx, deep + ny + nz + [jnp.zeros_like(deep[0])], ref)


def pack_sources_kernel(pos_ref, area_ref, dir_ref, ref):
    flat, deep = scaled(pos_ref[...])
    none = jnp.zeros((2, pos_ref.shape[1]), F32)
    lay(dir_ref[...].astype(F32).T, flat + [none], deep + three(area_ref[...] * TURNS**2) + [none], ref)


def pack(kernel, count, *arrays):
    out = jax.ShapeDtypeStruct((count, DEPTH, LANES), BF16)
    return pl.pallas_call(kernel, out_shape=out, name="pack")(*arrays)


def beside(a, b):
    return (
        jnp.concatenate([a[:, :COLS], b[:, :COLS]], axis=1),
        jnp.concatenate([a[:, COLS:], b[:, COLS:]], axis=1),
    )


def total(value, parts):
    return sum(value[m : m + 1, :] for m in parts)


ROWS = 32
CHUNK = 256
STEP = 1024


def device_place():
    at = {name: lax.axis_index(name) for name in NAMES}
    rho = at["core"] * PARTS["y"] + at["y"]
    return rho, (at["x"] * PARTS["z_lo"] + at["z_lo"]) * PARTS["z_hi"] + at["z_hi"]


def mixing_kernel(counts_ref, owner_ref, lists_ref, mix_ref):
    holder = lax.axis_index(NAMES)
    nx, ncore, ny, nlow = (PARTS[name] for name in ("x", "core", "y", "z_lo"))

    def iota(shape, dim):
        return lax.broadcasted_iota(jnp.int32, shape, dim)

    square = (NPATCH, NPATCH)
    counts = jnp.broadcast_to(counts_ref[...], square)
    eye = iota(square, 0) == iota(square, 1)
    starts = jnp.sum(jnp.where(iota(square, 1) < iota(square, 0), counts, 0).astype(F32), axis=1, keepdims=True)
    own_counts = jnp.sum(jnp.where(eye, counts, 0).astype(F32), axis=1, keepdims=True)
    lines = (NPATCH, NBLK)
    ids = iota(lines, 1).astype(F32)
    inside = (starts <= ids) & (ids < starts + own_counts)
    owner = jnp.broadcast_to(owner_ref[...], square)
    place = iota(square, 0)
    rho = place // 4
    output = ((place % 4) // 2) * (2 * NTGT) + 2 * ((rho % ny) * ncore + rho // ny) + place % 2
    owned = jnp.where(owner == output, 1.0, 0.0).astype(BF16)
    listed = jnp.max(jnp.where(lists_ref[...] == holder, 1.0, 0.0), axis=0, keepdims=True)
    member = jnp.where(inside, jnp.broadcast_to(listed, lines), 0.0).astype(BF16)
    by_block = jnp.dot(owned, member, preferred_element_type=F32).astype(BF16)
    cut = (NBLK, NBLK // 2)
    k = iota(cut, 1)
    for high in range(ncore):
        block = ((k // ny) % nlow) * (NTGT * nx) + ((k % ny) * ncore + high) * nx + k // (ny * nlow)
        order = jnp.where(iota(cut, 0) == block, 1.0, 0.0).astype(BF16)
        part = jnp.dot(by_block, order, preferred_element_type=F32).astype(BF16)
        mix_ref[high * NPATCH : (high + 1) * NPATCH, :] = part


def mixing(patch_counts, patch_owner, block_lists):
    return pl.pallas_call(
        mixing_kernel,
        out_shape=jax.ShapeDtypeStruct((2 * NPATCH, NBLK // 2), BF16),
        name="mixing",
    )(patch_counts.reshape(1, NPATCH), patch_owner.reshape(1, NPATCH), block_lists.T)


def tile_kernel(
    tgt_ref, src_ref, row_ref, col_ref, own_ref, tcols, scols, tfeat, sfeat, tgeo, sgeo, even, odd, rowacc, colacc
):
    rho, _ = device_place()
    at_row = lax.broadcasted_iota(jnp.int32, own_ref.shape, 0) == rho % 8
    at_lane = lax.broadcasted_iota(jnp.int32, own_ref.shape, 1) // COLS == rho // 8
    own_ref[...] = jnp.where(at_row & at_lane, 1.0, 0.0)
    targets, sources = tcols.shape[0], scols.shape[1]
    scale = wave_number / TURNS

    part = lax.broadcasted_iota(jnp.int32, (T_ROWS, LANES), 0)
    chosen = [selector(T_ROWS, {lane: (row, 1.0) for lane, row in LEFT.items()})]
    for parts in (X, Y, Z, tuple(range(T_AMP, T_AMP + 3))):
        chosen.append(jnp.where((part == parts[0]) | (part == parts[1]) | (part == parts[2]), 1.0, 0.0))
    chosen = jnp.concatenate(chosen, axis=1).astype(BF16)
    for g in range(targets // LANES):
        here = slice(g * LANES, (g + 1) * LANES)
        pieces = [tgt_ref[m].astype(F32) for m in (2 * g, 2 * g + 1)]
        for m, piece in enumerate(pieces):
            row = g * LANES + m * COLS
            tcols[row : row + HALF, :] = piece[:HALF, :COLS].astype(BF16)
            tcols[row + HALF : row + COLS, :] = piece[:HALF, COLS:].astype(BF16)
        geo = jnp.concatenate(beside(*(p[HALF:] for p in pieces)), axis=0)
        x, y, z, nx, ny, nz = (total(geo, parts) for parts in (X, Y, Z, NX, NY, NZ))
        rows = three(nx * x + ny * y + nz * z) + three((WAVE_SCALE * nz) * jnp.exp(scale * z)) + three(x * x + y * y + z * z)
        rows = [geo] + rows + [jnp.ones_like(x), jnp.zeros((T_ROWS - T_ONE - 1, LANES), F32)]
        wide = lax.dot_general(
            jnp.concatenate(rows, axis=0).astype(BF16), chosen, (((0,), (0,)), ((), ())), preferred_element_type=F32
        )
        tfeat[here, :] = wide[:, :LANES].astype(BF16)
        for k in range(4):
            tgeo[k, here, :] = wide[:, (k + 1) * LANES : (k + 2) * LANES]
    rights = [selector(S_ROWS, entries).T.astype(BF16) for entries in RIGHT]
    for g in range(sources // LANES):
        here = slice(g * LANES, (g + 1) * LANES)
        left, right = beside(*(src_ref[m].astype(F32) for m in (2 * g, 2 * g + 1)))
        scols[:HALF, here] = left[:HALF].astype(BF16)
        scols[HALF:, here] = right[:HALF].astype(BF16)
        geo = jnp.concatenate([left[HALF:], right[HALF:]], axis=0)
        x, y, z, area = (total(geo, parts) for parts in (X, Y, Z, AREA))
        share = area * (AREA_SCALE / TURNS**2)
        rows = three(share * x) + three(share * y) + three(share * z) + three(share)
        rows += three(x * x + y * y + z * z + area)
        rows = jnp.concatenate([geo] + rows + [jnp.ones_like(x)], axis=0).astype(BF16)
        for k in range(3):
            sfeat[k, :, here] = jnp.dot(rights[k], rows, preferred_element_type=F32).astype(BF16)
        for k, v in enumerate((x, y, z, area, (area * (1.0 / TURNS**2)) * jnp.exp(scale * z))):
            sgeo[k, :, here] = jnp.broadcast_to(v, (8, LANES))
    rowacc[...] = jnp.zeros_like(rowacc)
    colacc[...] = jnp.zeros_like(colacc)
    blocks = targets // STEP
    steps = blocks * (sources // CHUNK)

    def corner(k):
        return pl.multiple_of(lax.rem(k, blocks) * STEP, STEP), pl.multiple_of(lax.div(k, blocks) * CHUNK, CHUNK)

    def products(k, into):
        t0, s0 = corner(k)
        features = tfeat[pl.ds(t0, STEP), :]
        for m in range(3):
            into[m] = jnp.dot(features, sfeat[m, :, pl.ds(s0, CHUNK)], preferred_element_type=F32)
        into[3] = jnp.dot(tcols[pl.ds(t0, STEP), :], scols[:, pl.ds(s0, CHUNK)], preferred_element_type=F32)

    halves = range(CHUNK // LANES)

    def elements(k, made):
        t0, s0 = corner(k)
        lanes = [pl.ds(pl.multiple_of(s0 + h * LANES, LANES), LANES) for h in halves]
        src = [[jnp.concatenate([sgeo[m, :, lanes[h]]] * (ROWS // 8), axis=0) for m in range(5)] for h in halves]
        acc = [None for _ in halves]
        for r in range(0, STEP, ROWS):
            rows = pl.ds(pl.multiple_of(t0 + r, ROWS), ROWS)
            xt, yt, zt, amp = (tgeo[m, rows, :] for m in range(4))
            along = rowacc[rows, :]
            for h in halves:
                top, topi, mirror, image = (made[m, r : r + ROWS, h * LANES : (h + 1) * LANES] for m in range(4))
                xs, ys, zs, area, ebb = src[h]
                dx, dy, dz = xt - xs, yt - ys, zt - zs
                flat = dx * dx + dy * dy + area
                near = flat + dz * dz
                i1, i2, i3 = lax.rsqrt(near), lax.rsqrt(mirror), lax.rsqrt(flat)
                pair = top * (i1 * i1 * i1) + topi * (i2 * i2 * i2)
                phase = flat * i3
                f = phase - ((phase + ROUNDER) - ROUNDER)
                turn = 0.25 - jnp.abs(f)
                g = turn * turn
                p = g + MONIC[-1]
                for c in MONIC[-2::-1]:
                    p = p * g + c
                kern = pair - (amp * ebb) * (turn * p)
                w = kern.astype(BF16).astype(F32) * image
                acc[h] = w if acc[h] is None else acc[h] + w
                along = along + w
            rowacc[rows, :] = along
        for h in halves:
            colacc[:, lanes[h]] += sum(acc[h][m : m + 8] for m in range(0, ROWS, 8))

    products(0, even)

    def two(k, _):
        elements(2 * k, even)
        products(2 * k + 1, odd)
        elements(2 * k + 1, odd)
        products(jnp.minimum(2 * k + 2, steps - 1), even)
        return 0

    lax.fori_loop(0, steps // 2, two, 0)
    for g in range(sources // LANES):
        here = slice(g * LANES, (g + 1) * LANES)
        colacc[0:1, here] = jnp.sum(colacc[:, here], axis=0, keepdims=True)
    panels = col_ref.shape[2]
    for k in range(col_ref.shape[0]):
        col_ref[k] = colacc[0:1, k * panels : (k + 1) * panels]
    for g in range(targets // LANES):
        line = jnp.sum(rowacc[g * LANES : (g + 1) * LANES, :].T, axis=0, keepdims=True)
        for k in range(2):
            low, high = (2 * g + k) % 8, (2 * g + k) // 8
            row_ref[low : low + 1, high * panels : (high + 1) * panels] = line[:, k * panels : (k + 1) * panels]


def tile(tgt, src, panels):
    targets, sources = tgt.shape[0] * panels, src.shape[0] * panels
    return pl.pallas_call(
        tile_kernel,
        out_shape=(
            jax.ShapeDtypeStruct((8, LANES), F32),
            jax.ShapeDtypeStruct((src.shape[0], 1, panels), F32),
            jax.ShapeDtypeStruct((8, LANES), F32),
        ),
        scratch_shapes=[
            pltpu.VMEM((targets, COLS), BF16),
            pltpu.VMEM((COLS, sources), BF16),
            pltpu.VMEM((targets, LANES), BF16),
            pltpu.VMEM((3, LANES, sources), BF16),
            pltpu.VMEM((4, targets, LANES), F32),
            pltpu.VMEM((5, 8, sources), F32),
            pltpu.VMEM((4, STEP, CHUNK), F32),
            pltpu.VMEM((4, STEP, CHUNK), F32),
            pltpu.VMEM((targets, LANES), F32),
            pltpu.VMEM((8, sources), F32),
        ],
        compiler_params=pltpu.CompilerParams(vmem_limit_bytes=24 << 20),
        name="tile",
    )(tgt, src)


def patch_kernel(mix_ref, dens_ref, spline_ref, out_ref, own_ref):
    quarters = PARTS["z_hi"]
    panels = own_ref.shape[1]
    dens = jnp.concatenate(
        [
            jnp.concatenate([dens_ref[k] for k in range(q, dens_ref.shape[0], quarters)], axis=0)
            for q in range(quarters)
        ],
        axis=1,
    )
    mix = mix_ref[...]
    both = sum(jnp.dot(mix, part, preferred_element_type=F32) for part in split3(dens)[1::-1])
    got = jnp.concatenate(
        [
            both[:NPATCH, q * LANES : q * LANES + panels] + both[NPATCH:, q * LANES + panels : (q + 1) * LANES]
            for q in range(quarters)
        ],
        axis=1,
    )
    spline = spline_ref[...]
    rows = sum(jnp.dot(part, spline, preferred_element_type=F32) for part in split3(got)[1::-1])
    for piece in range(out_ref.shape[0]):
        for k in range(out_ref.shape[1] // 2):
            low, lanes = divmod(k, spline.shape[1] // LANES)
            row = 4 * piece + 2 * low
            out_ref[piece, 2 * k : 2 * k + 2, :] = rows[row : row + 2, lanes * LANES : (lanes + 1) * LANES]
    rho, gamma = device_place()
    line = dens_ref[gamma, pl.ds(rho % 8, 1), :]
    own_ref[...] = jnp.where(rho // 8 == 0, line[:, :panels], line[:, panels:])


def patch(mix, blocks, spline, panels):
    return pl.pallas_call(
        patch_kernel,
        out_shape=(
            jax.ShapeDtypeStruct((NTGT, NPATCH // NTGT * spline.shape[1] // LANES, LANES), F32),
            jax.ShapeDtypeStruct((1, panels), F32),
        ),
        compiler_params=pltpu.CompilerParams(vmem_limit_bytes=16 << 20),
        name="patch",
    )(mix, blocks, spline)


def exchange(pieces, axes):
    return lax.all_to_all(pieces, axes, 0, 0, tiled=True)


def copies(value, count):
    return jnp.broadcast_to(value[None], (count,) + value.shape)


def on_device(
    positions, normals, areas, direct, adjoint, spline, block_lists, patch_counts, patch_owner
):
    panels = positions.shape[1]
    tgt = pack(pack_targets_kernel, NTGT, positions, normals, adjoint)
    src = pack(pack_sources_kernel, NSRC, positions, areas.reshape(1, panels), direct)
    mix = mixing(patch_counts, patch_owner, block_lists)
    tgt_all = exchange(tgt, TGT_AXES)
    src, mix = lax.optimization_barrier((src, mix))
    src_all = exchange(src, SRC_AXES)
    row_part, col_part, own_place = tile(tgt_all, src_all, panels)

    mine = jnp.sum(exchange(col_part, SRC_AXES), axis=0)
    row_part = row_part + own_place * jnp.tile(mine, (1, 2))
    dens = jnp.sum(exchange(copies(row_part, NTGT), TGT_AXES), axis=0)
    blocks = exchange(copies(dens, NSRC), SRC_AXES)

    contrib, own = patch(mix, blocks, spline[0], panels)
    rows = jnp.sum(exchange(contrib, TGT_AXES), axis=0)
    low = PARTS["z_lo"]
    rows = rows.reshape(1, low, 1, 8, LANES)
    rows = jnp.broadcast_to(rows, (PARTS["x"], low, PARTS["z_hi"], 8, LANES)).reshape(NSRC, 8, LANES)
    rows = jnp.sum(exchange(rows, SRC_AXES), axis=0)
    patch_grad = rows.reshape(4, 2, LANES).transpose(1, 0, 2).reshape(2, 4 * LANES)
    return own.reshape(panels), patch_grad


def solution(mesh):
    fine = Mesh(mesh.devices.reshape(tuple(PARTS.values())), NAMES)
    placed = (
        P(None, NAMES),
        P(None, NAMES),
        P(NAMES),
        P(NAMES, None),
        P(NAMES, None),
        P(NAMES, None, None),
        P(),
        P(),
        P(),
    )
    return jax.shard_map(
        on_device,
        mesh=fine,
        in_specs=placed,
        out_specs=(P(NAMES), P(("z_lo", "y", "core"), None)),
        check_vma=False,
    )
```
